128 devices in a mesh: dp: 16 (over x_hi, z, core), tp: 8 (over y, x_lo).
Axes of the slice: x: 4 (x_hi: 2, x_lo: 2; x = x_hi * 2 + x_lo), y: 4, z: 4, core: 2. Of those that a mesh axis runs over, the one named last changes fastest.
Arguments:
- queries: bfloat16 [12288, 12288], P('dp', 'tp'), may hold values from -60 to 60
- latent: bfloat16 [12288, 576], P(('dp', 'tp')), may hold values from -6 to 6
- segments: int32 [16, 6], replicated, may hold values from 0 to 2, never falling along the last dimension, each value on 1 to 4 neighbouring positions
- offsets: int32 [6], replicated, may hold values from 0 to 15
- w_uk: bfloat16 [64, 128, 512], P('tp'), may hold values from -0.5 to 0.5
- w_uv: bfloat16 [64, 512, 128], P('tp'), may hold values from -0.25 to 0.25
- w_out: bfloat16 [8192, 7168], P('tp'), may hold values from -0.0625 to 0.0625
Outputs:
- layer_out: bfloat16 [12288, 7168], P(('dp', 'tp'))
The draws below stay inside these ranges and needn't reach their ends.
Inputs may be any that keep to these rules, and one draw needn't show every extreme that they name: `segments`: the request ids of one rank never fall along its blocks, so a request's blocks are consecutive.
All inputs are finite; a program needn't handle non-finite values.
Results may differ from the reference program's by a relative error of at most 0.024.
Values may be sent and summed in bfloat16 or wider, within the bound.
A program may use at most 192 MiB of HBM per device.

```python
import math
import jax
import jax.numpy as jnp
import numpy as np
from jax import lax

D = 7168
H = 64
NOPE = 128
ROPE = 64
LAT = 512
VH = 128
BLK = 128
NB = 6
TOKENS = 12288
KV = 576
N_DP = 16
N_TP = 8


def draw_queries(key, part):
    key = jax.random.fold_in(key, 7)
    key_base = jax.random.fold_in(key, 0)
    shape = (TOKENS, H * (NOPE + ROPE))
    base = jnp.clip(jax.random.normal(key_base, shape, jnp.float32), -6.0, 6.0)
    return base.astype(jnp.bfloat16)


def touch_ends(entries, own_key, least, top_value):
    dims = entries.shape
    spot = [jax.random.randint(jax.random.fold_in(own_key, axis), (), 0, dims[axis]) for axis in range(len(dims))]
    entries = entries.at[tuple(spot)].set(least)
    longest = dims.index(max(dims))
    spot[longest] = (spot[longest] + 1) % dims[longest]
    return entries.at[tuple(spot)].set(top_value)


def steps_of(rng, shape, cuts, least, largest):
    def one(dim, blocks):
        steps = jax.random.uniform(jax.random.fold_in(jax.random.fold_in(rng, 6), dim), (blocks,), jnp.float32, least / len(cuts), largest / len(cuts))
        return jnp.repeat(jnp.exp(steps), shape[dim] // blocks).reshape((-1,) + (1,) * (len(shape) - dim - 1))

    gain = one(*cuts[0])
    for cut in cuts[1:]:
        gain = gain * one(*cut)
    return gain


def split_up(amount, total, limit, slope):
    weights = [(1 << 20) // math.isqrt(rank ** slope) + 1 for rank in range(2, amount + 1)]
    rest, holding = total - limit - (amount - 1), [1] * (amount - 1)
    while rest > 0:
        candidates = [i for i in range(amount - 1) if holding[i] < limit]
        whole, budget = sum([weights[i] for i in candidates]), rest
        for i in candidates:
            more = min(limit - holding[i], max(1, budget * weights[i] // whole), rest)
            holding[i] = holding[i] + more
            rest = rest - more
    return np.array([limit] + holding)


def ragged(own_key, count, total, limit, skew):
    if count == 2:
        one = jax.random.randint(own_key, (), max(1, total - limit), min(limit, total - 1) + 1)
        return jnp.stack([one, total - one])
    sizes = jnp.asarray(split_up(count, total, limit, skew), jnp.int32)
    pairs = (count - 1) // 2
    giver, taker = sizes[1:1 + 2 * pairs:2], sizes[2:2 + 2 * pairs:2]
    slack = jnp.minimum(giver - 1, limit - taker)
    moved = jax.random.randint(jax.random.fold_in(own_key, 1), (pairs,), 0, 1 << 20) % (slack + 1)
    sizes = sizes.at[1:1 + 2 * pairs:2].set(giver - moved).at[2:2 + 2 * pairs:2].set(taker + moved)
    return sizes[jax.random.permutation(jax.random.fold_in(own_key, 2), count)]


def bell_draw(key, dims, spread, most, cuts=(), kind=jnp.bfloat16):
    result = spread * jax.random.normal(key, dims, jnp.float32)
    if cuts:
        result = result * steps_of(key, dims, cuts, -0.22, 0.18)
    return jnp.clip(result, -most, most).astype(kind)


def setup_inputs(seed: int = 0) -> dict:
    arg_keys = jax.random.split(jax.random.key(seed), 8)
    queries = draw_queries(jax.random.fold_in(arg_keys[7], 71), 0)
    latent = bell_draw(arg_keys[1], (TOKENS, KV), 1.0, 6.0, ((0, 128),))
    segments = jax.vmap(lambda own: jnp.searchsorted(jnp.cumsum(ragged(own, max(NB // 2, 2), NB, NB - max(NB // 2, 2) + 1, 2)), jnp.arange(NB), side="right"))(jax.random.split(arg_keys[2], N_DP)).reshape((N_DP, NB)).astype(jnp.int32)
    offsets = touch_ends(jax.random.randint(arg_keys[3], (NB,), 0, N_DP), jax.random.fold_in(arg_keys[3], 1), 0, N_DP - 1).astype(jnp.int32)
    w_uk = bell_draw(arg_keys[4], (H, NOPE, LAT), NOPE ** -0.5, 0.5, ((0, 8),))
    w_uv = bell_draw(arg_keys[5], (H, LAT, VH), LAT ** -0.5, 0.25, ((0, 8),))
    w_out = bell_draw(arg_keys[6], (H * VH, D), (H * VH) ** -0.5, 0.0625, ((0, 8),))
    return dict(queries=queries, latent=latent, segments=segments, offsets=offsets, w_uk=w_uk, w_uv=w_uv, w_out=w_out)


def attend(query_rows, keys, allowed, w_uk, w_uv):
    count = query_rows.shape[0]
    heads = w_uk.shape[0]
    scale = (NOPE + ROPE) ** -0.5
    split_q = query_rows.reshape(count, heads, NOPE + ROPE).astype(jnp.float32)
    q_latent = jnp.einsum("mhn,hnl->hml", split_q[:, :, :NOPE], w_uk.astype(jnp.float32)).astype(jnp.bfloat16)
    content = keys[:, :LAT].astype(jnp.float32)
    rope_keys = keys[:, LAT:].astype(jnp.float32)
    scores = jnp.einsum("hml,jl->hmj", q_latent.astype(jnp.float32), content)
    scores = (scores + jnp.einsum("mhr,jr->hmj", split_q[:, :, NOPE:], rope_keys)) * scale
    scores = jnp.where(allowed[None], scores, -jnp.inf)
    highest = jnp.max(scores, axis=-1, keepdims=True)
    weights = jnp.exp(scores - highest)
    shares = (weights / jnp.sum(weights, axis=-1, keepdims=True)).astype(jnp.bfloat16)
    o_latent = jnp.einsum("hmj,jl->hml", shares.astype(jnp.float32), content).astype(jnp.bfloat16)
    values = jnp.einsum("hml,hlv->mhv", o_latent.astype(jnp.float32), w_uv.astype(jnp.float32)).astype(jnp.bfloat16)
    return values.reshape(count, heads * VH)


def reference(queries, latent, segments, offsets, w_uk, w_uv, w_out):
    row_count = NB * BLK
    positions = jnp.arange(row_count, dtype=jnp.int32)

    def per_rank(rank):
        query_rows = lax.dynamic_slice_in_dim(queries, rank * row_count, row_count, 0)
        keys = lax.dynamic_slice_in_dim(latent, rank * row_count, row_count, 0)
        requests = jnp.repeat(segments[rank], BLK)
        allowed = (requests[:, None] == requests[None, :]) & (positions[None, :] <= positions[:, None])
        return attend(query_rows, keys, allowed, w_uk, w_uv)

    head_values = lax.map(per_rank, jnp.arange(N_DP, dtype=jnp.int32))
    blocked = head_values.reshape(N_DP, NB, BLK, H * VH)
    sources = (jnp.arange(N_DP, dtype=jnp.int32)[:, None] - offsets[None, :]) % N_DP
    moved = blocked[sources, jnp.arange(NB, dtype=jnp.int32)[None, :]]
    moved = moved.reshape(TOKENS, H * VH)
    group_width = H * VH // N_TP
    total = jnp.zeros((TOKENS, D), jnp.float32)
    for group in range(N_TP):
        columns = moved[:, group * group_width:(group + 1) * group_width]
        weights = w_out[group * group_width:(group + 1) * group_width]
        partial_sum = jnp.dot(columns, weights, preferred_element_type=jnp.float32).astype(jnp.bfloat16)
        total = total + partial_sum.astype(jnp.float32)
    return total.astype(jnp.bfloat16)
```

```python
import functools

import jax
import jax.numpy as jnp
from jax import lax
from jax.experimental import pallas as pl
from jax.experimental.pallas import tpu as pltpu
from jax.sharding import PartitionSpec as P

NOPE = 128
ROPE = 64
LAT = 512
VH = 128
BLK = 128
NB = 6
DP = 16
TP = 8
HEADS = 8
ROWS = NB * BLK
KV = LAT + ROPE
D = 7168
OWN = ROWS // TP
WINDOW = 4
UNIT = 32
PART = 256
SCALE = (NOPE + ROPE) ** (-0.5)
LOG2E = 1.4426950408889634

CHUNK = 512
CHUNKS = D // CHUNK
HALF = CHUNK // 2
W_SLOTS = 3
X_LAG = 2
Y1_LAG = 3
Y2_LAG = 5
ACC_SLOTS = Y2_LAG + 1

MESH = pl.DeviceIdType.MESH
BF16 = jnp.bfloat16
F32 = jnp.float32


def ranks():
    return lax.axis_index("dp"), lax.axis_index("tp")


def remote(src, dst, send, recv, dp, tp):
    return pltpu.make_async_remote_copy(
        src_ref=src,
        dst_ref=dst,
        send_sem=send,
        recv_sem=recv,
        device_id={"dp": dp, "tp": tp},
        device_id_type=MESH,
    )


def greet(peers):
    barrier = pltpu.get_barrier_semaphore()
    for dp, tp in peers:
        pl.semaphore_signal(
            barrier, inc=1, device_id={"dp": dp, "tp": tp}, device_id_type=MESH
        )
    pl.semaphore_wait(barrier, len(peers))


def nt_dot(a, b):
    return lax.dot_general(a, b, (((1,), (1,)), ((), ())), preferred_element_type=F32)


def write_bias(seg_ref, bias, dp):
    row = lax.broadcasted_iota(jnp.int32, (BLK, BLK), 0)
    col = lax.broadcasted_iota(jnp.int32, (BLK, BLK), 1)
    for qb in range(NB):
        first = max(0, qb - WINDOW + 1)
        for kb in range(first, qb + 1):
            if kb == qb:
                block = jnp.where(col <= row, 0.0, -jnp.inf).astype(F32)
            else:
                same = seg_ref[dp, kb] == seg_ref[dp, qb]
                block = jnp.full((BLK, BLK), jnp.where(same, 0.0, -jnp.inf), F32)
            bias[qb, :, (kb - first) * BLK : (kb - first + 1) * BLK] = block


def attend_pair(pair, slab, rope_even, rope_odd, bias, q_ref, wuk_ref, wuv_ref, keys, values, y_ref):
    content = slab[:, :, :LAT].reshape(ROWS, LAT)
    up = wuk_ref[pl.ds(2 * pair, 2)].reshape(2 * NOPE, LAT)
    both = nt_dot(content, up)
    lane = lax.broadcasted_iota(jnp.int32, (ROWS, NOPE), 1)
    keys[0, :, :NOPE] = both[:, :NOPE].astype(BF16)
    keys[0, :, NOPE:] = rope_even[...]
    turned = pltpu.roll(both[:, NOPE:], 64, 1)
    keys[1, :, :NOPE] = jnp.where(lane < 64, 0.0, turned).astype(BF16)
    keys[1, :, NOPE:] = jnp.where(lane < 64, turned, rope_odd[...].astype(F32)).astype(BF16)
    for e in range(2):
        values[:, e * VH : (e + 1) * VH] = jnp.dot(
            content, wuv_ref[2 * pair + e], preferred_element_type=F32
        ).astype(BF16)
    for qb in range(NB):
        first = max(0, qb - WINDOW + 1)
        keep = pl.ds(first * BLK, (qb - first + 1) * BLK)
        for e in range(2):
            start = pl.multiple_of(pair * 384 + 128 * e, 128)
            q = q_ref[pl.ds(qb * BLK, BLK), pl.ds(start, 256)]
            s = nt_dot(q, keys[e, keep, :])
            s = s + bias[qb, :, : (qb - first + 1) * BLK]
            top = jnp.max(s, axis=1, keepdims=True)
            p = jnp.exp2((s - top) * (SCALE * LOG2E))
            total = jnp.sum(p, axis=1, keepdims=True)
            o = jnp.dot(
                p.astype(BF16), values[keep, e * VH : (e + 1) * VH], preferred_element_type=F32
            )
            o = (o / total).astype(BF16)
            for part in range(4):
                y_ref[4 * pair + part, qb, :, e * VH : (e + 1) * VH] = o[
                    part * UNIT : (part + 1) * UNIT
                ]


def attend_kernel(
    seg_ref, lat_ref, q_hbm, wuk_hbm, wuv_hbm, y_ref,
    slab, q_ref, wuk_ref, wuv_ref, rope_even, rope_odd, bias, keys, values,
    send_sem, recv_sem, own_sem,
):
    dp, tp = ranks()
    loads = [
        pltpu.make_async_copy(lat_ref, slab.at[tp], own_sem.at[0]),
        pltpu.make_async_copy(wuk_hbm, wuk_ref, own_sem.at[1]),
        pltpu.make_async_copy(wuv_hbm, wuv_ref, own_sem.at[2]),
        pltpu.make_async_copy(q_hbm, q_ref, own_sem.at[3]),
    ]
    for load in loads:
        load.start()
    greet([(dp, lax.rem(tp + o, TP)) for o in range(1, TP)])
    sends = []
    for o in range(1, TP):
        copy = remote(
            lat_ref, slab.at[tp], send_sem.at[o - 1], recv_sem.at[o - 1], dp, lax.rem(tp + o, TP)
        )
        copy.start()
        sends.append(copy)
    write_bias(seg_ref, bias, dp)
    for load in loads:
        load.wait()
    for o, copy in enumerate(sends):
        copy.wait_recv()
    rope = slab[:, :, LAT:].reshape(ROWS, ROPE)
    blank = jnp.zeros((ROWS, ROPE), BF16)
    rope_even[...] = jnp.concatenate([rope, blank], axis=1)
    rope_odd[...] = jnp.concatenate([blank, rope], axis=1)

    def step(pair, carry):
        attend_pair(
            pair, slab, rope_even, rope_odd, bias, q_ref, wuk_ref, wuv_ref, keys, values, y_ref
        )
        return carry

    lax.fori_loop(0, HEADS // 2, step, 0)
    for copy in sends:
        copy.wait_send()


def attend(segments, latent, queries, w_uk, w_uv):
    any_spec = pl.BlockSpec(memory_space=pl.ANY)
    return pl.pallas_call(
        attend_kernel,
        out_shape=jax.ShapeDtypeStruct((DP, NB, UNIT, PART), BF16),
        in_specs=[pl.BlockSpec(memory_space=pltpu.SMEM)] + [any_spec] * 4,
        out_specs=pl.BlockSpec(memory_space=pltpu.VMEM),
        scratch_shapes=[
            pltpu.VMEM((TP, OWN, KV), BF16),
            pltpu.VMEM((ROWS, HEADS * (NOPE + ROPE)), BF16),
            pltpu.VMEM((HEADS, NOPE, LAT), BF16),
            pltpu.VMEM((HEADS, LAT, VH), BF16),
            pltpu.VMEM((ROWS, 2 * ROPE), BF16),
            pltpu.VMEM((ROWS, 2 * ROPE), BF16),
            pltpu.VMEM((NB, BLK, WINDOW * BLK), F32),
            pltpu.VMEM((2, ROWS, 2 * NOPE), BF16),
            pltpu.VMEM((ROWS, 2 * VH), BF16),
            pltpu.SemaphoreType.DMA((TP - 1,)),
            pltpu.SemaphoreType.DMA((TP - 1,)),
            pltpu.SemaphoreType.DMA((4,)),
        ],
        compiler_params=pltpu.CompilerParams(
            collective_id=0, has_side_effects=True, vmem_limit_bytes=40 * 2**20
        ),
        name="gather_attend",
    )(segments, latent, queries, w_uk, w_uv)


def pick(off_ref, me, lo, d, k):
    unit = 4 * k + lax.rem(me, 4)
    crossed = (lax.rem(unit // 6, 2) == 1) & (lax.rem(unit // 3, 2) != lo)
    rank = d + jnp.where(crossed, DP // 2, 0)
    return lax.rem(rank + DP - off_ref[k], DP)


def migrate_kernel(off_ref, y_ref, z_ref, gathered, staged, send1, recv1, send2, recv2, own_sem):
    dp, tp = ranks()
    lo = lax.rem(tp, 2)
    own = pltpu.make_async_copy(y_ref.at[dp], gathered.at[dp], own_sem)
    own.start()
    greet([(lax.rem(dp + o, DP), tp) for o in range(1, DP)])
    firsts = []
    for o in range(1, DP):
        peer = lax.rem(dp + o, DP)
        copy = remote(
            y_ref.at[peer], gathered.at[dp], send1.at[o - 1], recv1.at[o - 1], peer, tp
        )
        copy.start()
        firsts.append(copy)
    own.wait()
    for copy in firsts:
        copy.wait_recv()
    seconds = []
    for o in range(1, DP):
        peer = lax.rem(dp + o, DP)
        for k in range(NB):
            staged[o, k] = gathered[pick(off_ref, dp, lo, peer, k), k]
        copy = remote(
            staged.at[o], z_ref.at[dp], send2.at[o - 1], recv2.at[o - 1], peer, tp
        )
        copy.start()
        seconds.append(copy)
    for k in range(NB):
        z_ref[dp, k] = gathered[pick(off_ref, dp, lo, dp, k), k]
    for copy in seconds:
        copy.wait_recv()
    for copy in firsts + seconds:
        copy.wait_send()


def migrate(offsets, parts):
    return pl.pallas_call(
        migrate_kernel,
        out_shape=jax.ShapeDtypeStruct((DP, NB, UNIT, PART), BF16),
        in_specs=[
            pl.BlockSpec(memory_space=pltpu.SMEM),
            pl.BlockSpec(memory_space=pltpu.VMEM),
        ],
        out_specs=pl.BlockSpec(memory_space=pltpu.VMEM),
        scratch_shapes=[
            pltpu.VMEM((DP, NB, UNIT, PART), BF16),
            pltpu.VMEM((DP, NB, UNIT, PART), BF16),
            pltpu.SemaphoreType.DMA((DP - 1,)),
            pltpu.SemaphoreType.DMA((DP - 1,)),
            pltpu.SemaphoreType.DMA((DP - 1,)),
            pltpu.SemaphoreType.DMA((DP - 1,)),
            pltpu.SemaphoreType.DMA,
        ],
        compiler_params=pltpu.CompilerParams(
            collective_id=1, has_side_effects=True, vmem_limit_bytes=40 * 2**20
        ),
        name="migrate",
    )(offsets, parts)


def slot_of(y):
    return lax.rem(y, 2) * 2 + y // 2


def project_kernel(
    z_ref, w_ref, out_ref,
    rows, w_buf, acc, x_out, x_in, y1_out, y1_in, y2_out, y2_in,
    w_sem, xs_sem, xr_sem, y1s_sem, y1r_sem, y2s_sem, y2r_sem,
):
    dp, tp = ranks()
    y, lo = tp // 2, lax.rem(tp, 2)
    other_dp = lax.rem(dp + DP // 2, DP)
    across = 2 * y + 1 - lo
    up_y, down_y, far_y = lax.rem(y + 1, 4), lax.rem(y + 3, 4), lax.rem(y + 2, 4)
    up, down = 2 * up_y + lo, 2 * down_y + lo

    def load(c):
        start = pl.multiple_of(c * CHUNK, CHUNK)
        slot = lax.rem(c, W_SLOTS)
        return pltpu.make_async_copy(
            w_ref.at[:, pl.ds(start, CHUNK)], w_buf.at[slot], w_sem.at[slot]
        )

    def x_copies(c):
        return [
            remote(x_out.at[c, 0], x_in.at[c, 0], xs_sem.at[c, 0], xr_sem.at[c, 0], dp, across),
            remote(x_out.at[c, 1], x_in.at[c, 1], xs_sem.at[c, 1], xr_sem.at[c, 1], other_dp, across),
        ]

    def y1_copies(c):
        return [
            remote(y1_out.at[c, 0], y1_in.at[c, 0], y1s_sem.at[c, 0], y1r_sem.at[c, 0], dp, up),
            remote(y1_out.at[c, 1], y1_in.at[c, 1], y1s_sem.at[c, 1], y1r_sem.at[c, 1], dp, down),
        ]

    def y2_copies(c):
        return [
            remote(y2_out.at[c, 0], y2_in.at[c, 0], y2s_sem.at[c, 0], y2r_sem.at[c, 0], dp, up),
            remote(y2_out.at[c, 1], y2_in.at[c, 1], y2s_sem.at[c, 1], y2r_sem.at[c, 1], dp, down),
        ]

    for c in range(W_SLOTS - 1):
        load(c).start()
    for unit in range(ROWS // UNIT):
        t, third = unit // 3, unit % 3
        yp, lop = t // 2, t % 2
        at = (yp % 2) * 2 + yp // 2
        for pair in range(4):
            rows[lop, at, pl.ds(third * UNIT, UNIT), pl.ds(pair * PART, PART)] = z_ref[
                4 * pair + unit % 4, unit // 4
            ]
    greet([(dp, across), (other_dp, across), (dp, up), (dp, down)])

    def step(i, carry):
        @pl.when(i < CHUNKS)
        def _():
            slot = lax.rem(i, W_SLOTS)
            load(i).wait()

            @pl.when(i + W_SLOTS - 1 < CHUNKS)
            def _():
                load(i + W_SLOTS - 1).start()

            w = w_buf[slot]
            x_out[i] = (
                jnp.dot(rows[1 - lo].reshape(4 * OWN, TP * VH), w, preferred_element_type=F32)
                .astype(BF16)
                .reshape(2, 2, OWN, CHUNK)
            )
            for copy in x_copies(i):
                copy.start()
            acc[lax.rem(i, ACC_SLOTS)] = jnp.dot(
                rows[lo].reshape(4 * OWN, TP * VH), w, preferred_element_type=F32
            ).reshape(4, OWN, CHUNK)

        @pl.when((i >= X_LAG) & (i < CHUNKS + X_LAG))
        def _():
            c = i - X_LAG
            slot = lax.rem(c, ACC_SLOTS)
            for copy in x_copies(c):
                copy.wait_recv()
            acc[slot] = acc[slot] + x_in[c].reshape(4, OWN, CHUNK).astype(F32)
            far = acc[slot, slot_of(far_y)].astype(BF16)
            y1_out[c, 0] = far[:, :HALF]
            y1_out[c, 1] = far[:, HALF:]
            for copy in y1_copies(c):
                copy.start()

        @pl.when((i >= Y1_LAG) & (i < CHUNKS + Y1_LAG))
        def _():
            c = i - Y1_LAG
            slot = lax.rem(c, ACC_SLOTS)
            for copy in y1_copies(c):
                copy.wait_recv()
            to_up = acc[slot, slot_of(up_y)]
            y2_out[c, 0, :, :HALF] = (to_up[:, :HALF] + y1_in[c, 0].astype(F32)).astype(BF16)
            y2_out[c, 0, :, HALF:] = to_up[:, HALF:].astype(BF16)
            to_down = acc[slot, slot_of(down_y)]
            y2_out[c, 1, :, :HALF] = to_down[:, :HALF].astype(BF16)
            y2_out[c, 1, :, HALF:] = (to_down[:, HALF:] + y1_in[c, 1].astype(F32)).astype(BF16)
            for copy in y2_copies(c):
                copy.start()

        @pl.when((i >= Y2_LAG) & (i < CHUNKS + Y2_LAG))
        def _():
            c = i - Y2_LAG
            slot = lax.rem(c, ACC_SLOTS)
            for copy in y2_copies(c):
                copy.wait_recv()
            start = pl.multiple_of(c * CHUNK, CHUNK)
            out_ref[:, pl.ds(start, CHUNK)] = (
                acc[slot, slot_of(y)] + y2_in[c, 0].astype(F32) + y2_in[c, 1].astype(F32)
            ).astype(BF16)

        return carry

    lax.fori_loop(0, CHUNKS + Y2_LAG, step, 0)

    def drain(c, carry):
        for copy in x_copies(c) + y1_copies(c) + y2_copies(c):
            copy.wait_send()
        return carry

    lax.fori_loop(0, CHUNKS, drain, 0)


def project(moved, w_out):
    pairs = pltpu.SemaphoreType.DMA((CHUNKS, 2))
    return pl.pallas_call(
        project_kernel,
        out_shape=jax.ShapeDtypeStruct((OWN, D), BF16),
        in_specs=[
            pl.BlockSpec(memory_space=pltpu.VMEM),
            pl.BlockSpec(memory_space=pl.ANY),
        ],
        out_specs=pl.BlockSpec(memory_space=pltpu.VMEM),
        scratch_shapes=[
            pltpu.VMEM((2, 4, OWN, TP * VH), BF16),
            pltpu.VMEM((W_SLOTS, TP * VH, CHUNK), BF16),
            pltpu.VMEM((ACC_SLOTS, 4, OWN, CHUNK), F32),
            pltpu.VMEM((CHUNKS, 2, 2, OWN, CHUNK), BF16),
            pltpu.VMEM((CHUNKS, 2, 2, OWN, CHUNK), BF16),
            pltpu.VMEM((CHUNKS, 2, OWN, HALF), BF16),
            pltpu.VMEM((CHUNKS, 2, OWN, HALF), BF16),
            pltpu.VMEM((CHUNKS, 2, OWN, CHUNK), BF16),
            pltpu.VMEM((CHUNKS, 2, OWN, CHUNK), BF16),
            pltpu.SemaphoreType.DMA((W_SLOTS,)),
        ]
        + [pairs] * 6,
        compiler_params=pltpu.CompilerParams(
            collective_id=2, has_side_effects=True, vmem_limit_bytes=56 * 2**20
        ),
        name="project",
    )(moved, w_out)


def on_device(queries, latent, segments, offsets, w_uk, w_uv, w_out):
    parts = attend(segments, latent, queries, w_uk, w_uv)
    moved = migrate(offsets, parts)
    return project(moved, w_out)


def solution(mesh):
    return jax.shard_map(
        on_device,
        mesh=mesh,
        in_specs=(
            P("dp", "tp"),
            P(("dp", "tp"), None),
            P(),
            P(),
            P("tp", None, None),
            P("tp", None, None),
            P("tp", None),
        ),
        out_specs=P(("dp", "tp"), None),
        check_vma=False,
    )
```

```python
import functools

import jax
import jax.numpy as jnp
from jax import lax
from jax.experimental import pallas as pl
from jax.experimental.pallas import tpu as pltpu
from jax.sharding import PartitionSpec as P

NOPE = 128
ROPE = 64
LAT = 512
VH = 128
BLK = 128
NB = 6
DP = 16
TP = 8
HEADS = 8
ROWS = NB * BLK
KV = LAT + ROPE
D = 7168
OWN = ROWS // TP
PARTS = 4
PAIRS = HEADS // 2
WINDOW = 4
UNIT = 32
PART = 256
SCALE = (NOPE + ROPE) ** (-0.5)
LOG2E = 1.4426950408889634

CHUNK = 512
CHUNKS = D // CHUNK
HALF = CHUNK // 2
W_SLOTS = 3
X_LAG = 2
Y1_LAG = 3
Y2_LAG = 5
ACC_SLOTS = Y2_LAG + 1

MESH = pl.DeviceIdType.MESH
BF16 = jnp.bfloat16
F32 = jnp.float32


def ranks():
    return lax.axis_index("dp"), lax.axis_index("tp")


def remote(src, dst, send, recv, dp, tp):
    return pltpu.make_async_remote_copy(
        src_ref=src,
        dst_ref=dst,
        send_sem=send,
        recv_sem=recv,
        device_id={"dp": dp, "tp": tp},
        device_id_type=MESH,
    )


def greet(peers):
    barrier = pltpu.get_barrier_semaphore()
    for dp, tp in peers:
        pl.semaphore_signal(
            barrier, inc=1, device_id={"dp": dp, "tp": tp}, device_id_type=MESH
        )
    pl.semaphore_wait(barrier, len(peers))


def nt_dot(a, b):
    return lax.dot_general(a, b, (((1,), (1,)), ((), ())), preferred_element_type=F32)


HOME = ((3, 11, 6), (4, 0, 5), (9, 1, 7), (10, 2, 8))


def unit_of(p, e, u):
    y, third = divmod(HOME[p][u], 3)
    unit = 6 * y + third
    return 23 - unit if e else unit


PLACE = {
    unit_of(p, e, u): (p, e, u) for p in range(PARTS) for e in range(2) for u in range(3)
}


def block_of(p, e, u):
    first = (
        jnp.where(p < 2, 1, 4),
        jnp.where(p == 0, 5, 0),
        jnp.where(p == 1, 2, 3),
    )[u]
    return jnp.where(e == 1, NB - 1 - first, first)


def write_bias(seg_ref, bias, dp):
    row = lax.broadcasted_iota(jnp.int32, (BLK, BLK), 0)
    col = lax.broadcasted_iota(jnp.int32, (BLK, BLK), 1)
    for qb in range(NB):
        first = max(0, qb - WINDOW + 1)
        for kb in range(first, qb + 1):
            if kb == qb:
                block = jnp.where(col <= row, 0.0, -jnp.inf).astype(F32)
            else:
                same = seg_ref[dp, kb] == seg_ref[dp, qb]
                block = jnp.full((BLK, BLK), jnp.where(same, 0.0, -jnp.inf), F32)
            bias[qb, :, (kb - first) * BLK : (kb - first + 1) * BLK] = block


def attend_pair(pair, slab, rope_even, rope_odd, bias, q_ref, wuk_ref, wuv_ref, keys, values, parts):
    content = slab[:, :, :LAT].reshape(ROWS, LAT)
    up = wuk_ref[pl.ds(2 * pair, 2)].reshape(2 * NOPE, LAT)
    both = nt_dot(content, up)
    lane = lax.broadcasted_iota(jnp.int32, (ROWS, NOPE), 1)
    keys[0, :, :NOPE] = both[:, :NOPE].astype(BF16)
    keys[0, :, NOPE:] = rope_even[...]
    turned = pltpu.roll(both[:, NOPE:], 64, 1)
    keys[1, :, :NOPE] = jnp.where(lane < 64, 0.0, turned).astype(BF16)
    keys[1, :, NOPE:] = jnp.where(lane < 64, turned, rope_odd[...].astype(F32)).astype(BF16)
    for e in range(2):
        values[:, e * VH : (e + 1) * VH] = jnp.dot(
            content, wuv_ref[2 * pair + e], preferred_element_type=F32
        ).astype(BF16)
    for qb in range(NB):
        first = max(0, qb - WINDOW + 1)
        keep = pl.ds(first * BLK, (qb - first + 1) * BLK)
        for e in range(2):
            start = pl.multiple_of(pair * 384 + 128 * e, 128)
            q = q_ref[pl.ds(qb * BLK, BLK), pl.ds(start, 256)]
            s = nt_dot(q, keys[e, keep, :])
            s = s + bias[qb, :, : (qb - first + 1) * BLK]
            top = jnp.max(s, axis=1, keepdims=True)
            p = jnp.exp2((s - top) * (SCALE * LOG2E))
            total = jnp.sum(p, axis=1, keepdims=True)
            o = jnp.dot(
                p.astype(BF16), values[keep, e * VH : (e + 1) * VH], preferred_element_type=F32
            )
            o = (o / total).astype(BF16)
            for quarter in range(4):
                part, side, u = PLACE[4 * qb + quarter]
                parts[pair, part, side, u, :, e * VH : (e + 1) * VH] = o[
                    quarter * UNIT : (quarter + 1) * UNIT
                ]


def whole_kernel(
    seg_ref, off_ref, lat_hbm, q_hbm, wuk_hbm, wuv_hbm, w_hbm, out_ref,
    slab, q_ref, wuk_ref, wuv_ref, rope_even, rope_odd, bias, keys, values,
    parts, gathered, staged_near, staged_far, near, far, rows_keep, rows_away,
    w_buf, acc, x_out, x_in, y1_out, y1_in, y2_out, y2_in,
    own_sem, ag_s, ag_r, p1_s, p1_r, p2_s, p2_r,
    w_sem, xs_sem, xr_sem, y1s_sem, y1r_sem, y2s_sem, y2r_sem,
):
    dp, tp = ranks()
    y, lo = tp // 2, lax.rem(tp, 2)
    hi, z, core = dp // 8, lax.rem(dp // 2, 4), lax.rem(dp, 2)
    across = 2 * y + 1 - lo
    own_y = jnp.where(lo == 1, 3 - y, y)
    step_y = jnp.where(lo == 1, 3, 1)
    up = 2 * lax.rem(y + step_y, 4) + lo
    down = 2 * lax.rem(y + 4 - step_y, 4) + lo
    up_y, down_y, far_y = lax.rem(own_y + 1, 4), lax.rem(own_y + 3, 4), lax.rem(own_y + 2, 4)

    def flip(bit, by):
        return bit + by - 2 * bit * by

    def rank_at(o, a, b):
        return flip(hi, a) * 8 + lax.rem(z + o, 4) * 2 + flip(core, b)

    def load(c):
        start = pl.multiple_of(c * CHUNK, CHUNK)
        slot = lax.rem(c, W_SLOTS)
        return pltpu.make_async_copy(
            w_hbm.at[:, pl.ds(start, CHUNK)], w_buf.at[slot], w_sem.at[slot]
        )

    loads = [
        pltpu.make_async_copy(lat_hbm, slab.at[tp], own_sem.at[0]),
        pltpu.make_async_copy(wuk_hbm, wuk_ref, own_sem.at[1]),
        pltpu.make_async_copy(wuv_hbm, wuv_ref, own_sem.at[2]),
        pltpu.make_async_copy(q_hbm, q_ref, own_sem.at[3]),
    ]
    for copy in loads:
        copy.start()
    for c in range(W_SLOTS - 1):
        load(c).start()

    greet(
        [(dp, lax.rem(tp + o, TP)) for o in range(1, TP)]
        + [(lax.rem(dp + o, DP), tp) for o in range(1, DP)]
        + [(lax.rem(dp + DP // 2, DP), across)]
    )

    gathers = []
    for o in range(1, TP):
        copy = remote(
            lat_hbm, slab.at[tp], ag_s.at[o - 1], ag_r.at[o - 1], dp, lax.rem(tp + o, TP)
        )
        copy.start()
        gathers.append(copy)
    write_bias(seg_ref, bias, dp)
    for copy in loads:
        copy.wait()
    for copy in gathers:
        copy.wait_recv()
    rope = slab[:, :, LAT:].reshape(ROWS, ROPE)
    blank = jnp.zeros((ROWS, ROPE), BF16)
    rope_even[...] = jnp.concatenate([rope, blank], axis=1)
    rope_odd[...] = jnp.concatenate([blank, rope], axis=1)

    def spread(o, a, b):
        pair = lax.rem(z + o, 4)
        part = 2 * flip(core, b) + flip(hi, a)
        at = o * 4 + a * 2 + b
        return remote(
            parts.at[pair, part], gathered.at[dp], p1_s.at[at], p1_r.at[at], rank_at(o, a, b), tp
        )

    own_part = pltpu.make_async_copy(
        parts.at[z, 2 * core + hi], gathered.at[dp], p1_s.at[0]
    )

    def attend_step(i, carry):
        o = jnp.where(i == 0, 2, jnp.where(i == 1, 1, jnp.where(i == 2, 3, 0)))
        attend_pair(
            lax.rem(z + o, 4), slab, rope_even, rope_odd, bias, q_ref, wuk_ref, wuv_ref,
            keys, values, parts,
        )
        for a, b in ((1, 0), (1, 1), (0, 1)):
            spread(o, a, b).start()

        @pl.when(o != 0)
        def _():
            spread(o, 0, 0).start()

        return carry

    lax.fori_loop(0, PAIRS, attend_step, 0)
    own_part.start()
    ways = [(o, a, b) for o in (2, 1, 3, 0) for a in (1, 0) for b in (1, 0)]
    others = [way for way in ways if way != (0, 0, 0)]
    for way in others:
        spread(*way).wait_recv()
    own_part.wait()

    part = 2 * core + hi
    near_sends, far_sends = [], []

    def taken(rank, e, u):
        source = lax.rem(rank + DP - off_ref[block_of(part, e, u)], DP)
        return gathered[source, e, u]

    def deliver(o, a, b):
        at = o * 4 + a * 2 + b
        src = (staged_far if a else staged_near).at[2 * o + b]
        dst = (far if a else near).at[2 * z + core]
        return remote(src, dst, p2_s.at[at], p2_r.at[at], rank_at(o, a, b), tp)

    for o, a, b in ways:
        rank = rank_at(o, a, b)
        slot = 2 * o + b
        if a:
            target, index = staged_far, slot
        elif (o, b) == (0, 0):
            target, index = near, 2 * z + core
        else:
            target, index = staged_near, slot
        for u in range(3):
            target[index, u] = taken(rank, lo, u)
        if not a:
            for side in range(2):
                for u in range(3):
                    target[index, 3 + 3 * side + u] = taken(
                        rank + (side - hi) * 8, 1 - lo, u
                    )
        if (o, a, b) != (0, 0, 0):
            deliver(o, a, b).start()
    for way in others:
        deliver(*way).wait_recv()

    for pair in range(PAIRS):
        columns = pl.ds(pair * PART, PART)
        for c in range(2):
            for u in range(3):
                for a in range(2):
                    home = jnp.where(hi == 0, HOME[2 * c + a][u], HOME[2 * c + 1 - a][u])
                    rows_keep[home, :, columns] = (far if a else near)[2 * pair + c, u]
                for side in range(2):
                    rows_away[side, 3 * c + u, :, columns] = near[2 * pair + c, 3 + 3 * side + u]

    def x_copies(c):
        return [
            remote(
                x_out.at[c, flip(hi, a)], x_in.at[c, hi], xs_sem.at[c, a], xr_sem.at[c, a],
                rank_at(0, a, 0), across,
            )
            for a in range(2)
        ]

    def y1_copies(c):
        return [
            remote(y1_out.at[c, 0], y1_in.at[c, 0], y1s_sem.at[c, 0], y1r_sem.at[c, 0], dp, up),
            remote(y1_out.at[c, 1], y1_in.at[c, 1], y1s_sem.at[c, 1], y1r_sem.at[c, 1], dp, down),
        ]

    def y2_copies(c):
        return [
            remote(y2_out.at[c, 0], y2_in.at[c, 0], y2s_sem.at[c, 0], y2r_sem.at[c, 0], dp, up),
            remote(y2_out.at[c, 1], y2_in.at[c, 1], y2s_sem.at[c, 1], y2r_sem.at[c, 1], dp, down),
        ]

    def group(slot, at):
        return acc[slot, pl.ds(3 * at, 3)].reshape(OWN, CHUNK)

    def project_step(i, carry):
        @pl.when(i < CHUNKS)
        def _():
            slot = lax.rem(i, W_SLOTS)
            load(i).wait()

            @pl.when(i + W_SLOTS - 1 < CHUNKS)
            def _():
                load(i + W_SLOTS - 1).start()

            w = w_buf[slot]
            x_out[i] = (
                jnp.dot(rows_away[...].reshape(4 * OWN, TP * VH), w, preferred_element_type=F32)
                .astype(BF16)
                .reshape(2, 2 * OWN, CHUNK)
            )
            for copy in x_copies(i):
                copy.start()
            acc[lax.rem(i, ACC_SLOTS)] = jnp.dot(
                rows_keep[...].reshape(4 * OWN, TP * VH), w, preferred_element_type=F32
            ).reshape(12, UNIT, CHUNK)

        @pl.when((i >= X_LAG) & (i < CHUNKS + X_LAG))
        def _():
            c = i - X_LAG
            slot = lax.rem(c, ACC_SLOTS)
            for copy in x_copies(c):
                copy.wait_recv()
            for side in range(2):
                for half in range(2):
                    for u in range(3):
                        home = HOME[2 * half + side][u]
                        acc[slot, home] = acc[slot, home] + x_in[
                            c, side, pl.ds((3 * half + u) * UNIT, UNIT)
                        ].astype(F32)
            other = group(slot, far_y).astype(BF16)
            y1_out[c, 0] = other[:, :HALF]
            y1_out[c, 1] = other[:, HALF:]
            for copy in y1_copies(c):
                copy.start()

        @pl.when((i >= Y1_LAG) & (i < CHUNKS + Y1_LAG))
        def _():
            c = i - Y1_LAG
            slot = lax.rem(c, ACC_SLOTS)
            for copy in y1_copies(c):
                copy.wait_recv()
            to_up = group(slot, up_y)
            y2_out[c, 0, :, :HALF] = (to_up[:, :HALF] + y1_in[c, 0].astype(F32)).astype(BF16)
            y2_out[c, 0, :, HALF:] = to_up[:, HALF:].astype(BF16)
            to_down = group(slot, down_y)
            y2_out[c, 1, :, :HALF] = to_down[:, :HALF].astype(BF16)
            y2_out[c, 1, :, HALF:] = (to_down[:, HALF:] + y1_in[c, 1].astype(F32)).astype(BF16)
            for copy in y2_copies(c):
                copy.start()

        @pl.when((i >= Y2_LAG) & (i < CHUNKS + Y2_LAG))
        def _():
            c = i - Y2_LAG
            slot = lax.rem(c, ACC_SLOTS)
            for copy in y2_copies(c):
                copy.wait_recv()
            start = pl.multiple_of(c * CHUNK, CHUNK)
            total = group(slot, own_y) + y2_in[c, 0].astype(F32) + y2_in[c, 1].astype(F32)
            total = total.astype(BF16)
            for third in range(3):
                out_ref[jnp.where(lo == 1, 2 - third, third), :, pl.ds(start, CHUNK)] = total[
                    third * UNIT : (third + 1) * UNIT
                ]

        return carry

    lax.fori_loop(0, CHUNKS + Y2_LAG, project_step, 0)

    for copy in gathers:
        copy.wait_send()
    for way in others:
        spread(*way).wait_send()
        deliver(*way).wait_send()

    def drain(c, carry):
        for copy in x_copies(c) + y1_copies(c) + y2_copies(c):
            copy.wait_send()
        return carry

    lax.fori_loop(0, CHUNKS, drain, 0)


def on_device(queries, latent, segments, offsets, w_uk, w_uv, w_out):
    any_spec = pl.BlockSpec(memory_space=pl.ANY)
    smem_spec = pl.BlockSpec(memory_space=pltpu.SMEM)
    dma = pltpu.SemaphoreType.DMA
    out = pl.pallas_call(
        whole_kernel,
        out_shape=jax.ShapeDtypeStruct((3, UNIT, D), BF16),
        in_specs=[smem_spec] * 2 + [any_spec] * 5,
        out_specs=pl.BlockSpec(memory_space=pltpu.VMEM),
        scratch_shapes=[
            pltpu.VMEM((TP, OWN, KV), BF16),
            pltpu.VMEM((ROWS, HEADS * (NOPE + ROPE)), BF16),
            pltpu.VMEM((HEADS, NOPE, LAT), BF16),
            pltpu.VMEM((HEADS, LAT, VH), BF16),
            pltpu.VMEM((ROWS, 2 * ROPE), BF16),
            pltpu.VMEM((ROWS, 2 * ROPE), BF16),
            pltpu.VMEM((NB, BLK, WINDOW * BLK), F32),
            pltpu.VMEM((2, ROWS, 2 * NOPE), BF16),
            pltpu.VMEM((ROWS, 2 * VH), BF16),
            pltpu.VMEM((PAIRS, PARTS, 2, 3, UNIT, PART), BF16),
            pltpu.VMEM((DP, 2, 3, UNIT, PART), BF16),
            pltpu.VMEM((8, 9, UNIT, PART), BF16),
            pltpu.VMEM((8, 3, UNIT, PART), BF16),
            pltpu.VMEM((8, 9, UNIT, PART), BF16),
            pltpu.VMEM((8, 3, UNIT, PART), BF16),
            pltpu.VMEM((12, UNIT, TP * VH), BF16),
            pltpu.VMEM((2, 6, UNIT, TP * VH), BF16),
            pltpu.VMEM((W_SLOTS, TP * VH, CHUNK), BF16),
            pltpu.VMEM((ACC_SLOTS, 12, UNIT, CHUNK), F32),
            pltpu.VMEM((CHUNKS, 2, 2 * OWN, CHUNK), BF16),
            pltpu.VMEM((CHUNKS, 2, 2 * OWN, CHUNK), BF16),
            pltpu.VMEM((CHUNKS, 2, OWN, HALF), BF16),
            pltpu.VMEM((CHUNKS, 2, OWN, HALF), BF16),
            pltpu.VMEM((CHUNKS, 2, OWN, CHUNK), BF16),
            pltpu.VMEM((CHUNKS, 2, OWN, CHUNK), BF16),
            dma((4,)),
            dma((TP - 1,)),
            dma((TP - 1,)),
            dma((DP,)),
            dma((DP,)),
            dma((DP,)),
            dma((DP,)),
            dma((W_SLOTS,)),
        ]
        + [dma((CHUNKS, 2))] * 6,
        compiler_params=pltpu.CompilerParams(
            collective_id=0, has_side_effects=True, vmem_limit_bytes=58 * 2**20
        ),
        name="whole",
    )(segments, offsets, latent, queries, w_uk, w_uv, w_out)
    return out.reshape(OWN, D)


def solution(mesh):
    return jax.shard_map(
        on_device,
        mesh=mesh,
        in_specs=(
            P("dp", "tp"),
            P(("dp", "tp"), None),
            P(),
            P(),
            P("tp", None, None),
            P("tp", None, None),
            P("tp", None),
        ),
        out_specs=P(("dp", "tp"), None),
        check_vma=False,
    )
```

```python
import functools

import jax
import jax.numpy as jnp
from jax import lax
from jax.experimental import pallas as pl
from jax.experimental.pallas import tpu as pltpu
from jax.sharding import PartitionSpec as P

NOPE = 128
ROPE = 64
LAT = 512
VH = 128
BLK = 128
NB = 6
DP = 16
TP = 8
HEADS = 8
ROWS = NB * BLK
KV = LAT + ROPE
D = 7168
OWN = ROWS // TP
PARTS = 4
PAIRS = HEADS // 2
WINDOW = 4
UNIT = 32
PART = 256
SCALE = (NOPE + ROPE) ** (-0.5)
LOG2E = 1.4426950408889634

CHUNK = 512
CHUNKS = D // CHUNK
HALF = CHUNK // 2
STEPS = 2 * CHUNKS
W_SLOTS = 3
GROUPS = (1, 2)
LAGS = ((3, 4, 6), (2, 3, 5))

MESH = pl.DeviceIdType.MESH
BF16 = jnp.bfloat16
F32 = jnp.float32


def ranks():
    return lax.axis_index("dp"), lax.axis_index("tp")


def remote(src, dst, send, recv, dp, tp):
    return pltpu.make_async_remote_copy(
        src_ref=src,
        dst_ref=dst,
        send_sem=send,
        recv_sem=recv,
        device_id={"dp": dp, "tp": tp},
        device_id_type=MESH,
    )


def greet(peers):
    barrier = pltpu.get_barrier_semaphore()
    for dp, tp in peers:
        pl.semaphore_signal(
            barrier, inc=1, device_id={"dp": dp, "tp": tp}, device_id_type=MESH
        )
    pl.semaphore_wait(barrier, len(peers))


def nt_dot(a, b):
    return lax.dot_general(a, b, (((1,), (1,)), ((), ())), preferred_element_type=F32)


HOME = ((11, 3, 6), (4, 0, 5), (7, 1, 9), (2, 10, 8))
FIRST = (3, 1, 2, 0)
SECOND = ((2, 4), (0, 3), (1, 6), (7, 5))


def unit_of(p, e, u):
    y, third = divmod(HOME[p][u], 3)
    unit = 6 * y + third
    return 23 - unit if e else unit


PLACE = {
    unit_of(p, e, u): (p, e, u) for p in range(PARTS) for e in range(2) for u in range(3)
}


def choose(p, options):
    value = options[0]
    for i in range(1, PARTS):
        value = jnp.where(p == i, options[i], value)
    return value


def block_of(p, e, u):
    first = choose(p, [unit_of(i, 0, u) // 4 for i in range(PARTS)])
    return jnp.where(e == 1, NB - 1 - first, first)


def write_bias(seg_ref, bias, dp):
    row = lax.broadcasted_iota(jnp.int32, (BLK, BLK), 0)
    col = lax.broadcasted_iota(jnp.int32, (BLK, BLK), 1)
    for qb in range(NB):
        first = max(0, qb - WINDOW + 1)
        for kb in range(first, qb + 1):
            if kb == qb:
                block = jnp.where(col <= row, 0.0, -jnp.inf).astype(F32)
            else:
                same = seg_ref[dp, kb] == seg_ref[dp, qb]
                block = jnp.full((BLK, BLK), jnp.where(same, 0.0, -jnp.inf), F32)
            bias[qb, :, (kb - first) * BLK : (kb - first + 1) * BLK] = block


def attend_pair(pair, slab, rope_even, rope_odd, bias, q_ref, wuk_ref, wuv_ref, keys, values, parts):
    content = slab[:, :, :LAT].reshape(ROWS, LAT)
    up = wuk_ref[pl.ds(2 * pair, 2)].reshape(2 * NOPE, LAT)
    both = nt_dot(content, up)
    lane = lax.broadcasted_iota(jnp.int32, (ROWS, NOPE), 1)
    keys[0, :, :NOPE] = both[:, :NOPE].astype(BF16)
    keys[0, :, NOPE:] = rope_even[...]
    turned = pltpu.roll(both[:, NOPE:], 64, 1)
    keys[1, :, :NOPE] = jnp.where(lane < 64, 0.0, turned).astype(BF16)
    keys[1, :, NOPE:] = jnp.where(lane < 64, turned, rope_odd[...].astype(F32)).astype(BF16)
    for e in range(2):
        values[:, e * VH : (e + 1) * VH] = jnp.dot(
            content, wuv_ref[2 * pair + e], preferred_element_type=F32
        ).astype(BF16)
    for qb in range(NB):
        first = max(0, qb - WINDOW + 1)
        keep = pl.ds(first * BLK, (qb - first + 1) * BLK)
        for e in range(2):
            start = pl.multiple_of(pair * 384 + 128 * e, 128)
            q = q_ref[pl.ds(qb * BLK, BLK), pl.ds(start, 256)]
            s = nt_dot(q, keys[e, keep, :])
            s = s + bias[qb, :, : (qb - first + 1) * BLK]
            top = jnp.max(s, axis=1, keepdims=True)
            p = jnp.exp2((s - top) * (SCALE * LOG2E))
            total = jnp.sum(p, axis=1, keepdims=True)
            o = jnp.dot(
                p.astype(BF16), values[keep, e * VH : (e + 1) * VH], preferred_element_type=F32
            )
            o = (o / total).astype(BF16)
            for quarter in range(4):
                part, side, u = PLACE[4 * qb + quarter]
                parts[pair, part, side, u, :, e * VH : (e + 1) * VH] = o[
                    quarter * UNIT : (quarter + 1) * UNIT
                ]


def whole_kernel(
    seg_ref, off_ref, lat_hbm, q_hbm, wuk_hbm, wuv_hbm, w_hbm, out_ref,
    slab, q_ref, wuk_ref, wuv_ref, rope_even, rope_odd, bias, keys, values,
    parts, gathered, staged_near1, staged_near2, staged_far1, staged_far2, near1, near2, far1, far2,
    rows1, keep2, away2, w_buf,
    acc1, x_out1, x_in1, y1_out1, y1_in1, y2_out1, y2_in1,
    acc2, x_out2, x_in2, y1_out2, y1_in2, y2_out2, y2_in2,
    own_sem, ag_s, ag_r, p1_s, p1_r, p2_s, p2_r,
    w_sem, xs_sem, xr_sem, y1s_sem, y1r_sem, y2s_sem, y2r_sem,
):
    dp, tp = ranks()
    y, lo = tp // 2, lax.rem(tp, 2)
    hi, z, core = dp // 8, lax.rem(dp // 2, 4), lax.rem(dp, 2)
    across = 2 * y + 1 - lo
    own_y = jnp.where(lo == 1, 3 - y, y)
    step_y = jnp.where(lo == 1, 3, 1)
    up = 2 * lax.rem(y + step_y, 4) + lo
    down = 2 * lax.rem(y + 4 - step_y, 4) + lo
    up_y, down_y, far_y = lax.rem(own_y + 1, 4), lax.rem(own_y + 3, 4), lax.rem(own_y + 2, 4)

    def flip(bit, by):
        return bit + by - 2 * bit * by

    def rank_at(o, a, b):
        return flip(hi, a) * 8 + lax.rem(z + o, 4) * 2 + flip(core, b)

    def load(c):
        start = pl.multiple_of(lax.rem(c, CHUNKS) * CHUNK, CHUNK)
        slot = lax.rem(c, W_SLOTS)
        return pltpu.make_async_copy(
            w_hbm.at[:, pl.ds(start, CHUNK)], w_buf.at[slot], w_sem.at[slot]
        )

    loads = [
        pltpu.make_async_copy(lat_hbm, slab.at[tp], own_sem.at[0]),
        pltpu.make_async_copy(wuk_hbm, wuk_ref, own_sem.at[1]),
        pltpu.make_async_copy(wuv_hbm, wuv_ref, own_sem.at[2]),
        pltpu.make_async_copy(q_hbm, q_ref, own_sem.at[3]),
    ]
    for copy in loads:
        copy.start()
    for c in range(W_SLOTS - 1):
        load(c).start()

    greet(
        [(dp, lax.rem(tp + o, TP)) for o in range(1, TP)]
        + [(lax.rem(dp + o, DP), tp) for o in range(1, DP)]
        + [(lax.rem(dp + DP // 2, DP), across)]
    )

    opposite = 2 * lax.rem(y + 2, 4) + lo
    after, before = 2 * lax.rem(y + 1, 4) + lo, 2 * lax.rem(y + 3, 4) + lo

    def hand(index, src, at, to):
        return remote(src, slab.at[at], ag_s.at[index], ag_r.at[index], dp, to)

    gathers = [
        hand(0, lat_hbm, tp, opposite),
        hand(1, lat_hbm, tp, across),
        hand(2, lat_hbm, tp, after),
        hand(3, lat_hbm, tp, before),
        hand(4, slab.at[across], across, after),
        hand(5, slab.at[across], across, before),
        hand(6, slab.at[opposite], opposite, across),
    ]
    for copy in gathers[:4]:
        copy.start()
    gathers[1].wait_recv()
    gathers[4].start()
    gathers[5].start()
    gathers[0].wait_recv()
    gathers[6].start()
    write_bias(seg_ref, bias, dp)
    for copy in loads:
        copy.wait()
    for copy in gathers[2:]:
        copy.wait_recv()
    rope = slab[:, :, LAT:].reshape(ROWS, ROPE)
    blank = jnp.zeros((ROWS, ROPE), BF16)
    rope_even[...] = jnp.concatenate([rope, blank], axis=1)
    rope_odd[...] = jnp.concatenate([blank, rope], axis=1)

    def spread(o, a, b):
        pair = lax.rem(z + o, 4)
        part = 2 * flip(core, b) + flip(hi, a)
        at = o * 4 + a * 2 + b
        return remote(
            parts.at[pair, part], gathered.at[dp], p1_s.at[at], p1_r.at[at], rank_at(o, a, b), tp
        )

    own_part = pltpu.make_async_copy(
        parts.at[z, 2 * core + hi], gathered.at[dp], p1_s.at[0]
    )

    def attend_step(i, carry):
        o = jnp.where(i == 0, 2, jnp.where(i == 1, 1, jnp.where(i == 2, 3, 0)))
        attend_pair(
            lax.rem(z + o, 4), slab, rope_even, rope_odd, bias, q_ref, wuk_ref, wuv_ref,
            keys, values, parts,
        )
        for a, b in ((1, 0), (1, 1), (0, 1)):
            spread(o, a, b).start()

        @pl.when(o != 0)
        def _():
            spread(o, 0, 0).start()

        return carry

    lax.fori_loop(0, PAIRS, attend_step, 0)
    own_part.start()
    ways = [(o, a, b) for o in (2, 1, 3, 0) for a in (1, 0) for b in (1, 0)]
    others = [way for way in ways if way != (0, 0, 0)]
    for way in others:
        spread(*way).wait_recv()
    own_part.wait()

    part = 2 * core + hi
    staged_near, staged_far = (staged_near1, staged_near2), (staged_far1, staged_far2)
    near, far = (near1, near2), (far1, far2)

    def taken(rank, e, u):
        source = lax.rem(rank + DP - off_ref[block_of(part, e, u)], DP)
        return gathered[source, e, u]

    def deliver(g, o, a, b):
        at = g * DP + o * 4 + a * 2 + b
        src = (staged_far if a else staged_near)[g].at[2 * o + b]
        dst = (far if a else near)[g].at[2 * z + core]
        return remote(src, dst, p2_s.at[at], p2_r.at[at], rank_at(o, a, b), tp)

    for g, units in enumerate(((0,), (1, 2))):
        for o, a, b in ways:
            rank = rank_at(o, a, b)
            own = (o, a, b) == (0, 0, 0)
            if a:
                target, index = staged_far[g], 2 * o + b
            elif own:
                target, index = near[g], 2 * z + core
            else:
                target, index = staged_near[g], 2 * o + b
            count = len(units)
            for n, u in enumerate(units):
                target[index, n] = taken(rank, lo, u)
            if not a:
                for side in range(2):
                    for n, u in enumerate(units):
                        target[index, count * (1 + side) + n] = taken(
                            rank + (side - hi) * 8, 1 - lo, u
                        )
            if not own:
                deliver(g, o, a, b).start()

    def arrived(g):
        for way in others:
            deliver(g, *way).wait_recv()
        count = g + 1
        for pair in range(PAIRS):
            columns = pl.ds(pair * PART, PART)
            for c in range(2):
                for n in range(count):
                    for a in range(2):
                        mine, yours = 2 * c + a, 2 * c + 1 - a
                        unit = (far if a else near)[g][2 * pair + c, n]
                        if g == 0:
                            home = jnp.where(hi == 0, FIRST[mine], FIRST[yours])
                            rows1[4 + home, :, columns] = unit
                        else:
                            home = jnp.where(hi == 0, SECOND[mine][n], SECOND[yours][n])
                            keep2[home, :, columns] = unit
                    for side in range(2):
                        unit = near[g][2 * pair + c, count * (1 + side) + n]
                        if g == 0:
                            rows1[2 * side + c, :, columns] = unit
                        else:
                            away2[side, 2 * c + n, :, columns] = unit

    class Group:
        pass

    groups = []
    for g, (acc, x_out, x_in, y1_out, y1_in, y2_out, y2_in) in enumerate(
        (
            (acc1, x_out1, x_in1, y1_out1, y1_in1, y2_out1, y2_in1),
            (acc2, x_out2, x_in2, y1_out2, y1_in2, y2_out2, y2_in2),
        )
    ):
        t = Group()
        t.acc, t.x_out, t.x_in, t.y1_out, t.y1_in, t.y2_out, t.y2_in = (
            acc, x_out, x_in, y1_out, y1_in, y2_out, y2_in,
        )
        t.g, t.count, t.rows, t.lags = g, GROUPS[g], GROUPS[g] * UNIT, LAGS[g]
        groups.append(t)

    def x_copies(t, c):
        sems = t.g * CHUNKS + c
        return [
            remote(
                t.x_out.at[c, flip(hi, a)], t.x_in.at[c, hi], xs_sem.at[sems, a],
                xr_sem.at[sems, a], rank_at(0, a, 0), across,
            )
            for a in range(2)
        ]

    def y_copies(t, c, out, into, send, recv):
        sems = t.g * CHUNKS + c
        return [
            remote(out.at[c, a], into.at[c, a], send.at[sems, a], recv.at[sems, a], dp, to)
            for a, to in enumerate((up, down))
        ]

    def y1_copies(t, c):
        return y_copies(t, c, t.y1_out, t.y1_in, y1s_sem, y1r_sem)

    def y2_copies(t, c):
        return y_copies(t, c, t.y2_out, t.y2_in, y2s_sem, y2r_sem)

    def sums(t, slot, at):
        return t.acc[slot, pl.ds(t.count * at, t.count)].reshape(t.rows, CHUNK)

    def multiply(t, i):
        c = i - t.g * CHUNKS
        slot = lax.rem(i, W_SLOTS)
        load(i).wait()

        @pl.when(i + W_SLOTS - 1 < STEPS)
        def _():
            load(i + W_SLOTS - 1).start()

        w = w_buf[slot]
        at = lax.rem(c, t.lags[2] + 1)
        if t.g == 0:
            both = jnp.dot(
                rows1[...].reshape(8 * UNIT, TP * VH), w, preferred_element_type=F32
            )
            t.x_out[c] = both[: 4 * UNIT].astype(BF16).reshape(2, 2 * UNIT, CHUNK)
            for copy in x_copies(t, c):
                copy.start()
            t.acc[at] = both[4 * UNIT :].reshape(4, UNIT, CHUNK)
        else:
            t.x_out[c] = (
                jnp.dot(away2[...].reshape(8 * UNIT, TP * VH), w, preferred_element_type=F32)
                .astype(BF16)
                .reshape(2, 4 * UNIT, CHUNK)
            )
            for copy in x_copies(t, c):
                copy.start()
            t.acc[at] = jnp.dot(
                keep2[...].reshape(8 * UNIT, TP * VH), w, preferred_element_type=F32
            ).reshape(8, UNIT, CHUNK)

    def after_x(t, c):
        slot = lax.rem(c, t.lags[2] + 1)
        for copy in x_copies(t, c):
            copy.wait_recv()
        for side in range(2):
            for half in range(2):
                for n in range(t.count):
                    p = 2 * half + side
                    home = SECOND[p][n] if t.g else FIRST[p]
                    t.acc[slot, home] = t.acc[slot, home] + t.x_in[
                        c, side, pl.ds((t.count * half + n) * UNIT, UNIT)
                    ].astype(F32)
        other = sums(t, slot, far_y).astype(BF16)
        t.y1_out[c, 0] = other[:, :HALF]
        t.y1_out[c, 1] = other[:, HALF:]
        for copy in y1_copies(t, c):
            copy.start()

    def after_y1(t, c):
        slot = lax.rem(c, t.lags[2] + 1)
        for copy in y1_copies(t, c):
            copy.wait_recv()
        to_up = sums(t, slot, up_y)
        t.y2_out[c, 0, :, :HALF] = (to_up[:, :HALF] + t.y1_in[c, 0].astype(F32)).astype(BF16)
        t.y2_out[c, 0, :, HALF:] = to_up[:, HALF:].astype(BF16)
        to_down = sums(t, slot, down_y)
        t.y2_out[c, 1, :, :HALF] = to_down[:, :HALF].astype(BF16)
        t.y2_out[c, 1, :, HALF:] = (to_down[:, HALF:] + t.y1_in[c, 1].astype(F32)).astype(BF16)
        for copy in y2_copies(t, c):
            copy.start()

    edge = (own_y == 0) | (own_y == 3)

    def after_y2(t, c):
        slot = lax.rem(c, t.lags[2] + 1)
        for copy in y2_copies(t, c):
            copy.wait_recv()
        start = pl.multiple_of(c * CHUNK, CHUNK)
        total = sums(t, slot, own_y) + t.y2_in[c, 0].astype(F32) + t.y2_in[c, 1].astype(F32)
        total = total.astype(BF16)
        if t.g == 0:
            thirds = [jnp.where(edge, 2, 1)]
        else:
            thirds = [0, jnp.where(edge, 1, 2)]
        for n, third in enumerate(thirds):
            out_ref[jnp.where(lo == 1, 2 - third, third), :, pl.ds(start, CHUNK)] = total[
                n * UNIT : (n + 1) * UNIT
            ]

    def later(t, i, least, most):
        for lag, stage in zip(t.lags, (after_x, after_y1, after_y2)):
            low = t.g * CHUNKS + lag
            if most > low and least < low + CHUNKS:

                @pl.when((i >= low) & (i < low + CHUNKS))
                def _(stage=stage, low=low):
                    stage(t, i - low)

    def first_step(i, carry):
        multiply(groups[0], i)
        later(groups[0], i, 0, CHUNKS)
        return carry

    def second_step(i, carry):
        multiply(groups[1], i)
        later(groups[0], i, CHUNKS, STEPS)
        later(groups[1], i, CHUNKS, STEPS)
        return carry

    def last_step(i, carry):
        later(groups[1], i, STEPS, STEPS + LAGS[1][2])
        return carry

    arrived(0)
    lax.fori_loop(0, CHUNKS, first_step, 0)
    arrived(1)
    lax.fori_loop(CHUNKS, STEPS, second_step, 0)
    lax.fori_loop(STEPS, STEPS + LAGS[1][2], last_step, 0)

    for copy in gathers:
        copy.wait_send()
    for way in others:
        spread(*way).wait_send()
        deliver(0, *way).wait_send()
        deliver(1, *way).wait_send()

    def drain(c, carry):
        for t in groups:
            for copy in x_copies(t, c) + y1_copies(t, c) + y2_copies(t, c):
                copy.wait_send()
        return carry

    lax.fori_loop(0, CHUNKS, drain, 0)


def sum_scratch(g):
    rows = GROUPS[g] * UNIT
    return [
        pltpu.VMEM((LAGS[g][2] + 1, 4 * GROUPS[g], UNIT, CHUNK), F32),
        pltpu.VMEM((CHUNKS, 2, 2 * rows, CHUNK), BF16),
        pltpu.VMEM((CHUNKS, 2, 2 * rows, CHUNK), BF16),
        pltpu.VMEM((CHUNKS, 2, rows, HALF), BF16),
        pltpu.VMEM((CHUNKS, 2, rows, HALF), BF16),
        pltpu.VMEM((CHUNKS, 2, rows, CHUNK), BF16),
        pltpu.VMEM((CHUNKS, 2, rows, CHUNK), BF16),
    ]


def on_device(queries, latent, segments, offsets, w_uk, w_uv, w_out):
    any_spec = pl.BlockSpec(memory_space=pl.ANY)
    smem_spec = pl.BlockSpec(memory_space=pltpu.SMEM)
    dma = pltpu.SemaphoreType.DMA
    out = pl.pallas_call(
        whole_kernel,
        out_shape=jax.ShapeDtypeStruct((3, UNIT, D), BF16),
        in_specs=[smem_spec] * 2 + [any_spec] * 5,
        out_specs=pl.BlockSpec(memory_space=pltpu.VMEM),
        scratch_shapes=[
            pltpu.VMEM((TP, OWN, KV), BF16),
            pltpu.VMEM((ROWS, HEADS * (NOPE + ROPE)), BF16),
            pltpu.VMEM((HEADS, NOPE, LAT), BF16),
            pltpu.VMEM((HEADS, LAT, VH), BF16),
            pltpu.VMEM((ROWS, 2 * ROPE), BF16),
            pltpu.VMEM((ROWS, 2 * ROPE), BF16),
            pltpu.VMEM((NB, BLK, WINDOW * BLK), F32),
            pltpu.VMEM((2, ROWS, 2 * NOPE), BF16),
            pltpu.VMEM((ROWS, 2 * VH), BF16),
            pltpu.VMEM((PAIRS, PARTS, 2, 3, UNIT, PART), BF16),
            pltpu.VMEM((DP, 2, 3, UNIT, PART), BF16),
            pltpu.VMEM((8, 3, UNIT, PART), BF16),
            pltpu.VMEM((8, 6, UNIT, PART), BF16),
            pltpu.VMEM((8, 1, UNIT, PART), BF16),
            pltpu.VMEM((8, 2, UNIT, PART), BF16),
            pltpu.VMEM((8, 3, UNIT, PART), BF16),
            pltpu.VMEM((8, 6, UNIT, PART), BF16),
            pltpu.VMEM((8, 1, UNIT, PART), BF16),
            pltpu.VMEM((8, 2, UNIT, PART), BF16),
            pltpu.VMEM((8, UNIT, TP * VH), BF16),
            pltpu.VMEM((8, UNIT, TP * VH), BF16),
            pltpu.VMEM((2, 4, UNIT, TP * VH), BF16),
            pltpu.VMEM((W_SLOTS, TP * VH, CHUNK), BF16),
        ]
        + sum_scratch(0)
        + sum_scratch(1)
        + [
            dma((4,)),
            dma((TP - 1,)),
            dma((TP - 1,)),
            dma((DP,)),
            dma((DP,)),
            dma((2 * DP,)),
            dma((2 * DP,)),
            dma((W_SLOTS,)),
        ]
        + [dma((STEPS, 2))] * 6,
        compiler_params=pltpu.CompilerParams(
            collective_id=0, has_side_effects=True, vmem_limit_bytes=58 * 2**20
        ),
        name="whole",
    )(segments, offsets, latent, queries, w_uk, w_uv, w_out)
    return out.reshape(OWN, D)


def solution(mesh):
    return jax.shard_map(
        on_device,
        mesh=mesh,
        in_specs=(
            P("dp", "tp"),
            P(("dp", "tp"), None),
            P(),
            P(),
            P("tp", None, None),
            P("tp", None, None),
            P("tp", None),
        ),
        out_specs=P(("dp", "tp"), None),
        check_vma=False,
    )
```

```python
import functools

import jax
import jax.numpy as jnp
from jax import lax
from jax.experimental import pallas as pl
from jax.experimental.pallas import tpu as pltpu
from jax.sharding import PartitionSpec as P

NOPE = 128
ROPE = 64
LAT = 512
VH = 128
BLK = 128
NB = 6
DP = 16
TP = 8
HEADS = 8
ROWS = NB * BLK
KV = LAT + ROPE
D = 7168
OWN = ROWS // TP
PARTS = 4
PAIRS = HEADS // 2
WINDOW = 4
UNIT = 32
PART = 256
SCALE = (NOPE + ROPE) ** (-0.5)
LOG2E = 1.4426950408889634

CHUNK = 512
CHUNKS = D // CHUNK
HALF = CHUNK // 2
STEPS = 2 * CHUNKS
W_SLOTS = 3
GROUPS = (1, 2)
LAGS = ((4, 7, 10), (3, 5, 8))
Y_FIRST = 6

MESH = pl.DeviceIdType.MESH
BF16 = jnp.bfloat16
F32 = jnp.float32


def ranks():
    return lax.axis_index("dp"), lax.axis_index("tp")


def remote(src, dst, send, recv, dp, tp):
    return pltpu.make_async_remote_copy(
        src_ref=src,
        dst_ref=dst,
        send_sem=send,
        recv_sem=recv,
        device_id={"dp": dp, "tp": tp},
        device_id_type=MESH,
    )


def greet(peers):
    barrier = pltpu.get_barrier_semaphore()
    for dp, tp in peers:
        pl.semaphore_signal(
            barrier, inc=1, device_id={"dp": dp, "tp": tp}, device_id_type=MESH
        )
    pl.semaphore_wait(barrier, len(peers))


def nt_dot(a, b):
    return lax.dot_general(a, b, (((1,), (1,)), ((), ())), preferred_element_type=F32)


HOME = ((11, 3, 6), (4, 0, 5), (7, 1, 9), (2, 10, 8))
FIRST = (3, 1, 2, 0)
SECOND = ((2, 4), (0, 3), (1, 6), (7, 5))
AWAY = ((2, 0, 1, 3), (0, 1, 3, 2))


def unit_of(p, e, u):
    y, third = divmod(HOME[p][u], 3)
    unit = 6 * y + third
    return 23 - unit if e else unit


PLACE = {
    unit_of(p, e, u): (p, e, u) for p in range(PARTS) for e in range(2) for u in range(3)
}


def choose(p, options):
    value = options[0]
    for i in range(1, PARTS):
        value = jnp.where(p == i, options[i], value)
    return value


def block_of(p, e, u):
    first = choose(p, [unit_of(i, 0, u) // 4 for i in range(PARTS)])
    return jnp.where(e == 1, NB - 1 - first, first)


def write_bias(seg_ref, bias, dp):
    row = lax.broadcasted_iota(jnp.int32, (BLK, BLK), 0)
    col = lax.broadcasted_iota(jnp.int32, (BLK, BLK), 1)
    for qb in range(NB):
        first = max(0, qb - WINDOW + 1)
        for kb in range(first, qb + 1):
            if kb == qb:
                block = jnp.where(col <= row, 0.0, -jnp.inf).astype(F32)
            else:
                same = seg_ref[dp, kb] == seg_ref[dp, qb]
                block = jnp.full((BLK, BLK), jnp.where(same, 0.0, -jnp.inf), F32)
            bias[qb, :, (kb - first) * BLK : (kb - first + 1) * BLK] = block


def attend_pair(pair, slab, rope_even, rope_odd, bias, q_ref, wuk_ref, wuv_ref, keys, values, parts):
    content = slab[:, :, :LAT].reshape(ROWS, LAT)
    up = wuk_ref[pl.ds(2 * pair, 2)].reshape(2 * NOPE, LAT)
    both = nt_dot(content, up)
    lane = lax.broadcasted_iota(jnp.int32, (ROWS, NOPE), 1)
    keys[0, :, :NOPE] = both[:, :NOPE].astype(BF16)
    keys[0, :, NOPE:] = rope_even[...]
    turned = pltpu.roll(both[:, NOPE:], 64, 1)
    keys[1, :, :NOPE] = jnp.where(lane < 64, 0.0, turned).astype(BF16)
    keys[1, :, NOPE:] = jnp.where(lane < 64, turned, rope_odd[...].astype(F32)).astype(BF16)
    for e in range(2):
        values[:, e * VH : (e + 1) * VH] = jnp.dot(
            content, wuv_ref[2 * pair + e], preferred_element_type=F32
        ).astype(BF16)
    for qb in range(NB):
        first = max(0, qb - WINDOW + 1)
        keep = pl.ds(first * BLK, (qb - first + 1) * BLK)
        for e in range(2):
            start = pl.multiple_of(pair * 384 + 128 * e, 128)
            q = q_ref[pl.ds(qb * BLK, BLK), pl.ds(start, 256)]
            s = nt_dot(q, keys[e, keep, :])
            s = s + bias[qb, :, : (qb - first + 1) * BLK]
            top = jnp.max(s, axis=1, keepdims=True)
            p = jnp.exp2((s - top) * (SCALE * LOG2E))
            total = jnp.sum(p, axis=1, keepdims=True)
            o = jnp.dot(
                p.astype(BF16), values[keep, e * VH : (e + 1) * VH], preferred_element_type=F32
            )
            o = (o / total).astype(BF16)
            for quarter in range(4):
                part, side, u = PLACE[4 * qb + quarter]
                parts[pair, part, side, u, :, e * VH : (e + 1) * VH] = o[
                    quarter * UNIT : (quarter + 1) * UNIT
                ]


def whole_kernel(
    seg_ref, off_ref, lat_hbm, q_hbm, wuk_hbm, wuv_hbm, w_hbm, out_ref,
    slab, q_ref, wuk_ref, wuv_ref, rope_even, rope_odd, bias, keys, values,
    parts, gathered, staged_near1, staged_near2, staged_far1, staged_far2, near1, near2, far1, far2,
    rows1, keep2, away2, w_buf,
    acc1, x_out1, x_in1, y1_out1, y1_in1, y2_out1, y2_in1,
    acc2, x_out2, x_in2, y1_out2, y1_in2, y2_out2, y2_in2,
    a1_out, a1_in, a2_out, a2_in, x2_out, x2_in,
    own_sem, ag_s, ag_r, p1_s, p1_r, p2_s, p2_r,
    w_sem, xs_sem, xr_sem, y1s_sem, y1r_sem, y2s_sem, y2r_sem,
    a1s_sem, a1r_sem, a2s_sem, a2r_sem, x2s_sem, x2r_sem,
):
    dp, tp = ranks()
    y, lo = tp // 2, lax.rem(tp, 2)
    hi, z, core = dp // 8, lax.rem(dp // 2, 4), lax.rem(dp, 2)
    across = 2 * y + 1 - lo
    own_y = jnp.where(lo == 1, 3 - y, y)
    step_y = jnp.where(lo == 1, 3, 1)
    up = 2 * lax.rem(y + step_y, 4) + lo
    down = 2 * lax.rem(y + 4 - step_y, 4) + lo
    up_y, down_y, far_y = lax.rem(own_y + 1, 4), lax.rem(own_y + 3, 4), lax.rem(own_y + 2, 4)

    def flip(bit, by):
        return bit + by - 2 * bit * by

    def rank_at(o, a, b):
        return flip(hi, a) * 8 + lax.rem(z + o, 4) * 2 + flip(core, b)

    def load(c):
        start = pl.multiple_of(lax.rem(c, CHUNKS) * CHUNK, CHUNK)
        slot = lax.rem(c, W_SLOTS)
        return pltpu.make_async_copy(
            w_hbm.at[:, pl.ds(start, CHUNK)], w_buf.at[slot], w_sem.at[slot]
        )

    loads = [
        pltpu.make_async_copy(lat_hbm, slab.at[tp], own_sem.at[0]),
        pltpu.make_async_copy(wuk_hbm, wuk_ref, own_sem.at[1]),
        pltpu.make_async_copy(wuv_hbm, wuv_ref, own_sem.at[2]),
        pltpu.make_async_copy(q_hbm, q_ref, own_sem.at[3]),
    ]
    for copy in loads:
        copy.start()
    for c in range(W_SLOTS - 1):
        load(c).start()

    greet(
        [(dp, lax.rem(tp + o, TP)) for o in range(1, TP)]
        + [(lax.rem(dp + o, DP), tp) for o in range(1, DP)]
        + [(lax.rem(dp + DP // 2, DP), across)]
    )

    opposite = 2 * lax.rem(y + 2, 4) + lo
    after, before = 2 * lax.rem(y + 1, 4) + lo, 2 * lax.rem(y + 3, 4) + lo

    def hand(index, src, at, to):
        return remote(src, slab.at[at], ag_s.at[index], ag_r.at[index], dp, to)

    gathers = [
        hand(0, lat_hbm, tp, opposite),
        hand(1, lat_hbm, tp, across),
        hand(2, lat_hbm, tp, after),
        hand(3, lat_hbm, tp, before),
        hand(4, slab.at[across], across, after),
        hand(5, slab.at[across], across, before),
        hand(6, slab.at[opposite], opposite, across),
    ]
    for copy in gathers[:4]:
        copy.start()
    gathers[1].wait_recv()
    gathers[4].start()
    gathers[5].start()
    gathers[0].wait_recv()
    gathers[6].start()
    write_bias(seg_ref, bias, dp)
    for copy in loads:
        copy.wait()
    for copy in gathers[2:]:
        copy.wait_recv()
    rope = slab[:, :, LAT:].reshape(ROWS, ROPE)
    blank = jnp.zeros((ROWS, ROPE), BF16)
    rope_even[...] = jnp.concatenate([rope, blank], axis=1)
    rope_odd[...] = jnp.concatenate([blank, rope], axis=1)

    def spread(o, a, b):
        pair = lax.rem(z + o, 4)
        part = 2 * flip(core, b) + flip(hi, a)
        at = o * 4 + a * 2 + b
        return remote(
            parts.at[pair, part], gathered.at[dp], p1_s.at[at], p1_r.at[at], rank_at(o, a, b), tp
        )

    own_part = pltpu.make_async_copy(
        parts.at[z, 2 * core + hi], gathered.at[dp], p1_s.at[0]
    )

    def attend_step(i, carry):
        o = jnp.where(i == 0, 2, jnp.where(i == 1, 1, jnp.where(i == 2, 3, 0)))
        attend_pair(
            lax.rem(z + o, 4), slab, rope_even, rope_odd, bias, q_ref, wuk_ref, wuv_ref,
            keys, values, parts,
        )
        for a, b in ((1, 0), (1, 1), (0, 1)):
            spread(o, a, b).start()

        @pl.when(o != 0)
        def _():
            spread(o, 0, 0).start()

        return carry

    lax.fori_loop(0, PAIRS, attend_step, 0)
    own_part.start()
    ways = [(o, a, b) for o in (2, 1, 3, 0) for a in (1, 0) for b in (1, 0)]
    others = [way for way in ways if way != (0, 0, 0)]
    for way in others:
        spread(*way).wait_recv()
    own_part.wait()

    part = 2 * core + hi
    staged_near, staged_far = (staged_near1, staged_near2), (staged_far1, staged_far2)
    near, far = (near1, near2), (far1, far2)

    def taken(rank, e, u):
        source = lax.rem(rank + DP - off_ref[block_of(part, e, u)], DP)
        return gathered[source, e, u]

    def deliver(g, o, a, b):
        at = g * DP + o * 4 + a * 2 + b
        src = (staged_far if a else staged_near)[g].at[2 * o + b]
        dst = (far if a else near)[g].at[2 * z + core]
        return remote(src, dst, p2_s.at[at], p2_r.at[at], rank_at(o, a, b), tp)

    for g, units in enumerate(((0,), (1, 2))):
        for o, a, b in ways:
            rank = rank_at(o, a, b)
            own = (o, a, b) == (0, 0, 0)
            if a:
                target, index = staged_far[g], 2 * o + b
            elif own:
                target, index = near[g], 2 * z + core
            else:
                target, index = staged_near[g], 2 * o + b
            count = len(units)
            for n, u in enumerate(units):
                target[index, n] = taken(rank, lo, u)
            if not a:
                for side in range(2):
                    for n, u in enumerate(units):
                        target[index, count * (1 + side) + n] = taken(
                            rank + (side - hi) * 8, 1 - lo, u
                        )
            if not own:
                deliver(g, o, a, b).start()

    def arrived(g):
        for way in others:
            deliver(g, *way).wait_recv()
        count = g + 1
        for pair in range(PAIRS):
            columns = pl.ds(pair * PART, PART)
            for c in range(2):
                for n in range(count):
                    for a in range(2):
                        mine, yours = 2 * c + a, 2 * c + 1 - a
                        unit = (far if a else near)[g][2 * pair + c, n]
                        if g == 0:
                            home = jnp.where(hi == 0, FIRST[mine], FIRST[yours])
                            rows1[4 + home, :, columns] = unit
                        else:
                            home = jnp.where(hi == 0, SECOND[mine][n], SECOND[yours][n])
                            keep2[home, :, columns] = unit
                    for side in range(2):
                        unit = near[g][2 * pair + c, count * (1 + side) + n]
                        if g == 0:
                            rows1[2 * side + c, :, columns] = unit
                        else:
                            away2[side, 2 * c + n, :, columns] = unit

    class Group:
        pass

    groups = []
    for g, (acc, x_out, x_in, y1_out, y1_in, y2_out, y2_in) in enumerate(
        (
            (acc1, x_out1, x_in1, y1_out1, y1_in1, y2_out1, y2_in1),
            (acc2, x_out2, x_in2, y1_out2, y1_in2, y2_out2, y2_in2),
        )
    ):
        t = Group()
        t.acc, t.x_out, t.x_in, t.y1_out, t.y1_in, t.y2_out, t.y2_in = (
            acc, x_out, x_in, y1_out, y1_in, y2_out, y2_in,
        )
        t.g, t.count, t.rows, t.lags = g, GROUPS[g], GROUPS[g] * UNIT, LAGS[g]
        groups.append(t)

    def x_copies(t, c):
        sems = t.g * CHUNKS + c
        return [
            remote(
                t.x_out.at[c, flip(hi, a)], t.x_in.at[c, hi], xs_sem.at[sems, a],
                xr_sem.at[sems, a], rank_at(0, a, 0), across,
            )
            for a in range(2)
        ]

    def y_copies(t, c, out, into, send, recv):
        sems = t.g * CHUNKS + c
        return [
            remote(out.at[c, a], into.at[c, a], send.at[sems, a], recv.at[sems, a], dp, to)
            for a, to in enumerate((up, down))
        ]

    def y1_copies(t, c):
        return y_copies(t, c, t.y1_out, t.y1_in, y1s_sem, y1r_sem)

    def y2_copies(t, c):
        return y_copies(t, c, t.y2_out, t.y2_in, y2s_sem, y2r_sem)

    def sums(t, slot, at):
        return t.acc[slot, pl.ds(t.count * at, t.count)].reshape(t.rows, CHUNK)

    def multiply(t, i):
        c = i - t.g * CHUNKS
        slot = lax.rem(i, W_SLOTS)
        load(i).wait()

        @pl.when(i + W_SLOTS - 1 < STEPS)
        def _():
            load(i + W_SLOTS - 1).start()

        w = w_buf[slot]
        at = lax.rem(c, t.lags[2] + 1)
        if t.g == 0:
            both = jnp.dot(
                rows1[...].reshape(8 * UNIT, TP * VH), w, preferred_element_type=F32
            )
            t.x_out[c] = both[: 4 * UNIT].astype(BF16).reshape(2, 2, UNIT, CHUNK)
            for copy in x_copies(t, c):
                copy.start()
            t.acc[at] = both[4 * UNIT :].reshape(4, UNIT, CHUNK)
        else:
            t.x_out[c] = (
                jnp.dot(away2[...].reshape(8 * UNIT, TP * VH), w, preferred_element_type=F32)
                .astype(BF16)
                .reshape(2, 4, UNIT, CHUNK)
            )
            start_x(t, c)
            start_y_first(t, c)
            t.acc[at] = jnp.dot(
                keep2[...].reshape(8 * UNIT, TP * VH), w, preferred_element_type=F32
            ).reshape(8, UNIT, CHUNK)

    def goes_over_x(t, c, to):
        return (c >= Y_FIRST) | (lax.rem(c, 2) != to)

    def start_x(t, c):
        for a, copy in enumerate(x_copies(t, c)):
            pl.when(goes_over_x(t, c, flip(hi, a)))(copy.start)

    def away_unit(c, to):
        at = choose(3 - to, [jnp.where(hi == 0, AWAY[0][i], AWAY[1][i]) for i in range(4)])
        return x_out2[c, lax.rem(c, 2), at]

    def a1_copies(c):
        return [
            remote(a1_out.at[c, a], a1_in.at[c, a], a1s_sem.at[c, a], a1r_sem.at[c, a], dp, to)
            for a, to in enumerate((up, down))
        ]

    def a2_copies(c):
        return [
            remote(a2_out.at[c, a], a2_in.at[c, a], a2s_sem.at[c, a], a2r_sem.at[c, a], dp, to)
            for a, to in enumerate((up, down))
        ]

    def x2_copy(c):
        rank = lax.rem(c, 2) * 8 + 2 * z + core
        return remote(x2_out.at[c], x2_in.at[c, hi], x2s_sem.at[c], x2r_sem.at[c, hi], rank, across)

    def start_y_first(t, c):
        @pl.when(c < Y_FIRST)
        def _():
            other = away_unit(c, far_y)
            a1_out[c, 0] = other[:, :HALF]
            a1_out[c, 1] = other[:, HALF:]
            for copy in a1_copies(c):
                copy.start()

    def after_a1(t, c):
        for copy in a1_copies(c):
            copy.wait_recv()
        to_up = away_unit(c, up_y)
        a2_out[c, 0, :, :HALF] = (
            to_up[:, :HALF].astype(F32) + a1_in[c, 0].astype(F32)
        ).astype(BF16)
        a2_out[c, 0, :, HALF:] = to_up[:, HALF:]
        to_down = away_unit(c, down_y)
        a2_out[c, 1, :, :HALF] = to_down[:, :HALF]
        a2_out[c, 1, :, HALF:] = (
            to_down[:, HALF:].astype(F32) + a1_in[c, 1].astype(F32)
        ).astype(BF16)
        for copy in a2_copies(c):
            copy.start()

    def after_a2(t, c):
        for copy in a2_copies(c):
            copy.wait_recv()
        x2_out[c] = (
            away_unit(c, own_y).astype(F32) + a2_in[c, 0].astype(F32) + a2_in[c, 1].astype(F32)
        ).astype(BF16)
        x2_copy(c).start()

    def add_x(t, c):
        slot = lax.rem(c, t.lags[2] + 1)
        for copy in x_copies(t, c):
            copy.wait_recv()
        for side in range(2):
            for half in range(2):
                for n in range(t.count):
                    p = 2 * half + side
                    home = SECOND[p][n] if t.g else FIRST[p]
                    t.acc[slot, home] = t.acc[slot, home] + t.x_in[
                        c, side, t.count * half + n
                    ].astype(F32)

    def after_x(t, c):
        if t.g == 0:
            add_x(t, c)
        else:
            pl.when(goes_over_x(t, c, hi))(lambda: add_x(t, c))
        slot = lax.rem(c, t.lags[2] + 1)
        other = sums(t, slot, far_y).astype(BF16)
        t.y1_out[c, 0] = other[:, :HALF]
        t.y1_out[c, 1] = other[:, HALF:]
        for copy in y1_copies(t, c):
            copy.start()

    def after_y1(t, c):
        slot = lax.rem(c, t.lags[2] + 1)
        for copy in y1_copies(t, c):
            copy.wait_recv()
        to_up = sums(t, slot, up_y)
        t.y2_out[c, 0, :, :HALF] = (to_up[:, :HALF] + t.y1_in[c, 0].astype(F32)).astype(BF16)
        t.y2_out[c, 0, :, HALF:] = to_up[:, HALF:].astype(BF16)
        to_down = sums(t, slot, down_y)
        t.y2_out[c, 1, :, :HALF] = to_down[:, :HALF].astype(BF16)
        t.y2_out[c, 1, :, HALF:] = (to_down[:, HALF:] + t.y1_in[c, 1].astype(F32)).astype(BF16)
        for copy in y2_copies(t, c):
            copy.start()

    edge = (own_y == 0) | (own_y == 3)

    def after_y2(t, c):
        slot = lax.rem(c, t.lags[2] + 1)
        for copy in y2_copies(t, c):
            copy.wait_recv()
        start = pl.multiple_of(c * CHUNK, CHUNK)
        if t.g == 0:
            thirds = [jnp.where(edge, 2, 1)]
        else:
            thirds = [0, jnp.where(edge, 1, 2)]

        def finish(more):
            total = sums(t, slot, own_y) + t.y2_in[c, 0].astype(F32) + t.y2_in[c, 1].astype(F32)
            for n, third in enumerate(thirds):
                unit = total[n * UNIT : (n + 1) * UNIT]
                if more:
                    side = jnp.where(own_y == 0, 1 - n, n)
                    unit = unit + x2_in[c, side].astype(F32)
                out_ref[jnp.where(lo == 1, 2 - third, third), :, pl.ds(start, CHUNK)] = (
                    unit.astype(BF16)
                )

        if t.g == 0:
            finish(False)
        else:
            over_x = goes_over_x(t, c, hi)
            pl.when(over_x)(lambda: finish(False))

            @pl.when(jnp.logical_not(over_x))
            def _():
                for side in range(2):
                    remote(
                        x2_out.at[c], x2_in.at[c, side], x2s_sem.at[c], x2r_sem.at[c, side],
                        dp, across,
                    ).wait_recv()
                finish(True)

    def later(t, i, least, most):
        for lag, stage in zip(t.lags, (after_x, after_y1, after_y2)):
            low = t.g * CHUNKS + lag
            if most > low and least < low + CHUNKS:

                @pl.when((i >= low) & (i < low + CHUNKS))
                def _(stage=stage, low=low):
                    stage(t, i - low)

        if t.g == 1:
            for lag, stage in zip(t.lags[:2], (after_a1, after_a2)):
                low = CHUNKS + lag

                @pl.when((i >= low) & (i < low + Y_FIRST))
                def _(stage=stage, low=low):
                    stage(t, i - low)

    def first_step(i, carry):
        multiply(groups[0], i)
        later(groups[0], i, 0, CHUNKS)
        return carry

    def second_step(i, carry):
        multiply(groups[1], i)
        later(groups[0], i, CHUNKS, STEPS)
        later(groups[1], i, CHUNKS, STEPS)
        return carry

    def last_step(i, carry):
        later(groups[1], i, STEPS, STEPS + LAGS[1][2])
        return carry

    arrived(0)
    lax.fori_loop(0, CHUNKS, first_step, 0)
    arrived(1)
    lax.fori_loop(CHUNKS, STEPS, second_step, 0)
    lax.fori_loop(STEPS, STEPS + LAGS[1][2], last_step, 0)

    for copy in gathers:
        copy.wait_send()
    for way in others:
        spread(*way).wait_send()
        deliver(0, *way).wait_send()
        deliver(1, *way).wait_send()

    def drain(c, carry):
        for t in groups:
            for copy in y1_copies(t, c) + y2_copies(t, c):
                copy.wait_send()
        for copy in x_copies(groups[0], c):
            copy.wait_send()
        for a, copy in enumerate(x_copies(groups[1], c)):
            pl.when(goes_over_x(groups[1], c, flip(hi, a)))(copy.wait_send)

        @pl.when(c < Y_FIRST)
        def _():
            for copy in a1_copies(c) + a2_copies(c) + [x2_copy(c)]:
                copy.wait_send()

        return carry

    lax.fori_loop(0, CHUNKS, drain, 0)


def sum_scratch(g):
    rows = GROUPS[g] * UNIT
    return [
        pltpu.VMEM((LAGS[g][2] + 1, 4 * GROUPS[g], UNIT, CHUNK), F32),
        pltpu.VMEM((CHUNKS, 2, 2 * GROUPS[g], UNIT, CHUNK), BF16),
        pltpu.VMEM((CHUNKS, 2, 2 * GROUPS[g], UNIT, CHUNK), BF16),
        pltpu.VMEM((CHUNKS, 2, rows, HALF), BF16),
        pltpu.VMEM((CHUNKS, 2, rows, HALF), BF16),
        pltpu.VMEM((CHUNKS, 2, rows, CHUNK), BF16),
        pltpu.VMEM((CHUNKS, 2, rows, CHUNK), BF16),
    ]


def on_device(queries, latent, segments, offsets, w_uk, w_uv, w_out):
    any_spec = pl.BlockSpec(memory_space=pl.ANY)
    smem_spec = pl.BlockSpec(memory_space=pltpu.SMEM)
    dma = pltpu.SemaphoreType.DMA
    out = pl.pallas_call(
        whole_kernel,
        out_shape=jax.ShapeDtypeStruct((3, UNIT, D), BF16),
        in_specs=[smem_spec] * 2 + [any_spec] * 5,
        out_specs=pl.BlockSpec(memory_space=pltpu.VMEM),
        scratch_shapes=[
            pltpu.VMEM((TP, OWN, KV), BF16),
            pltpu.VMEM((ROWS, HEADS * (NOPE + ROPE)), BF16),
            pltpu.VMEM((HEADS, NOPE, LAT), BF16),
            pltpu.VMEM((HEADS, LAT, VH), BF16),
            pltpu.VMEM((ROWS, 2 * ROPE), BF16),
            pltpu.VMEM((ROWS, 2 * ROPE), BF16),
            pltpu.VMEM((NB, BLK, WINDOW * BLK), F32),
            pltpu.VMEM((2, ROWS, 2 * NOPE), BF16),
            pltpu.VMEM((ROWS, 2 * VH), BF16),
            pltpu.VMEM((PAIRS, PARTS, 2, 3, UNIT, PART), BF16),
            pltpu.VMEM((DP, 2, 3, UNIT, PART), BF16),
            pltpu.VMEM((8, 3, UNIT, PART), BF16),
            pltpu.VMEM((8, 6, UNIT, PART), BF16),
            pltpu.VMEM((8, 1, UNIT, PART), BF16),
            pltpu.VMEM((8, 2, UNIT, PART), BF16),
            pltpu.VMEM((8, 3, UNIT, PART), BF16),
            pltpu.VMEM((8, 6, UNIT, PART), BF16),
            pltpu.VMEM((8, 1, UNIT, PART), BF16),
            pltpu.VMEM((8, 2, UNIT, PART), BF16),
            pltpu.VMEM((8, UNIT, TP * VH), BF16),
            pltpu.VMEM((8, UNIT, TP * VH), BF16),
            pltpu.VMEM((2, 4, UNIT, TP * VH), BF16),
            pltpu.VMEM((W_SLOTS, TP * VH, CHUNK), BF16),
        ]
        + sum_scratch(0)
        + sum_scratch(1)
        + [
            pltpu.VMEM((Y_FIRST, 2, UNIT, HALF), BF16),
            pltpu.VMEM((Y_FIRST, 2, UNIT, HALF), BF16),
            pltpu.VMEM((Y_FIRST, 2, UNIT, CHUNK), BF16),
            pltpu.VMEM((Y_FIRST, 2, UNIT, CHUNK), BF16),
            pltpu.VMEM((Y_FIRST, UNIT, CHUNK), BF16),
            pltpu.VMEM((Y_FIRST, 2, UNIT, CHUNK), BF16),
            dma((4,)),
            dma((TP - 1,)),
            dma((TP - 1,)),
            dma((DP,)),
            dma((DP,)),
            dma((2 * DP,)),
            dma((2 * DP,)),
            dma((W_SLOTS,)),
        ]
        + [dma((STEPS, 2))] * 6
        + [dma((Y_FIRST, 2))] * 4
        + [dma((Y_FIRST,)), dma((Y_FIRST, 2))],
        compiler_params=pltpu.CompilerParams(
            collective_id=0, has_side_effects=True, vmem_limit_bytes=58 * 2**20
        ),
        name="whole",
    )(segments, offsets, latent, queries, w_uk, w_uv, w_out)
    return out.reshape(OWN, D)


def solution(mesh):
    return jax.shard_map(
        on_device,
        mesh=mesh,
        in_specs=(
            P("dp", "tp"),
            P(("dp", "tp"), None),
            P(),
            P(),
            P("tp", None, None),
            P("tp", None, None),
            P("tp", None),
        ),
        out_specs=P(("dp", "tp"), None),
        check_vma=False,
    )
```

```python
import functools

import jax
import jax.numpy as jnp
from jax import lax
from jax.experimental import pallas as pl
from jax.experimental.pallas import tpu as pltpu
from jax.sharding import PartitionSpec as P

NOPE = 128
ROPE = 64
LAT = 512
VH = 128
BLK = 128
NB = 6
DP = 16
TP = 8
HEADS = 8
ROWS = NB * BLK
KV = LAT + ROPE
D = 7168
OWN = ROWS // TP
PARTS = 4
PAIRS = HEADS // 2
WINDOW = 4
UNIT = 32
PART = 256
SCALE = (NOPE + ROPE) ** (-0.5)
LOG2E = 1.4426950408889634

CHUNK = 512
CHUNKS = D // CHUNK
HALF = CHUNK // 2
STEPS = 2 * CHUNKS
W_SLOTS = 3
GROUPS = (1, 2)
LAGS = ((4, 7, 10), (3, 5, 8))
Y_FIRST = 5
AHEAD = 3
DELIVER_AT = 5

MESH = pl.DeviceIdType.MESH
BF16 = jnp.bfloat16
F32 = jnp.float32


def ranks():
    return lax.axis_index("dp"), lax.axis_index("tp")


def remote(src, dst, send, recv, dp, tp):
    return pltpu.make_async_remote_copy(
        src_ref=src,
        dst_ref=dst,
        send_sem=send,
        recv_sem=recv,
        device_id={"dp": dp, "tp": tp},
        device_id_type=MESH,
    )


def greet(peers):
    barrier = pltpu.get_barrier_semaphore()
    for dp, tp in peers:
        pl.semaphore_signal(
            barrier, inc=1, device_id={"dp": dp, "tp": tp}, device_id_type=MESH
        )
    pl.semaphore_wait(barrier, len(peers))


def nt_dot(a, b):
    return lax.dot_general(a, b, (((1,), (1,)), ((), ())), preferred_element_type=F32)


HOME = ((11, 3, 6), (4, 0, 5), (7, 1, 9), (2, 10, 8))
FIRST = (3, 1, 2, 0)
SECOND = ((2, 4), (0, 3), (1, 6), (7, 5))
AWAY = ((2, 0, 1, 3), (0, 1, 3, 2))


def unit_of(p, e, u):
    y, third = divmod(HOME[p][u], 3)
    unit = 6 * y + third
    return 23 - unit if e else unit


PLACE = {
    unit_of(p, e, u): (p, e, u) for p in range(PARTS) for e in range(2) for u in range(3)
}


HOLDS = (
    tuple(((FIRST.index(y) % 2, FIRST.index(y) // 2),) for y in range(4)),
    tuple(
        tuple(
            (p % 2, 2 * (p // 2) + n)
            for home in (2 * y, 2 * y + 1)
            for p in range(PARTS)
            for n in range(2)
            if SECOND[p][n] == home
        )
        for y in range(4)
    ),
)


def choose(p, options):
    value = options[0]
    for i in range(1, PARTS):
        value = jnp.where(p == i, options[i], value)
    return value


def block_of(p, e, u):
    first = choose(p, [unit_of(i, 0, u) // 4 for i in range(PARTS)])
    return jnp.where(e == 1, NB - 1 - first, first)


def write_bias(seg_ref, bias, dp):
    row = lax.broadcasted_iota(jnp.int32, (BLK, BLK), 0)
    col = lax.broadcasted_iota(jnp.int32, (BLK, BLK), 1)
    for qb in range(NB):
        first = max(0, qb - WINDOW + 1)
        for kb in range(first, qb + 1):
            if kb == qb:
                block = jnp.where(col <= row, 0.0, -jnp.inf).astype(F32)
            else:
                same = seg_ref[kb, dp] == seg_ref[qb, dp]
                block = jnp.full((BLK, BLK), jnp.where(same, 0.0, -jnp.inf), F32)
            bias[qb, :, (kb - first) * BLK : (kb - first + 1) * BLK] = block


def attend_pair(pair, slab, rope_even, rope_odd, bias, q_ref, wuk_ref, wuv_ref, keys, values, parts1, parts2):
    content = slab[:, :, :LAT].reshape(ROWS, LAT)
    up = wuk_ref[pl.ds(2 * pair, 2)].reshape(2 * NOPE, LAT)
    both = nt_dot(content, up)
    lane = lax.broadcasted_iota(jnp.int32, (ROWS, NOPE), 1)
    keys[0, :, :NOPE] = both[:, :NOPE].astype(BF16)
    keys[0, :, NOPE:] = rope_even[...]
    turned = pltpu.roll(both[:, NOPE:], 64, 1)
    keys[1, :, :NOPE] = jnp.where(lane < 64, 0.0, turned).astype(BF16)
    keys[1, :, NOPE:] = jnp.where(lane < 64, turned, rope_odd[...].astype(F32)).astype(BF16)
    for e in range(2):
        values[e, :, :VH] = jnp.dot(
            content, wuv_ref[2 * pair + e], preferred_element_type=F32
        ).astype(BF16)

    def window(qb):
        first = max(0, qb - WINDOW + 1)
        return pl.ds(first * BLK, (qb - first + 1) * BLK), (qb - first + 1) * BLK

    def score(qb, e):
        keep, width = window(qb)
        start = pl.multiple_of(pair * 384 + 128 * e, 128)
        q = q_ref[pl.ds(qb * BLK, BLK), pl.ds(start, 256)]
        return nt_dot(q, keys[e, keep, :]) + bias[qb, :, :width]

    def finish(qb, e, s):
        keep, _ = window(qb)
        top = jnp.max(s, axis=1, keepdims=True)
        p = jnp.exp2((s - top) * (SCALE * LOG2E)).astype(BF16)
        o = jnp.dot(p, values[e, keep, :], preferred_element_type=F32)
        o = (o[:, :VH] / o[:, VH:]).astype(BF16)
        for quarter in range(4):
            part, side, u = PLACE[4 * qb + quarter]
            target, n = (parts2, u - 1) if u else (parts1, 0)
            target[pair, part, side, n, :, e * VH : (e + 1) * VH] = o[
                quarter * UNIT : (quarter + 1) * UNIT
            ]

    units = [(qb, e) for qb in range(NB) for e in range(2)]
    waiting = []
    for unit in units:
        waiting.append((*unit, score(*unit)))
        if len(waiting) > AHEAD:
            finish(*waiting.pop(0))
    for held in waiting:
        finish(*held)


def whole_kernel(
    seg_ref, off_ref, lat_hbm, q_hbm, wuk_hbm, wuv_hbm, w_hbm, out_ref,
    slab, q_ref, wuk_ref, wuv_ref, rope_even, rope_odd, bias, keys, values,
    parts1, parts2, gathered1, gathered2, staged_near1, staged_near2, staged_far1, staged_far2, near1, near2, far1, far2,
    rows1, keep2, away2, w_buf,
    acc1, x_out1, x_in1, y1_out1, y1_in1, y2_out1, y2_in1,
    acc2, x_out2, x_in2, y1_out2, y1_in2, y2_out2, y2_in2,
    a1_out, a1_in, a2_out, a2_in, x2_out, x2_in,
    own_sem, ag_s, ag_r, p1_s, p1_r, p2_s, p2_r,
    w_sem, xs_sem, xr_sem, y1s_sem, y1r_sem, y2s_sem, y2r_sem,
    a1s_sem, a1r_sem, a2s_sem, a2r_sem, x2s_sem, x2r_sem,
):
    dp, tp = ranks()
    y, lo = tp // 2, lax.rem(tp, 2)
    hi, z, core = dp // 8, lax.rem(dp // 2, 4), lax.rem(dp, 2)
    across = 2 * y + 1 - lo
    own_y = jnp.where(lo == 1, 3 - y, y)
    step_y = jnp.where(lo == 1, 3, 1)
    up = 2 * lax.rem(y + step_y, 4) + lo
    down = 2 * lax.rem(y + 4 - step_y, 4) + lo
    up_y, down_y, far_y = lax.rem(own_y + 1, 4), lax.rem(own_y + 3, 4), lax.rem(own_y + 2, 4)

    def flip(bit, by):
        return bit + by - 2 * bit * by

    def rank_at(o, a, b):
        return flip(hi, a) * 8 + lax.rem(z + o, 4) * 2 + flip(core, b)

    def load(c):
        start = pl.multiple_of(lax.rem(c, CHUNKS) * CHUNK, CHUNK)
        slot = lax.rem(c, W_SLOTS)
        return pltpu.make_async_copy(
            w_hbm.at[:, pl.ds(start, CHUNK)], w_buf.at[slot], w_sem.at[slot]
        )

    loads = [
        pltpu.make_async_copy(lat_hbm, slab.at[tp], own_sem.at[0]),
        pltpu.make_async_copy(wuk_hbm, wuk_ref, own_sem.at[1]),
        pltpu.make_async_copy(wuv_hbm, wuv_ref, own_sem.at[2]),
        pltpu.make_async_copy(q_hbm, q_ref, own_sem.at[3]),
    ]
    for copy in loads:
        copy.start()
    for c in range(W_SLOTS - 1):
        load(c).start()

    greet(
        [(dp, lax.rem(tp + o, TP)) for o in range(1, TP)]
        + [(lax.rem(dp + o, DP), tp) for o in range(1, DP)]
        + [(lax.rem(dp + DP // 2, DP), across)]
    )

    opposite = 2 * lax.rem(y + 2, 4) + lo
    after, before = 2 * lax.rem(y + 1, 4) + lo, 2 * lax.rem(y + 3, 4) + lo

    def hand(index, src, at, to):
        return remote(src, slab.at[at], ag_s.at[index], ag_r.at[index], dp, to)

    gathers = [
        hand(0, lat_hbm, tp, opposite),
        hand(1, lat_hbm, tp, across),
        hand(2, lat_hbm, tp, after),
        hand(3, lat_hbm, tp, before),
        hand(4, slab.at[across], across, after),
        hand(5, slab.at[across], across, before),
        hand(6, slab.at[opposite], opposite, across),
    ]
    for copy in gathers[:4]:
        copy.start()
    gathers[1].wait_recv()
    gathers[4].start()
    gathers[5].start()
    gathers[0].wait_recv()
    gathers[6].start()
    write_bias(seg_ref, bias, dp)
    for copy in loads:
        copy.wait()
    for copy in gathers[2:]:
        copy.wait_recv()
    rope = slab[:, :, LAT:].reshape(ROWS, ROPE)
    blank = jnp.zeros((ROWS, ROPE), BF16)
    rope_even[...] = jnp.concatenate([rope, blank], axis=1)
    rope_odd[...] = jnp.concatenate([blank, rope], axis=1)
    values[:, :, VH:] = jnp.ones((2, ROWS, VH), BF16)

    parts, gathered = (parts1, parts2), (gathered1, gathered2)

    def spread(g, o, a, b):
        pair = lax.rem(z + o, 4)
        part = 2 * flip(core, b) + flip(hi, a)
        at = g * DP + o * 4 + a * 2 + b
        return remote(
            parts[g].at[pair, part], gathered[g].at[dp], p1_s.at[at], p1_r.at[at],
            rank_at(o, a, b), tp,
        )

    def own_part(g):
        return pltpu.make_async_copy(
            parts[g].at[z, 2 * core + hi], gathered[g].at[dp], p1_s.at[g * DP]
        )

    def attend_step(i, carry):
        o = jnp.where(i == 0, 2, jnp.where(i == 1, 1, jnp.where(i == 2, 3, 0)))
        attend_pair(
            lax.rem(z + o, 4), slab, rope_even, rope_odd, bias, q_ref, wuk_ref, wuv_ref,
            keys, values, parts1, parts2,
        )
        for a, b in ((1, 0), (1, 1), (0, 1)):
            spread(0, o, a, b).start()

        @pl.when(o != 0)
        def _():
            spread(0, o, 0, 0).start()

        return carry

    ways = [(o, a, b) for o in (2, 1, 3, 0) for a in (1, 0) for b in (1, 0)]
    others = [way for way in ways if way != (0, 0, 0)]

    def spread_second(a):
        for way in others:
            if way[1] == a:
                spread(1, *way).start()

    def spread_done(g):
        for way in others:
            spread(g, *way).wait_recv()
        own_part(g).wait()

    lax.fori_loop(0, PAIRS, attend_step, 0)
    own_part(0).start()
    own_part(1).start()
    spread_second(1)
    spread_done(0)

    part = 2 * core + hi
    staged_near, staged_far = (staged_near1, staged_near2), (staged_far1, staged_far2)
    near, far = (near1, near2), (far1, far2)

    def taken(rank, e, u):
        source = lax.rem(rank + DP - off_ref[block_of(part, e, u)], DP)
        return gathered2[source, e, u - 1] if u else gathered1[source, e, 0]

    def deliver(g, o, a, b):
        at = g * DP + o * 4 + a * 2 + b
        src = (staged_far if a else staged_near)[g].at[2 * o + b]
        dst = (far if a else near)[g].at[2 * z + core]
        return remote(src, dst, p2_s.at[at], p2_r.at[at], rank_at(o, a, b), tp)

    def deliver_all(g):
        units = ((0,), (1, 2))[g]
        count = len(units)
        for o, a, b in ways:
            rank = rank_at(o, a, b)
            own = (o, a, b) == (0, 0, 0)
            if a:
                target, index = staged_far[g], 2 * o + b
            elif own:
                target, index = near[g], 2 * z + core
            else:
                target, index = staged_near[g], 2 * o + b
            for n, u in enumerate(units):
                target[index, n] = taken(rank, lo, u)
            if not a:
                for side in range(2):
                    for n, u in enumerate(units):
                        target[index, count * (1 + side) + n] = taken(
                            rank + (side - hi) * 8, 1 - lo, u
                        )
            if not own:
                deliver(g, o, a, b).start()

    def arrived(g):
        for way in others:
            deliver(g, *way).wait_recv()
        if g == 0:
            spread_second(0)
        count = g + 1
        for pair in range(PAIRS):
            columns = pl.ds(pair * PART, PART)
            for c in range(2):
                for n in range(count):
                    for a in range(2):
                        mine, yours = 2 * c + a, 2 * c + 1 - a
                        unit = (far if a else near)[g][2 * pair + c, n]
                        if g == 0:
                            home = jnp.where(hi == 0, FIRST[mine], FIRST[yours])
                            rows1[4 + home, :, columns] = unit
                        else:
                            home = jnp.where(hi == 0, SECOND[mine][n], SECOND[yours][n])
                            keep2[home, :, columns] = unit
                    for side in range(2):
                        unit = near[g][2 * pair + c, count * (1 + side) + n]
                        if g == 0:
                            rows1[2 * side + c, :, columns] = unit
                        else:
                            away2[side, 2 * c + n, :, columns] = unit

    class Group:
        pass

    groups = []
    for g, (acc, x_out, x_in, y1_out, y1_in, y2_out, y2_in) in enumerate(
        (
            (acc1, x_out1, x_in1, y1_out1, y1_in1, y2_out1, y2_in1),
            (acc2, x_out2, x_in2, y1_out2, y1_in2, y2_out2, y2_in2),
        )
    ):
        t = Group()
        t.acc, t.x_out, t.x_in, t.y1_out, t.y1_in, t.y2_out, t.y2_in = (
            acc, x_out, x_in, y1_out, y1_in, y2_out, y2_in,
        )
        t.g, t.count, t.rows, t.lags = g, GROUPS[g], GROUPS[g] * UNIT, LAGS[g]
        groups.append(t)

    def x_copies(t, c):
        sems = t.g * CHUNKS + c
        return [
            remote(
                t.x_out.at[c, flip(hi, a)], t.x_in.at[c, hi], xs_sem.at[sems, a],
                xr_sem.at[sems, a], rank_at(0, a, 0), across,
            )
            for a in range(2)
        ]

    def y_copies(t, c, out, into, send, recv):
        sems = t.g * CHUNKS + c
        return [
            remote(out.at[c, a], into.at[c, a], send.at[sems, a], recv.at[sems, a], dp, to)
            for a, to in enumerate((up, down))
        ]

    def y1_copies(t, c):
        return y_copies(t, c, t.y1_out, t.y1_in, y1s_sem, y1r_sem)

    def y2_copies(t, c):
        return y_copies(t, c, t.y2_out, t.y2_in, y2s_sem, y2r_sem)

    def sums(t, c, at, over_x):
        own = t.acc[lax.rem(c, t.lags[2] + 1), pl.ds(t.count * at, t.count)].astype(F32)
        if over_x:
            units = []
            for n in range(t.count):
                places = HOLDS[t.g]
                side = choose(at, [places[i][n][0] for i in range(4)])
                place = choose(at, [places[i][n][1] for i in range(4)])
                units.append(t.x_in[c, side, place].astype(F32))
            own = own + jnp.stack(units)
        return own.reshape(t.rows, CHUNK)

    def either_way(t, c, body):
        if t.g == 0:
            body(True)
        else:
            over_x = goes_over_x(t, c, hi)
            pl.when(over_x)(lambda: body(True))
            pl.when(jnp.logical_not(over_x))(lambda: body(False))

    def multiply(t, i):
        c = i - t.g * CHUNKS
        slot = lax.rem(i, W_SLOTS)
        load(i).wait()

        @pl.when(i + W_SLOTS - 1 < STEPS)
        def _():
            load(i + W_SLOTS - 1).start()

        w = w_buf[slot]
        at = lax.rem(c, t.lags[2] + 1)
        if t.g == 0:
            both = jnp.dot(
                rows1[...].reshape(8 * UNIT, TP * VH), w, preferred_element_type=F32
            )
            t.x_out[c] = both[: 4 * UNIT].astype(BF16).reshape(2, 2, UNIT, CHUNK)
            for copy in x_copies(t, c):
                copy.start()
            t.acc[at] = both[4 * UNIT :].astype(BF16).reshape(4, UNIT, CHUNK)
        else:
            t.x_out[c] = (
                jnp.dot(away2[...].reshape(8 * UNIT, TP * VH), w, preferred_element_type=F32)
                .astype(BF16)
                .reshape(2, 4, UNIT, CHUNK)
            )
            start_x(t, c)
            start_y_first(t, c)
            t.acc[at] = (
                jnp.dot(keep2[...].reshape(8 * UNIT, TP * VH), w, preferred_element_type=F32)
                .astype(BF16)
                .reshape(8, UNIT, CHUNK)
            )

    def y_first(c):
        return (lax.rem(c, 2) == 0) & (c < 2 * Y_FIRST)

    def y_side(c):
        return lax.rem(c // 2, 2)

    def goes_over_x(t, c, to):
        return jnp.logical_not(y_first(c)) | (y_side(c) != to)

    def start_x(t, c):
        for a, copy in enumerate(x_copies(t, c)):
            pl.when(goes_over_x(t, c, flip(hi, a)))(copy.start)

    def away_unit(c, to):
        at = choose(3 - to, [jnp.where(hi == 0, AWAY[0][i], AWAY[1][i]) for i in range(4)])
        return x_out2[c, y_side(c), at]

    def a1_copies(c):
        c = c // 2
        return [
            remote(a1_out.at[c, a], a1_in.at[c, a], a1s_sem.at[c, a], a1r_sem.at[c, a], dp, to)
            for a, to in enumerate((up, down))
        ]

    def a2_copies(c):
        c = c // 2
        return [
            remote(a2_out.at[c, a], a2_in.at[c, a], a2s_sem.at[c, a], a2r_sem.at[c, a], dp, to)
            for a, to in enumerate((up, down))
        ]

    def x2_copy(c):
        rank = y_side(c) * 8 + 2 * z + core
        c = c // 2
        return remote(x2_out.at[c], x2_in.at[c, hi], x2s_sem.at[c], x2r_sem.at[c, hi], rank, across)

    def start_y_first(t, c):
        @pl.when(y_first(c))
        def _():
            other = away_unit(c, far_y)
            a1_out[c // 2, 0] = other[:, :HALF]
            a1_out[c // 2, 1] = other[:, HALF:]
            for copy in a1_copies(c):
                copy.start()

    def after_a1(t, c):
        for copy in a1_copies(c):
            copy.wait_recv()
        to_up = away_unit(c, up_y)
        a2_out[c // 2, 0, :, :HALF] = (
            to_up[:, :HALF].astype(F32) + a1_in[c // 2, 0].astype(F32)
        ).astype(BF16)
        a2_out[c // 2, 0, :, HALF:] = to_up[:, HALF:]
        to_down = away_unit(c, down_y)
        a2_out[c // 2, 1, :, :HALF] = to_down[:, :HALF]
        a2_out[c // 2, 1, :, HALF:] = (
            to_down[:, HALF:].astype(F32) + a1_in[c // 2, 1].astype(F32)
        ).astype(BF16)
        for copy in a2_copies(c):
            copy.start()

    def after_a2(t, c):
        for copy in a2_copies(c):
            copy.wait_recv()
        x2_out[c // 2] = (
            away_unit(c, own_y).astype(F32) + a2_in[c // 2, 0].astype(F32) + a2_in[c // 2, 1].astype(F32)
        ).astype(BF16)
        x2_copy(c).start()

    def after_x(t, c):
        def body(over_x):
            if over_x:
                for copy in x_copies(t, c):
                    copy.wait_recv()
            other = sums(t, c, far_y, over_x).astype(BF16)
            t.y1_out[c, 0] = other[:, :HALF]
            t.y1_out[c, 1] = other[:, HALF:]

        either_way(t, c, body)
        for copy in y1_copies(t, c):
            copy.start()

    def after_y1(t, c):
        for copy in y1_copies(t, c):
            copy.wait_recv()

        def body(over_x):
            to_up = sums(t, c, up_y, over_x)
            t.y2_out[c, 0, :, :HALF] = (to_up[:, :HALF] + t.y1_in[c, 0].astype(F32)).astype(BF16)
            t.y2_out[c, 0, :, HALF:] = to_up[:, HALF:].astype(BF16)
            to_down = sums(t, c, down_y, over_x)
            t.y2_out[c, 1, :, :HALF] = to_down[:, :HALF].astype(BF16)
            t.y2_out[c, 1, :, HALF:] = (
                to_down[:, HALF:] + t.y1_in[c, 1].astype(F32)
            ).astype(BF16)

        either_way(t, c, body)
        for copy in y2_copies(t, c):
            copy.start()

    edge = (own_y == 0) | (own_y == 3)

    def after_y2(t, c):
        for copy in y2_copies(t, c):
            copy.wait_recv()
        start = pl.multiple_of(c * CHUNK, CHUNK)
        if t.g == 0:
            thirds = [jnp.where(edge, 2, 1)]
        else:
            thirds = [0, jnp.where(edge, 1, 2)]

        def body(over_x):
            if not over_x:
                for side in range(2):
                    remote(
                        x2_out.at[c // 2], x2_in.at[c // 2, side], x2s_sem.at[c // 2],
                        x2r_sem.at[c // 2, side], dp, across,
                    ).wait_recv()
            total = sums(t, c, own_y, over_x)
            total = total + t.y2_in[c, 0].astype(F32) + t.y2_in[c, 1].astype(F32)
            for n, third in enumerate(thirds):
                unit = total[n * UNIT : (n + 1) * UNIT]
                if not over_x:
                    side = jnp.where(own_y == 0, 1 - n, n)
                    unit = unit + x2_in[c // 2, side].astype(F32)
                out_ref[jnp.where(lo == 1, 2 - third, third), :, pl.ds(start, CHUNK)] = (
                    unit.astype(BF16)
                )

        either_way(t, c, body)

    def later(t, i, least, most):
        for lag, stage in zip(t.lags, (after_x, after_y1, after_y2)):
            low = t.g * CHUNKS + lag
            if most > low and least < low + CHUNKS:

                @pl.when((i >= low) & (i < low + CHUNKS))
                def _(stage=stage, low=low):
                    stage(t, i - low)

        if t.g == 1:
            for lag, stage in zip(t.lags[:2], (after_a1, after_a2)):
                low = CHUNKS + lag

                @pl.when((i >= low) & y_first(i - low))
                def _(stage=stage, low=low):
                    stage(t, i - low)

    def first_step(i, carry):
        multiply(groups[0], i)
        later(groups[0], i, 0, CHUNKS)
        return carry

    def second_step(i, carry):
        multiply(groups[1], i)
        later(groups[0], i, CHUNKS, STEPS)
        later(groups[1], i, CHUNKS, STEPS)
        return carry

    def last_step(i, carry):
        later(groups[1], i, STEPS, STEPS + LAGS[1][2])
        return carry

    deliver_all(0)
    arrived(0)
    lax.fori_loop(0, DELIVER_AT, first_step, 0)
    spread_done(1)
    deliver_all(1)
    lax.fori_loop(DELIVER_AT, CHUNKS, first_step, 0)
    arrived(1)
    lax.fori_loop(CHUNKS, STEPS, second_step, 0)
    lax.fori_loop(STEPS, STEPS + LAGS[1][2], last_step, 0)

    for copy in gathers:
        copy.wait_send()
    for way in others:
        spread(0, *way).wait_send()
        spread(1, *way).wait_send()
        deliver(0, *way).wait_send()
        deliver(1, *way).wait_send()

    def drain(c, carry):
        for t in groups:
            for copy in y1_copies(t, c) + y2_copies(t, c):
                copy.wait_send()
        for copy in x_copies(groups[0], c):
            copy.wait_send()
        for a, copy in enumerate(x_copies(groups[1], c)):
            pl.when(goes_over_x(groups[1], c, flip(hi, a)))(copy.wait_send)

        @pl.when(y_first(c))
        def _():
            for copy in a1_copies(c) + a2_copies(c) + [x2_copy(c)]:
                copy.wait_send()

        return carry

    lax.fori_loop(0, CHUNKS, drain, 0)


def sum_scratch(g):
    rows = GROUPS[g] * UNIT
    return [
        pltpu.VMEM((LAGS[g][2] + 1, 4 * GROUPS[g], UNIT, CHUNK), BF16),
        pltpu.VMEM((CHUNKS, 2, 2 * GROUPS[g], UNIT, CHUNK), BF16),
        pltpu.VMEM((CHUNKS, 2, 2 * GROUPS[g], UNIT, CHUNK), BF16),
        pltpu.VMEM((CHUNKS, 2, rows, HALF), BF16),
        pltpu.VMEM((CHUNKS, 2, rows, HALF), BF16),
        pltpu.VMEM((CHUNKS, 2, rows, CHUNK), BF16),
        pltpu.VMEM((CHUNKS, 2, rows, CHUNK), BF16),
    ]


def on_device(queries, latent, segments, offsets, w_uk, w_uv, w_out):
    any_spec = pl.BlockSpec(memory_space=pl.ANY)
    smem_spec = pl.BlockSpec(memory_space=pltpu.SMEM)
    dma = pltpu.SemaphoreType.DMA
    out = pl.pallas_call(
        whole_kernel,
        out_shape=jax.ShapeDtypeStruct((3, UNIT, D), BF16),
        in_specs=[smem_spec] * 2 + [any_spec] * 5,
        out_specs=pl.BlockSpec(memory_space=pltpu.VMEM),
        scratch_shapes=[
            pltpu.VMEM((TP, OWN, KV), BF16),
            pltpu.VMEM((ROWS, HEADS * (NOPE + ROPE)), BF16),
            pltpu.VMEM((HEADS, NOPE, LAT), BF16),
            pltpu.VMEM((HEADS, LAT, VH), BF16),
            pltpu.VMEM((ROWS, 2 * ROPE), BF16),
            pltpu.VMEM((ROWS, 2 * ROPE), BF16),
            pltpu.VMEM((NB, BLK, WINDOW * BLK), F32),
            pltpu.VMEM((2, ROWS, 2 * NOPE), BF16),
            pltpu.VMEM((2, ROWS, 2 * VH), BF16),
            pltpu.VMEM((PAIRS, PARTS, 2, 1, UNIT, PART), BF16),
            pltpu.VMEM((PAIRS, PARTS, 2, 2, UNIT, PART), BF16),
            pltpu.VMEM((DP, 2, 1, UNIT, PART), BF16),
            pltpu.VMEM((DP, 2, 2, UNIT, PART), BF16),
            pltpu.VMEM((8, 3, UNIT, PART), BF16),
            pltpu.VMEM((8, 6, UNIT, PART), BF16),
            pltpu.VMEM((8, 1, UNIT, PART), BF16),
            pltpu.VMEM((8, 2, UNIT, PART), BF16),
            pltpu.VMEM((8, 3, UNIT, PART), BF16),
            pltpu.VMEM((8, 6, UNIT, PART), BF16),
            pltpu.VMEM((8, 1, UNIT, PART), BF16),
            pltpu.VMEM((8, 2, UNIT, PART), BF16),
            pltpu.VMEM((8, UNIT, TP * VH), BF16),
            pltpu.VMEM((8, UNIT, TP * VH), BF16),
            pltpu.VMEM((2, 4, UNIT, TP * VH), BF16),
            pltpu.VMEM((W_SLOTS, TP * VH, CHUNK), BF16),
        ]
        + sum_scratch(0)
        + sum_scratch(1)
        + [
            pltpu.VMEM((Y_FIRST, 2, UNIT, HALF), BF16),
            pltpu.VMEM((Y_FIRST, 2, UNIT, HALF), BF16),
            pltpu.VMEM((Y_FIRST, 2, UNIT, CHUNK), BF16),
            pltpu.VMEM((Y_FIRST, 2, UNIT, CHUNK), BF16),
            pltpu.VMEM((Y_FIRST, UNIT, CHUNK), BF16),
            pltpu.VMEM((Y_FIRST, 2, UNIT, CHUNK), BF16),
            dma((4,)),
            dma((TP - 1,)),
            dma((TP - 1,)),
            dma((2 * DP,)),
            dma((2 * DP,)),
            dma((2 * DP,)),
            dma((2 * DP,)),
            dma((W_SLOTS,)),
        ]
        + [dma((STEPS, 2))] * 6
        + [dma((Y_FIRST, 2))] * 4
        + [dma((Y_FIRST,)), dma((Y_FIRST, 2))],
        compiler_params=pltpu.CompilerParams(
            collective_id=0, has_side_effects=True, vmem_limit_bytes=58 * 2**20
        ),
        name="whole",
    )(segments.T, offsets, latent, queries, w_uk, w_uv, w_out)
    return out.reshape(OWN, D)


def solution(mesh):
    return jax.shard_map(
        on_device,
        mesh=mesh,
        in_specs=(
            P("dp", "tp"),
            P(("dp", "tp"), None),
            P(),
            P(),
            P("tp", None, None),
            P("tp", None, None),
            P("tp", None),
        ),
        out_specs=P(("dp", "tp"), None),
        check_vma=False,
    )
```

```python
import functools

import jax
import jax.numpy as jnp
from jax import lax
from jax.experimental import pallas as pl
from jax.experimental.pallas import tpu as pltpu
from jax.sharding import PartitionSpec as P

NOPE = 128
ROPE = 64
LAT = 512
VH = 128
BLK = 128
NB = 6
DP = 16
TP = 8
HEADS = 8
ROWS = NB * BLK
KV = LAT + ROPE
D = 7168
OWN = ROWS // TP
PARTS = 4
PAIRS = HEADS // 2
WINDOW = 4
UNIT = 32
PART = 256
SCALE = (NOPE + ROPE) ** (-0.5)
LOG2E = 1.4426950408889634

CHUNK = 512
CHUNKS = D // CHUNK
HALF = CHUNK // 2
STEPS = 2 * CHUNKS
W_SLOTS = 3
GROUPS = (1, 2)
LAGS = ((4, 7, 10), (3, 5, 8))
Y_FIRST = 5
AHEAD = 5
DELIVER_AT = 5

MESH = pl.DeviceIdType.MESH
BF16 = jnp.bfloat16
F32 = jnp.float32


def ranks():
    return lax.axis_index("dp"), lax.axis_index("tp")


def remote(src, dst, send, recv, dp, tp):
    return pltpu.make_async_remote_copy(
        src_ref=src,
        dst_ref=dst,
        send_sem=send,
        recv_sem=recv,
        device_id={"dp": dp, "tp": tp},
        device_id_type=MESH,
    )


def greet(peers):
    barrier = pltpu.get_barrier_semaphore()
    for dp, tp in peers:
        pl.semaphore_signal(
            barrier, inc=1, device_id={"dp": dp, "tp": tp}, device_id_type=MESH
        )
    pl.semaphore_wait(barrier, len(peers))


def nt_dot(a, b):
    return lax.dot_general(a, b, (((1,), (1,)), ((), ())), preferred_element_type=F32)


HOME = ((11, 3, 6), (4, 0, 5), (7, 1, 9), (2, 10, 8))
FIRST = (3, 1, 2, 0)
SECOND = ((2, 4), (0, 3), (1, 6), (7, 5))
AWAY = ((2, 0, 1, 3), (0, 1, 3, 2))


def unit_of(p, e, u):
    y, third = divmod(HOME[p][u], 3)
    unit = 6 * y + third
    return 23 - unit if e else unit


PLACE = {
    unit_of(p, e, u): (p, e, u) for p in range(PARTS) for e in range(2) for u in range(3)
}


HOLDS = (
    tuple(((FIRST.index(y) % 2, FIRST.index(y) // 2),) for y in range(4)),
    tuple(
        tuple(
            (p % 2, 2 * (p // 2) + n)
            for home in (2 * y, 2 * y + 1)
            for p in range(PARTS)
            for n in range(2)
            if SECOND[p][n] == home
        )
        for y in range(4)
    ),
)


def choose(p, options):
    value = options[0]
    for i in range(1, PARTS):
        value = jnp.where(p == i, options[i], value)
    return value


def block_of(p, e, u):
    first = choose(p, [unit_of(i, 0, u) // 4 for i in range(PARTS)])
    return jnp.where(e == 1, NB - 1 - first, first)


def write_bias(seg_ref, bias, dp):
    row = lax.broadcasted_iota(jnp.int32, (BLK, BLK), 0)
    col = lax.broadcasted_iota(jnp.int32, (BLK, BLK), 1)
    for qb in range(NB):
        first = max(0, qb - WINDOW + 1)
        for kb in range(first, qb + 1):
            if kb == qb:
                block = jnp.where(col <= row, 0.0, -jnp.inf).astype(F32)
            else:
                same = seg_ref[kb, dp] == seg_ref[qb, dp]
                block = jnp.full((BLK, BLK), jnp.where(same, 0.0, -jnp.inf), F32)
            bias[qb, :, (kb - first) * BLK : (kb - first + 1) * BLK] = block


def attend_pair(pair, slab, rope_even, rope_odd, bias, q_ref, wuk_ref, wuv_ref, keys, values, parts1, parts2):
    content = slab[:, :, :LAT].reshape(ROWS, LAT)
    up = wuk_ref[pl.ds(2 * pair, 2)].reshape(2 * NOPE, LAT)
    both = nt_dot(content, up)
    lane = lax.broadcasted_iota(jnp.int32, (ROWS, NOPE), 1)
    keys[0, :, :NOPE] = both[:, :NOPE].astype(BF16)
    keys[0, :, NOPE:] = rope_even[...]
    turned = pltpu.roll(both[:, NOPE:], 64, 1)
    keys[1, :, :NOPE] = jnp.where(lane < 64, 0.0, turned).astype(BF16)
    keys[1, :, NOPE:] = jnp.where(lane < 64, turned, rope_odd[...].astype(F32)).astype(BF16)
    for e in range(2):
        values[e, :, :VH] = jnp.dot(
            content, wuv_ref[2 * pair + e], preferred_element_type=F32
        ).astype(BF16)

    def window(qb):
        first = max(0, qb - WINDOW + 1)
        return pl.ds(first * BLK, (qb - first + 1) * BLK), (qb - first + 1) * BLK

    def score(qb, e):
        keep, width = window(qb)
        start = pl.multiple_of(pair * 384 + 128 * e, 128)
        q = q_ref[pl.ds(qb * BLK, BLK), pl.ds(start, 256)]
        return nt_dot(q, keys[e, keep, :]) + bias[qb, :, :width]

    def finish(qb, e, s):
        keep, _ = window(qb)
        top = jnp.max(s, axis=1, keepdims=True)
        p = jnp.exp2((s - top) * (SCALE * LOG2E)).astype(BF16)
        o = jnp.dot(p, values[e, keep, :], preferred_element_type=F32)
        o = (o[:, :VH] / o[:, VH:]).astype(BF16)
        for quarter in range(4):
            part, side, u = PLACE[4 * qb + quarter]
            target, n = (parts2, u - 1) if u else (parts1, 0)
            target[pair, part, side, n, :, e * VH : (e + 1) * VH] = o[
                quarter * UNIT : (quarter + 1) * UNIT
            ]

    units = [(qb, e) for qb in range(NB) for e in range(2)]
    waiting = []
    for unit in units:
        waiting.append((*unit, score(*unit)))
        if len(waiting) > AHEAD:
            finish(*waiting.pop(0))
    for held in waiting:
        finish(*held)


def whole_kernel(
    seg_ref, off_ref, lat_hbm, q_hbm, wuk_hbm, wuv_hbm, w_hbm, out_ref,
    slab, q_ref, wuk_ref, wuv_ref, rope_even, rope_odd, bias, keys, values,
    parts1, parts2, gathered1, gathered2, staged_near1, staged_near2, staged_far1, staged_far2, near1, near2, far1, far2,
    rows1, keep2, away2, w_buf,
    acc1, x_out1, x_in1, y1_out1, y1_in1, y2_out1, y2_in1,
    acc2, x_out2, x_in2, y1_out2, y1_in2, y2_out2, y2_in2,
    a1_out, a1_in, a2_out, a2_in, x2_out, x2_in,
    own_sem, ag_s, ag_r, p1_s, p1_r, p2_s, p2_r,
    w_sem, xs_sem, xr_sem, y1s_sem, y1r_sem, y2s_sem, y2r_sem,
    a1s_sem, a1r_sem, a2s_sem, a2r_sem, x2s_sem, x2r_sem,
):
    dp, tp = ranks()
    y, lo = tp // 2, lax.rem(tp, 2)
    hi, z, core = dp // 8, lax.rem(dp // 2, 4), lax.rem(dp, 2)
    across = 2 * y + 1 - lo
    own_y = jnp.where(lo == 1, 3 - y, y)
    step_y = jnp.where(lo == 1, 3, 1)
    up = 2 * lax.rem(y + step_y, 4) + lo
    down = 2 * lax.rem(y + 4 - step_y, 4) + lo
    up_y, down_y, far_y = lax.rem(own_y + 1, 4), lax.rem(own_y + 3, 4), lax.rem(own_y + 2, 4)

    def flip(bit, by):
        return bit + by - 2 * bit * by

    def rank_at(o, a, b):
        return flip(hi, a) * 8 + lax.rem(z + o, 4) * 2 + flip(core, b)

    def load(c):
        start = pl.multiple_of(lax.rem(c, CHUNKS) * CHUNK, CHUNK)
        slot = lax.rem(c, W_SLOTS)
        return pltpu.make_async_copy(
            w_hbm.at[:, pl.ds(start, CHUNK)], w_buf.at[slot], w_sem.at[slot]
        )

    loads = [
        pltpu.make_async_copy(lat_hbm, slab.at[tp], own_sem.at[0]),
        pltpu.make_async_copy(wuk_hbm, wuk_ref, own_sem.at[1]),
        pltpu.make_async_copy(wuv_hbm, wuv_ref, own_sem.at[2]),
        pltpu.make_async_copy(q_hbm, q_ref, own_sem.at[3]),
    ]
    for copy in loads:
        copy.start()
    for c in range(W_SLOTS - 1):
        load(c).start()

    greet(
        [(dp, lax.rem(tp + o, TP)) for o in range(1, TP)]
        + [(lax.rem(dp + o, DP), tp) for o in range(1, DP)]
        + [(lax.rem(dp + DP // 2, DP), across)]
    )

    opposite = 2 * lax.rem(y + 2, 4) + lo
    after, before = 2 * lax.rem(y + 1, 4) + lo, 2 * lax.rem(y + 3, 4) + lo

    def hand(index, src, at, to):
        return remote(src, slab.at[at], ag_s.at[index], ag_r.at[index], dp, to)

    gathers = [
        hand(0, lat_hbm, tp, opposite),
        hand(1, lat_hbm, tp, across),
        hand(2, lat_hbm, tp, after),
        hand(3, lat_hbm, tp, before),
        hand(4, slab.at[across], across, after),
        hand(5, slab.at[across], across, before),
        hand(6, slab.at[opposite], opposite, across),
    ]
    for copy in gathers[:4]:
        copy.start()
    gathers[1].wait_recv()
    gathers[4].start()
    gathers[5].start()
    gathers[0].wait_recv()
    gathers[6].start()
    write_bias(seg_ref, bias, dp)
    for copy in loads:
        copy.wait()
    for copy in gathers[2:]:
        copy.wait_recv()
    rope = slab[:, :, LAT:].reshape(ROWS, ROPE)
    blank = jnp.zeros((ROWS, ROPE), BF16)
    rope_even[...] = jnp.concatenate([rope, blank], axis=1)
    rope_odd[...] = jnp.concatenate([blank, rope], axis=1)
    values[:, :, VH:] = jnp.ones((2, ROWS, VH), BF16)

    parts, gathered = (parts1, parts2), (gathered1, gathered2)

    def spread(g, o, a, b):
        pair = lax.rem(z + o, 4)
        part = 2 * flip(core, b) + flip(hi, a)
        at = g * DP + o * 4 + a * 2 + b
        return remote(
            parts[g].at[pair, part], gathered[g].at[dp], p1_s.at[at], p1_r.at[at],
            rank_at(o, a, b), tp,
        )

    def own_part(g):
        return pltpu.make_async_copy(
            parts[g].at[z, 2 * core + hi], gathered[g].at[dp], p1_s.at[g * DP]
        )

    def attend_step(i, carry):
        o = jnp.where(i == 0, 2, jnp.where(i == 1, 1, jnp.where(i == 2, 3, 0)))
        attend_pair(
            lax.rem(z + o, 4), slab, rope_even, rope_odd, bias, q_ref, wuk_ref, wuv_ref,
            keys, values, parts1, parts2,
        )
        for a, b in ((1, 0), (1, 1), (0, 1)):
            spread(0, o, a, b).start()

        @pl.when(o != 0)
        def _():
            spread(0, o, 0, 0).start()

        return carry

    ways = [(o, a, b) for o in (2, 1, 3, 0) for a in (1, 0) for b in (1, 0)]
    others = [way for way in ways if way != (0, 0, 0)]

    def spread_second(a):
        for way in others:
            if way[1] == a:
                spread(1, *way).start()

    def spread_done(g):
        for way in others:
            spread(g, *way).wait_recv()
        own_part(g).wait()

    lax.fori_loop(0, PAIRS, attend_step, 0)
    own_part(0).start()
    own_part(1).start()
    spread_done(0)

    part = 2 * core + hi
    staged_near, staged_far = (staged_near1, staged_near2), (staged_far1, staged_far2)
    near, far = (near1, near2), (far1, far2)

    def taken(rank, e, u):
        source = lax.rem(rank + DP - off_ref[block_of(part, e, u)], DP)
        return gathered2[source, e, u - 1] if u else gathered1[source, e, 0]

    def deliver(g, o, a, b):
        at = g * DP + o * 4 + a * 2 + b
        src = (staged_far if a else staged_near)[g].at[2 * o + b]
        dst = (far if a else near)[g].at[2 * z + core]
        return remote(src, dst, p2_s.at[at], p2_r.at[at], rank_at(o, a, b), tp)

    def deliver_all(g):
        units = ((0,), (1, 2))[g]
        count = len(units)
        for o, a, b in ways:
            rank = rank_at(o, a, b)
            own = (o, a, b) == (0, 0, 0)
            if a:
                target, index = staged_far[g], 2 * o + b
            elif own:
                target, index = near[g], 2 * z + core
            else:
                target, index = staged_near[g], 2 * o + b
            for n, u in enumerate(units):
                target[index, n] = taken(rank, lo, u)
            if not a:
                for side in range(2):
                    for n, u in enumerate(units):
                        target[index, count * (1 + side) + n] = taken(
                            rank + (side - hi) * 8, 1 - lo, u
                        )
            if not own:
                deliver(g, o, a, b).start()

    def arrived(g):
        for way in others:
            deliver(g, *way).wait_recv()
        if g == 0:
            spread_second(0)
        count = g + 1
        for pair in range(PAIRS):
            columns = pl.ds(pair * PART, PART)
            for c in range(2):
                for n in range(count):
                    for a in range(2):
                        mine, yours = 2 * c + a, 2 * c + 1 - a
                        unit = (far if a else near)[g][2 * pair + c, n]
                        if g == 0:
                            home = jnp.where(hi == 0, FIRST[mine], FIRST[yours])
                            rows1[4 + home, :, columns] = unit
                        else:
                            home = jnp.where(hi == 0, SECOND[mine][n], SECOND[yours][n])
                            keep2[home, :, columns] = unit
                    for side in range(2):
                        unit = near[g][2 * pair + c, count * (1 + side) + n]
                        if g == 0:
                            rows1[2 * side + c, :, columns] = unit
                        else:
                            away2[side, 2 * c + n, :, columns] = unit

    class Group:
        pass

    groups = []
    for g, (acc, x_out, x_in, y1_out, y1_in, y2_out, y2_in) in enumerate(
        (
            (acc1, x_out1, x_in1, y1_out1, y1_in1, y2_out1, y2_in1),
            (acc2, x_out2, x_in2, y1_out2, y1_in2, y2_out2, y2_in2),
        )
    ):
        t = Group()
        t.acc, t.x_out, t.x_in, t.y1_out, t.y1_in, t.y2_out, t.y2_in = (
            acc, x_out, x_in, y1_out, y1_in, y2_out, y2_in,
        )
        t.g, t.count, t.rows, t.lags = g, GROUPS[g], GROUPS[g] * UNIT, LAGS[g]
        groups.append(t)

    def x_copies(t, c):
        sems = t.g * CHUNKS + c
        return [
            remote(
                t.x_out.at[c, flip(hi, a)], t.x_in.at[c, hi], xs_sem.at[sems, a],
                xr_sem.at[sems, a], rank_at(0, a, 0), across,
            )
            for a in range(2)
        ]

    def y_copies(t, c, out, into, send, recv):
        sems = t.g * CHUNKS + c
        return [
            remote(out.at[c, a], into.at[c, a], send.at[sems, a], recv.at[sems, a], dp, to)
            for a, to in enumerate((up, down))
        ]

    def y1_copies(t, c):
        return y_copies(t, c, t.y1_out, t.y1_in, y1s_sem, y1r_sem)

    def y2_copies(t, c):
        return y_copies(t, c, t.y2_out, t.y2_in, y2s_sem, y2r_sem)

    def sums(t, c, at, over_x):
        own = t.acc[lax.rem(c, t.lags[2] + 1), pl.ds(t.count * at, t.count)].astype(F32)
        if over_x:
            units = []
            for n in range(t.count):
                places = HOLDS[t.g]
                side = choose(at, [places[i][n][0] for i in range(4)])
                place = choose(at, [places[i][n][1] for i in range(4)])
                units.append(t.x_in[c, side, place].astype(F32))
            own = own + jnp.stack(units)
        return own.reshape(t.rows, CHUNK)

    def either_way(t, c, body):
        if t.g == 0:
            body(True)
        else:
            over_x = goes_over_x(t, c, hi)
            pl.when(over_x)(lambda: body(True))
            pl.when(jnp.logical_not(over_x))(lambda: body(False))

    def multiply(t, i):
        c = i - t.g * CHUNKS
        slot = lax.rem(i, W_SLOTS)
        load(i).wait()

        @pl.when(i + W_SLOTS - 1 < STEPS)
        def _():
            load(i + W_SLOTS - 1).start()

        w = w_buf[slot]
        at = lax.rem(c, t.lags[2] + 1)
        if t.g == 0:
            both = jnp.dot(
                rows1[...].reshape(8 * UNIT, TP * VH), w, preferred_element_type=F32
            )
            t.x_out[c] = both[: 4 * UNIT].astype(BF16).reshape(2, 2, UNIT, CHUNK)
            for copy in x_copies(t, c):
                copy.start()
            t.acc[at] = both[4 * UNIT :].astype(BF16).reshape(4, UNIT, CHUNK)
        else:
            t.x_out[c] = (
                jnp.dot(away2[...].reshape(8 * UNIT, TP * VH), w, preferred_element_type=F32)
                .astype(BF16)
                .reshape(2, 4, UNIT, CHUNK)
            )
            start_x(t, c)
            start_y_first(t, c)
            t.acc[at] = (
                jnp.dot(keep2[...].reshape(8 * UNIT, TP * VH), w, preferred_element_type=F32)
                .astype(BF16)
                .reshape(8, UNIT, CHUNK)
            )

    def y_first(c):
        return (lax.rem(c, 2) == 0) & (c < 2 * Y_FIRST)

    def y_side(c):
        return lax.rem(c // 2, 2)

    def goes_over_x(t, c, to):
        return jnp.logical_not(y_first(c)) | (y_side(c) != to)

    def start_x(t, c):
        for a, copy in enumerate(x_copies(t, c)):
            pl.when(goes_over_x(t, c, flip(hi, a)))(copy.start)

    def away_unit(c, to):
        at = choose(3 - to, [jnp.where(hi == 0, AWAY[0][i], AWAY[1][i]) for i in range(4)])
        return x_out2[c, y_side(c), at]

    def a1_copies(c):
        c = c // 2
        return [
            remote(a1_out.at[c, a], a1_in.at[c, a], a1s_sem.at[c, a], a1r_sem.at[c, a], dp, to)
            for a, to in enumerate((up, down))
        ]

    def a2_copies(c):
        c = c // 2
        return [
            remote(a2_out.at[c, a], a2_in.at[c, a], a2s_sem.at[c, a], a2r_sem.at[c, a], dp, to)
            for a, to in enumerate((up, down))
        ]

    def x2_copy(c):
        rank = y_side(c) * 8 + 2 * z + core
        c = c // 2
        return remote(x2_out.at[c], x2_in.at[c, hi], x2s_sem.at[c], x2r_sem.at[c, hi], rank, across)

    def start_y_first(t, c):
        @pl.when(y_first(c))
        def _():
            other = away_unit(c, far_y)
            a1_out[c // 2, 0] = other[:, :HALF]
            a1_out[c // 2, 1] = other[:, HALF:]
            for copy in a1_copies(c):
                copy.start()

    def after_a1(t, c):
        for copy in a1_copies(c):
            copy.wait_recv()
        to_up = away_unit(c, up_y)
        a2_out[c // 2, 0, :, :HALF] = (
            to_up[:, :HALF].astype(F32) + a1_in[c // 2, 0].astype(F32)
        ).astype(BF16)
        a2_out[c // 2, 0, :, HALF:] = to_up[:, HALF:]
        to_down = away_unit(c, down_y)
        a2_out[c // 2, 1, :, :HALF] = to_down[:, :HALF]
        a2_out[c // 2, 1, :, HALF:] = (
            to_down[:, HALF:].astype(F32) + a1_in[c // 2, 1].astype(F32)
        ).astype(BF16)
        for copy in a2_copies(c):
            copy.start()

    def after_a2(t, c):
        for copy in a2_copies(c):
            copy.wait_recv()
        x2_out[c // 2] = (
            away_unit(c, own_y).astype(F32) + a2_in[c // 2, 0].astype(F32) + a2_in[c // 2, 1].astype(F32)
        ).astype(BF16)
        x2_copy(c).start()

    def after_x(t, c):
        def body(over_x):
            if over_x:
                for copy in x_copies(t, c):
                    copy.wait_recv()
            other = sums(t, c, far_y, over_x).astype(BF16)
            t.y1_out[c, 0] = other[:, :HALF]
            t.y1_out[c, 1] = other[:, HALF:]

        either_way(t, c, body)
        for copy in y1_copies(t, c):
            copy.start()

    def after_y1(t, c):
        for copy in y1_copies(t, c):
            copy.wait_recv()

        def body(over_x):
            to_up = sums(t, c, up_y, over_x)
            t.y2_out[c, 0, :, :HALF] = (to_up[:, :HALF] + t.y1_in[c, 0].astype(F32)).astype(BF16)
            t.y2_out[c, 0, :, HALF:] = to_up[:, HALF:].astype(BF16)
            to_down = sums(t, c, down_y, over_x)
            t.y2_out[c, 1, :, :HALF] = to_down[:, :HALF].astype(BF16)
            t.y2_out[c, 1, :, HALF:] = (
                to_down[:, HALF:] + t.y1_in[c, 1].astype(F32)
            ).astype(BF16)

        either_way(t, c, body)
        for copy in y2_copies(t, c):
            copy.start()

    edge = (own_y == 0) | (own_y == 3)

    def after_y2(t, c):
        for copy in y2_copies(t, c):
            copy.wait_recv()
        start = pl.multiple_of(c * CHUNK, CHUNK)
        if t.g == 0:
            thirds = [jnp.where(edge, 2, 1)]
        else:
            thirds = [0, jnp.where(edge, 1, 2)]

        def body(over_x):
            if not over_x:
                for side in range(2):
                    remote(
                        x2_out.at[c // 2], x2_in.at[c // 2, side], x2s_sem.at[c // 2],
                        x2r_sem.at[c // 2, side], dp, across,
                    ).wait_recv()
            total = sums(t, c, own_y, over_x)
            total = total + t.y2_in[c, 0].astype(F32) + t.y2_in[c, 1].astype(F32)
            for n, third in enumerate(thirds):
                unit = total[n * UNIT : (n + 1) * UNIT]
                if not over_x:
                    side = jnp.where(own_y == 0, 1 - n, n)
                    unit = unit + x2_in[c // 2, side].astype(F32)
                out_ref[jnp.where(lo == 1, 2 - third, third), :, pl.ds(start, CHUNK)] = (
                    unit.astype(BF16)
                )

        either_way(t, c, body)

    def later(t, i, least, most):
        for lag, stage in zip(t.lags, (after_x, after_y1, after_y2)):
            low = t.g * CHUNKS + lag
            if most > low and least < low + CHUNKS:

                @pl.when((i >= low) & (i < low + CHUNKS))
                def _(stage=stage, low=low):
                    stage(t, i - low)

        if t.g == 1:
            for lag, stage in zip(t.lags[:2], (after_a1, after_a2)):
                low = CHUNKS + lag

                @pl.when((i >= low) & y_first(i - low))
                def _(stage=stage, low=low):
                    stage(t, i - low)

    def first_step(i, carry):
        multiply(groups[0], i)
        later(groups[0], i, 0, CHUNKS)
        return carry

    def second_step(i, carry):
        multiply(groups[1], i)
        later(groups[0], i, CHUNKS, STEPS)
        later(groups[1], i, CHUNKS, STEPS)
        return carry

    def last_step(i, carry):
        later(groups[1], i, STEPS, STEPS + LAGS[1][2])
        return carry

    deliver_all(0)
    spread_second(1)
    arrived(0)
    lax.fori_loop(0, DELIVER_AT, first_step, 0)
    spread_done(1)
    deliver_all(1)
    lax.fori_loop(DELIVER_AT, CHUNKS, first_step, 0)
    arrived(1)
    lax.fori_loop(CHUNKS, STEPS, second_step, 0)
    lax.fori_loop(STEPS, STEPS + LAGS[1][2], last_step, 0)

    for copy in gathers:
        copy.wait_send()
    for way in others:
        spread(0, *way).wait_send()
        spread(1, *way).wait_send()
        deliver(0, *way).wait_send()
        deliver(1, *way).wait_send()

    def drain(c, carry):
        for t in groups:
            for copy in y1_copies(t, c) + y2_copies(t, c):
                copy.wait_send()
        for copy in x_copies(groups[0], c):
            copy.wait_send()
        for a, copy in enumerate(x_copies(groups[1], c)):
            pl.when(goes_over_x(groups[1], c, flip(hi, a)))(copy.wait_send)

        @pl.when(y_first(c))
        def _():
            for copy in a1_copies(c) + a2_copies(c) + [x2_copy(c)]:
                copy.wait_send()

        return carry

    lax.fori_loop(0, CHUNKS, drain, 0)


def sum_scratch(g):
    rows = GROUPS[g] * UNIT
    return [
        pltpu.VMEM((LAGS[g][2] + 1, 4 * GROUPS[g], UNIT, CHUNK), BF16),
        pltpu.VMEM((CHUNKS, 2, 2 * GROUPS[g], UNIT, CHUNK), BF16),
        pltpu.VMEM((CHUNKS, 2, 2 * GROUPS[g], UNIT, CHUNK), BF16),
        pltpu.VMEM((CHUNKS, 2, rows, HALF), BF16),
        pltpu.VMEM((CHUNKS, 2, rows, HALF), BF16),
        pltpu.VMEM((CHUNKS, 2, rows, CHUNK), BF16),
        pltpu.VMEM((CHUNKS, 2, rows, CHUNK), BF16),
    ]


def on_device(queries, latent, segments, offsets, w_uk, w_uv, w_out):
    any_spec = pl.BlockSpec(memory_space=pl.ANY)
    smem_spec = pl.BlockSpec(memory_space=pltpu.SMEM)
    dma = pltpu.SemaphoreType.DMA
    out = pl.pallas_call(
        whole_kernel,
        out_shape=jax.ShapeDtypeStruct((3, UNIT, D), BF16),
        in_specs=[smem_spec] * 2 + [any_spec] * 5,
        out_specs=pl.BlockSpec(memory_space=pltpu.VMEM),
        scratch_shapes=[
            pltpu.VMEM((TP, OWN, KV), BF16),
            pltpu.VMEM((ROWS, HEADS * (NOPE + ROPE)), BF16),
            pltpu.VMEM((HEADS, NOPE, LAT), BF16),
            pltpu.VMEM((HEADS, LAT, VH), BF16),
            pltpu.VMEM((ROWS, 2 * ROPE), BF16),
            pltpu.VMEM((ROWS, 2 * ROPE), BF16),
            pltpu.VMEM((NB, BLK, WINDOW * BLK), F32),
            pltpu.VMEM((2, ROWS, 2 * NOPE), BF16),
            pltpu.VMEM((2, ROWS, 2 * VH), BF16),
            pltpu.VMEM((PAIRS, PARTS, 2, 1, UNIT, PART), BF16),
            pltpu.VMEM((PAIRS, PARTS, 2, 2, UNIT, PART), BF16),
            pltpu.VMEM((DP, 2, 1, UNIT, PART), BF16),
            pltpu.VMEM((DP, 2, 2, UNIT, PART), BF16),
            pltpu.VMEM((8, 3, UNIT, PART), BF16),
            pltpu.VMEM((8, 6, UNIT, PART), BF16),
            pltpu.VMEM((8, 1, UNIT, PART), BF16),
            pltpu.VMEM((8, 2, UNIT, PART), BF16),
            pltpu.VMEM((8, 3, UNIT, PART), BF16),
            pltpu.VMEM((8, 6, UNIT, PART), BF16),
            pltpu.VMEM((8, 1, UNIT, PART), BF16),
            pltpu.VMEM((8, 2, UNIT, PART), BF16),
            pltpu.VMEM((8, UNIT, TP * VH), BF16),
            pltpu.VMEM((8, UNIT, TP * VH), BF16),
            pltpu.VMEM((2, 4, UNIT, TP * VH), BF16),
            pltpu.VMEM((W_SLOTS, TP * VH, CHUNK), BF16),
        ]
        + sum_scratch(0)
        + sum_scratch(1)
        + [
            pltpu.VMEM((Y_FIRST, 2, UNIT, HALF), BF16),
            pltpu.VMEM((Y_FIRST, 2, UNIT, HALF), BF16),
            pltpu.VMEM((Y_FIRST, 2, UNIT, CHUNK), BF16),
            pltpu.VMEM((Y_FIRST, 2, UNIT, CHUNK), BF16),
            pltpu.VMEM((Y_FIRST, UNIT, CHUNK), BF16),
            pltpu.VMEM((Y_FIRST, 2, UNIT, CHUNK), BF16),
            dma((4,)),
            dma((TP - 1,)),
            dma((TP - 1,)),
            dma((2 * DP,)),
            dma((2 * DP,)),
            dma((2 * DP,)),
            dma((2 * DP,)),
            dma((W_SLOTS,)),
        ]
        + [dma((STEPS, 2))] * 6
        + [dma((Y_FIRST, 2))] * 4
        + [dma((Y_FIRST,)), dma((Y_FIRST, 2))],
        compiler_params=pltpu.CompilerParams(
            collective_id=0, has_side_effects=True, vmem_limit_bytes=58 * 2**20
        ),
        name="whole",
    )(segments.T, offsets, latent, queries, w_uk, w_uv, w_out)
    return out.reshape(OWN, D)


def solution(mesh):
    return jax.shard_map(
        on_device,
        mesh=mesh,
        in_specs=(
            P("dp", "tp"),
            P(("dp", "tp"), None),
            P(),
            P(),
            P("tp", None, None),
            P("tp", None, None),
            P("tp", None),
        ),
        out_specs=P(("dp", "tp"), None),
        check_vma=False,
    )
```

```python
import functools

import jax
import jax.numpy as jnp
from jax import lax
from jax.experimental import pallas as pl
from jax.experimental.pallas import tpu as pltpu
from jax.sharding import PartitionSpec as P

NOPE = 128
ROPE = 64
LAT = 512
VH = 128
BLK = 128
NB = 6
DP = 16
TP = 8
HEADS = 8
ROWS = NB * BLK
KV = LAT + ROPE
D = 7168
OWN = ROWS // TP
PARTS = 4
PAIRS = HEADS // 2
WINDOW = 4
UNIT = 32
PART = 256
SCALE = (NOPE + ROPE) ** (-0.5)
LOG2E = 1.4426950408889634

CHUNK = 512
CHUNKS = D // CHUNK
HALF = CHUNK // 2
STEPS = 2 * CHUNKS
W_SLOTS = 3
GROUPS = (1, 2)
LAGS = ((4, 7, 10), (3, 5, 8))
Y_FIRST = 5
AHEAD = 5
DELIVER_AT = 5

MESH = pl.DeviceIdType.MESH
BF16 = jnp.bfloat16
F32 = jnp.float32


def ranks():
    return lax.axis_index("dp"), lax.axis_index("tp")


def remote(src, dst, send, recv, dp, tp):
    return pltpu.make_async_remote_copy(
        src_ref=src,
        dst_ref=dst,
        send_sem=send,
        recv_sem=recv,
        device_id={"dp": dp, "tp": tp},
        device_id_type=MESH,
    )


def greet(peers):
    barrier = pltpu.get_barrier_semaphore()
    for dp, tp in peers:
        pl.semaphore_signal(
            barrier, inc=1, device_id={"dp": dp, "tp": tp}, device_id_type=MESH
        )
    pl.semaphore_wait(barrier, len(peers))


def nt_dot(a, b):
    return lax.dot_general(a, b, (((1,), (1,)), ((), ())), preferred_element_type=F32)


HOME = ((11, 3, 6), (4, 0, 5), (7, 1, 9), (2, 10, 8))
FIRST = (3, 1, 2, 0)
SECOND = ((2, 4), (0, 3), (1, 6), (7, 5))
AWAY = ((2, 0, 1, 3), (0, 1, 3, 2))


def unit_of(p, e, u):
    y, third = divmod(HOME[p][u], 3)
    unit = 6 * y + third
    return 23 - unit if e else unit


PLACE = {
    unit_of(p, e, u): (p, e, u) for p in range(PARTS) for e in range(2) for u in range(3)
}


HOLDS = (
    tuple(((FIRST.index(y) % 2, FIRST.index(y) // 2),) for y in range(4)),
    tuple(
        tuple(
            (p % 2, 2 * (p // 2) + n)
            for home in (2 * y, 2 * y + 1)
            for p in range(PARTS)
            for n in range(2)
            if SECOND[p][n] == home
        )
        for y in range(4)
    ),
)


def choose(p, options):
    value = options[0]
    for i in range(1, PARTS):
        value = jnp.where(p == i, options[i], value)
    return value


def block_of(p, e, u):
    first = choose(p, [unit_of(i, 0, u) // 4 for i in range(PARTS)])
    return jnp.where(e == 1, NB - 1 - first, first)


def write_bias(seg_ref, bias, dp):
    row = lax.broadcasted_iota(jnp.int32, (BLK, BLK), 0)
    col = lax.broadcasted_iota(jnp.int32, (BLK, BLK), 1)
    for qb in range(NB):
        first = max(0, qb - WINDOW + 1)
        for kb in range(first, qb + 1):
            if kb == qb:
                block = jnp.where(col <= row, 0.0, -jnp.inf).astype(F32)
            else:
                same = seg_ref[kb, dp] == seg_ref[qb, dp]
                block = jnp.full((BLK, BLK), jnp.where(same, 0.0, -jnp.inf), F32)
            bias[qb, :, (kb - first) * BLK : (kb - first + 1) * BLK] = block


def attend_pair(pair, slab, rope_even, rope_odd, bias, q_ref, wuk_ref, wuv_ref, keys, values, parts1, parts2):
    content = slab[:, :, :LAT].reshape(ROWS, LAT)
    up = wuk_ref[pl.ds(2 * pair, 2)].reshape(2 * NOPE, LAT)
    both = nt_dot(content, up)
    lane = lax.broadcasted_iota(jnp.int32, (ROWS, NOPE), 1)
    keys[0, :, :NOPE] = both[:, :NOPE].astype(BF16)
    keys[0, :, NOPE:] = rope_even[...]
    turned = pltpu.roll(both[:, NOPE:], 64, 1)
    keys[1, :, :NOPE] = jnp.where(lane < 64, 0.0, turned).astype(BF16)
    keys[1, :, NOPE:] = jnp.where(lane < 64, turned, rope_odd[...].astype(F32)).astype(BF16)
    for e in range(2):
        values[e, :, :VH] = jnp.dot(
            content, wuv_ref[2 * pair + e], preferred_element_type=F32
        ).astype(BF16)

    def window(qb):
        first = max(0, qb - WINDOW + 1)
        return pl.ds(first * BLK, (qb - first + 1) * BLK), (qb - first + 1) * BLK

    def score(qb, e):
        keep, width = window(qb)
        start = pl.multiple_of(pair * 384 + 128 * e, 128)
        q = q_ref[pl.ds(qb * BLK, BLK), pl.ds(start, 256)]
        return nt_dot(q, keys[e, keep, :]) + bias[qb, :, :width]

    def finish(qb, e, s):
        keep, _ = window(qb)
        top = jnp.max(s, axis=1, keepdims=True)
        p = jnp.exp2((s - top) * (SCALE * LOG2E)).astype(BF16)
        o = jnp.dot(p, values[e, keep, :], preferred_element_type=F32)
        o = (o[:, :VH] / o[:, VH:]).astype(BF16)
        for quarter in range(4):
            part, side, u = PLACE[4 * qb + quarter]
            target, n = (parts2, u - 1) if u else (parts1, 0)
            target[pair, part, side, n, :, e * VH : (e + 1) * VH] = o[
                quarter * UNIT : (quarter + 1) * UNIT
            ]

    units = [(qb, e) for qb in range(NB) for e in range(2)]
    waiting = []
    for unit in units:
        waiting.append((*unit, score(*unit)))
        if len(waiting) > AHEAD:
            finish(*waiting.pop(0))
    for held in waiting:
        finish(*held)


def whole_kernel(
    seg_ref, off_ref, lat_hbm, q_hbm, wuk_hbm, wuv_hbm, w_hbm, out_hbm,
    slab, q_ref, wuk_ref, wuv_ref, rope_even, rope_odd, bias, keys, values,
    parts1, parts2, gathered1, gathered2, staged_near1, staged_near2, staged_far1, staged_far2, near1, near2, far1, far2,
    rows1, keep2, away2, w_buf,
    acc1, x_out1, x_in1, y1_out1, y1_in1, y2_out1, y2_in1,
    acc2, x_out2, x_in2, y1_out2, y1_in2, y2_out2, y2_in2,
    a1_out, a1_in, a2_out, a2_in, x2_out, x2_in, out_ref,
    own_sem, ag_s, ag_r, p1_s, p1_r, p2_s, p2_r,
    w_sem, xs_sem, xr_sem, y1s_sem, y1r_sem, y2s_sem, y2r_sem,
    a1s_sem, a1r_sem, a2s_sem, a2r_sem, x2s_sem, x2r_sem, out_sem,
):
    dp, tp = ranks()
    y, lo = tp // 2, lax.rem(tp, 2)
    hi, z, core = dp // 8, lax.rem(dp // 2, 4), lax.rem(dp, 2)
    across = 2 * y + 1 - lo
    own_y = jnp.where(lo == 1, 3 - y, y)
    step_y = jnp.where(lo == 1, 3, 1)
    up = 2 * lax.rem(y + step_y, 4) + lo
    down = 2 * lax.rem(y + 4 - step_y, 4) + lo
    up_y, down_y, far_y = lax.rem(own_y + 1, 4), lax.rem(own_y + 3, 4), lax.rem(own_y + 2, 4)

    def flip(bit, by):
        return bit + by - 2 * bit * by

    def rank_at(o, a, b):
        return flip(hi, a) * 8 + lax.rem(z + o, 4) * 2 + flip(core, b)

    def load(c):
        start = pl.multiple_of(lax.rem(c, CHUNKS) * CHUNK, CHUNK)
        slot = lax.rem(c, W_SLOTS)
        return pltpu.make_async_copy(
            w_hbm.at[:, pl.ds(start, CHUNK)], w_buf.at[slot], w_sem.at[slot]
        )

    loads = [
        pltpu.make_async_copy(lat_hbm, slab.at[tp], own_sem.at[0]),
        pltpu.make_async_copy(wuk_hbm, wuk_ref, own_sem.at[1]),
        pltpu.make_async_copy(wuv_hbm, wuv_ref, own_sem.at[2]),
        pltpu.make_async_copy(q_hbm, q_ref, own_sem.at[3]),
    ]
    for copy in loads:
        copy.start()
    for c in range(W_SLOTS - 1):
        load(c).start()

    greet(
        [(dp, lax.rem(tp + o, TP)) for o in range(1, TP)]
        + [(lax.rem(dp + o, DP), tp) for o in range(1, DP)]
        + [(lax.rem(dp + DP // 2, DP), across)]
    )

    opposite = 2 * lax.rem(y + 2, 4) + lo
    after, before = 2 * lax.rem(y + 1, 4) + lo, 2 * lax.rem(y + 3, 4) + lo

    def hand(index, src, at, to):
        return remote(src, slab.at[at], ag_s.at[index], ag_r.at[index], dp, to)

    gathers = [
        hand(0, lat_hbm, tp, opposite),
        hand(1, lat_hbm, tp, across),
        hand(2, lat_hbm, tp, after),
        hand(3, lat_hbm, tp, before),
        hand(4, slab.at[across], across, after),
        hand(5, slab.at[across], across, before),
        hand(6, slab.at[opposite], opposite, across),
    ]
    for copy in gathers[:4]:
        copy.start()
    gathers[1].wait_recv()
    gathers[4].start()
    gathers[5].start()
    gathers[0].wait_recv()
    gathers[6].start()
    write_bias(seg_ref, bias, dp)
    for copy in loads:
        copy.wait()
    for copy in gathers[2:]:
        copy.wait_recv()
    rope = slab[:, :, LAT:].reshape(ROWS, ROPE)
    blank = jnp.zeros((ROWS, ROPE), BF16)
    rope_even[...] = jnp.concatenate([rope, blank], axis=1)
    rope_odd[...] = jnp.concatenate([blank, rope], axis=1)
    values[:, :, VH:] = jnp.ones((2, ROWS, VH), BF16)

    parts, gathered = (parts1, parts2), (gathered1, gathered2)

    def spread(g, o, a, b):
        pair = lax.rem(z + o, 4)
        part = 2 * flip(core, b) + flip(hi, a)
        at = g * DP + o * 4 + a * 2 + b
        return remote(
            parts[g].at[pair, part], gathered[g].at[dp], p1_s.at[at], p1_r.at[at],
            rank_at(o, a, b), tp,
        )

    def own_part(g):
        return pltpu.make_async_copy(
            parts[g].at[z, 2 * core + hi], gathered[g].at[dp], p1_s.at[g * DP]
        )

    def attend_step(i, carry):
        o = jnp.where(i == 0, 2, jnp.where(i == 1, 1, jnp.where(i == 2, 3, 0)))
        attend_pair(
            lax.rem(z + o, 4), slab, rope_even, rope_odd, bias, q_ref, wuk_ref, wuv_ref,
            keys, values, parts1, parts2,
        )
        for a, b in ((1, 0), (1, 1), (0, 1)):
            spread(0, o, a, b).start()

        @pl.when(o != 0)
        def _():
            spread(0, o, 0, 0).start()

        return carry

    ways = [(o, a, b) for o in (2, 1, 3, 0) for a in (1, 0) for b in (1, 0)]
    others = [way for way in ways if way != (0, 0, 0)]

    def spread_second(a):
        for way in others:
            if way[1] == a:
                spread(1, *way).start()

    def spread_done(g):
        for way in others:
            spread(g, *way).wait_recv()
        own_part(g).wait()

    lax.fori_loop(0, PAIRS, attend_step, 0)
    own_part(0).start()
    own_part(1).start()
    spread_done(0)

    part = 2 * core + hi
    staged_near, staged_far = (staged_near1, staged_near2), (staged_far1, staged_far2)
    near, far = (near1, near2), (far1, far2)

    def taken(rank, e, u):
        source = lax.rem(rank + DP - off_ref[block_of(part, e, u)], DP)
        return gathered2[source, e, u - 1] if u else gathered1[source, e, 0]

    def deliver(g, o, a, b):
        at = g * DP + o * 4 + a * 2 + b
        src = (staged_far if a else staged_near)[g].at[2 * o + b]
        dst = (far if a else near)[g].at[2 * z + core]
        return remote(src, dst, p2_s.at[at], p2_r.at[at], rank_at(o, a, b), tp)

    def deliver_all(g):
        units = ((0,), (1, 2))[g]
        count = len(units)
        for o, a, b in ways:
            rank = rank_at(o, a, b)
            own = (o, a, b) == (0, 0, 0)
            if a:
                target, index = staged_far[g], 2 * o + b
            elif own:
                target, index = near[g], 2 * z + core
            else:
                target, index = staged_near[g], 2 * o + b
            for n, u in enumerate(units):
                target[index, n] = taken(rank, lo, u)
            if not a:
                for side in range(2):
                    for n, u in enumerate(units):
                        target[index, count * (1 + side) + n] = taken(
                            rank + (side - hi) * 8, 1 - lo, u
                        )
            if not own:
                deliver(g, o, a, b).start()

    def arrived(g):
        for way in others:
            deliver(g, *way).wait_recv()
        if g == 0:
            spread_second(0)
        count = g + 1
        for pair in range(PAIRS):
            columns = pl.ds(pair * PART, PART)
            for c in range(2):
                for n in range(count):
                    for a in range(2):
                        mine, yours = 2 * c + a, 2 * c + 1 - a
                        unit = (far if a else near)[g][2 * pair + c, n]
                        if g == 0:
                            home = jnp.where(hi == 0, FIRST[mine], FIRST[yours])
                            rows1[4 + home, :, columns] = unit
                        else:
                            home = jnp.where(hi == 0, SECOND[mine][n], SECOND[yours][n])
                            keep2[home, :, columns] = unit
                    for side in range(2):
                        unit = near[g][2 * pair + c, count * (1 + side) + n]
                        if g == 0:
                            rows1[2 * side + c, :, columns] = unit
                        else:
                            away2[side, 2 * c + n, :, columns] = unit

    class Group:
        pass

    groups = []
    for g, (acc, x_out, x_in, y1_out, y1_in, y2_out, y2_in) in enumerate(
        (
            (acc1, x_out1, x_in1, y1_out1, y1_in1, y2_out1, y2_in1),
            (acc2, x_out2, x_in2, y1_out2, y1_in2, y2_out2, y2_in2),
        )
    ):
        t = Group()
        t.acc, t.x_out, t.x_in, t.y1_out, t.y1_in, t.y2_out, t.y2_in = (
            acc, x_out, x_in, y1_out, y1_in, y2_out, y2_in,
        )
        t.g, t.count, t.rows, t.lags = g, GROUPS[g], GROUPS[g] * UNIT, LAGS[g]
        groups.append(t)

    def x_copies(t, c):
        sems = t.g * CHUNKS + c
        return [
            remote(
                t.x_out.at[c, flip(hi, a)], t.x_in.at[c, hi], xs_sem.at[sems, a],
                xr_sem.at[sems, a], rank_at(0, a, 0), across,
            )
            for a in range(2)
        ]

    def y_copies(t, c, out, into, send, recv):
        sems = t.g * CHUNKS + c
        return [
            remote(out.at[c, a], into.at[c, a], send.at[sems, a], recv.at[sems, a], dp, to)
            for a, to in enumerate((up, down))
        ]

    def y1_copies(t, c):
        return y_copies(t, c, t.y1_out, t.y1_in, y1s_sem, y1r_sem)

    def y2_copies(t, c):
        return y_copies(t, c, t.y2_out, t.y2_in, y2s_sem, y2r_sem)

    def sums(t, c, at, over_x):
        own = t.acc[lax.rem(c, t.lags[2] + 1), pl.ds(t.count * at, t.count)].astype(F32)
        if over_x:
            units = []
            for n in range(t.count):
                places = HOLDS[t.g]
                side = choose(at, [places[i][n][0] for i in range(4)])
                place = choose(at, [places[i][n][1] for i in range(4)])
                units.append(t.x_in[c, side, place].astype(F32))
            own = own + jnp.stack(units)
        return own.reshape(t.rows, CHUNK)

    def either_way(t, c, body):
        if t.g == 0:
            body(True)
        else:
            over_x = goes_over_x(t, c, hi)
            pl.when(over_x)(lambda: body(True))
            pl.when(jnp.logical_not(over_x))(lambda: body(False))

    def multiply(t, i):
        c = i - t.g * CHUNKS
        slot = lax.rem(i, W_SLOTS)
        load(i).wait()

        @pl.when(i + W_SLOTS - 1 < STEPS)
        def _():
            load(i + W_SLOTS - 1).start()

        w = w_buf[slot]
        at = lax.rem(c, t.lags[2] + 1)
        if t.g == 0:
            both = jnp.dot(
                rows1[...].reshape(8 * UNIT, TP * VH), w, preferred_element_type=F32
            )
            t.x_out[c] = both[: 4 * UNIT].astype(BF16).reshape(2, 2, UNIT, CHUNK)
            for copy in x_copies(t, c):
                copy.start()
            t.acc[at] = both[4 * UNIT :].astype(BF16).reshape(4, UNIT, CHUNK)
        else:
            t.x_out[c] = (
                jnp.dot(away2[...].reshape(8 * UNIT, TP * VH), w, preferred_element_type=F32)
                .astype(BF16)
                .reshape(2, 4, UNIT, CHUNK)
            )
            start_x(t, c)
            start_y_first(t, c)
            t.acc[at] = (
                jnp.dot(keep2[...].reshape(8 * UNIT, TP * VH), w, preferred_element_type=F32)
                .astype(BF16)
                .reshape(8, UNIT, CHUNK)
            )

    def y_first(c):
        return (lax.rem(c, 2) == 0) & (c < 2 * Y_FIRST)

    def y_side(c):
        return lax.rem(c // 2, 2)

    def goes_over_x(t, c, to):
        return jnp.logical_not(y_first(c)) | (y_side(c) != to)

    def start_x(t, c):
        for a, copy in enumerate(x_copies(t, c)):
            pl.when(goes_over_x(t, c, flip(hi, a)))(copy.start)

    def away_unit(c, to):
        at = choose(3 - to, [jnp.where(hi == 0, AWAY[0][i], AWAY[1][i]) for i in range(4)])
        return x_out2[c, y_side(c), at]

    def a1_copies(c):
        c = c // 2
        return [
            remote(a1_out.at[c, a], a1_in.at[c, a], a1s_sem.at[c, a], a1r_sem.at[c, a], dp, to)
            for a, to in enumerate((up, down))
        ]

    def a2_copies(c):
        c = c // 2
        return [
            remote(a2_out.at[c, a], a2_in.at[c, a], a2s_sem.at[c, a], a2r_sem.at[c, a], dp, to)
            for a, to in enumerate((up, down))
        ]

    def x2_copy(c):
        rank = y_side(c) * 8 + 2 * z + core
        c = c // 2
        return remote(x2_out.at[c], x2_in.at[c, hi], x2s_sem.at[c], x2r_sem.at[c, hi], rank, across)

    def start_y_first(t, c):
        @pl.when(y_first(c))
        def _():
            other = away_unit(c, far_y)
            a1_out[c // 2, 0] = other[:, :HALF]
            a1_out[c // 2, 1] = other[:, HALF:]
            for copy in a1_copies(c):
                copy.start()

    def after_a1(t, c):
        for copy in a1_copies(c):
            copy.wait_recv()
        to_up = away_unit(c, up_y)
        a2_out[c // 2, 0, :, :HALF] = (
            to_up[:, :HALF].astype(F32) + a1_in[c // 2, 0].astype(F32)
        ).astype(BF16)
        a2_out[c // 2, 0, :, HALF:] = to_up[:, HALF:]
        to_down = away_unit(c, down_y)
        a2_out[c // 2, 1, :, :HALF] = to_down[:, :HALF]
        a2_out[c // 2, 1, :, HALF:] = (
            to_down[:, HALF:].astype(F32) + a1_in[c // 2, 1].astype(F32)
        ).astype(BF16)
        for copy in a2_copies(c):
            copy.start()

    def after_a2(t, c):
        for copy in a2_copies(c):
            copy.wait_recv()
        x2_out[c // 2] = (
            away_unit(c, own_y).astype(F32) + a2_in[c // 2, 0].astype(F32) + a2_in[c // 2, 1].astype(F32)
        ).astype(BF16)
        x2_copy(c).start()

    def after_x(t, c):
        def body(over_x):
            if over_x:
                for copy in x_copies(t, c):
                    copy.wait_recv()
            other = sums(t, c, far_y, over_x).astype(BF16)
            t.y1_out[c, 0] = other[:, :HALF]
            t.y1_out[c, 1] = other[:, HALF:]

        either_way(t, c, body)
        for copy in y1_copies(t, c):
            copy.start()

    def after_y1(t, c):
        for copy in y1_copies(t, c):
            copy.wait_recv()

        def body(over_x):
            to_up = sums(t, c, up_y, over_x)
            t.y2_out[c, 0, :, :HALF] = (to_up[:, :HALF] + t.y1_in[c, 0].astype(F32)).astype(BF16)
            t.y2_out[c, 0, :, HALF:] = to_up[:, HALF:].astype(BF16)
            to_down = sums(t, c, down_y, over_x)
            t.y2_out[c, 1, :, :HALF] = to_down[:, :HALF].astype(BF16)
            t.y2_out[c, 1, :, HALF:] = (
                to_down[:, HALF:] + t.y1_in[c, 1].astype(F32)
            ).astype(BF16)

        either_way(t, c, body)
        for copy in y2_copies(t, c):
            copy.start()

    edge = (own_y == 0) | (own_y == 3)

    def thirds_of(t):
        thirds = [0, jnp.where(edge, 1, 2)] if t.g else [jnp.where(edge, 2, 1)]
        return [jnp.where(lo == 1, 2 - third, third) for third in thirds]

    def out_copies(t, c):
        columns = pl.ds(pl.multiple_of(c * CHUNK, CHUNK), CHUNK)
        return [
            pltpu.make_async_copy(
                out_ref.at[third, :, columns], out_hbm.at[third, :, columns],
                out_sem.at[c, t.g + n],
            )
            for n, third in enumerate(thirds_of(t))
        ]

    def after_y2(t, c):
        for copy in y2_copies(t, c):
            copy.wait_recv()
        start = pl.multiple_of(c * CHUNK, CHUNK)
        thirds = thirds_of(t)

        def body(over_x):
            if not over_x:
                for side in range(2):
                    remote(
                        x2_out.at[c // 2], x2_in.at[c // 2, side], x2s_sem.at[c // 2],
                        x2r_sem.at[c // 2, side], dp, across,
                    ).wait_recv()
            total = sums(t, c, own_y, over_x)
            total = total + t.y2_in[c, 0].astype(F32) + t.y2_in[c, 1].astype(F32)
            for n, third in enumerate(thirds):
                unit = total[n * UNIT : (n + 1) * UNIT]
                if not over_x:
                    side = jnp.where(own_y == 0, 1 - n, n)
                    unit = unit + x2_in[c // 2, side].astype(F32)
                out_ref[third, :, pl.ds(start, CHUNK)] = (
                    unit.astype(BF16)
                )

        either_way(t, c, body)
        for copy in out_copies(t, c):
            copy.start()

    def later(t, i, least, most):
        for lag, stage in zip(t.lags, (after_x, after_y1, after_y2)):
            low = t.g * CHUNKS + lag
            if most > low and least < low + CHUNKS:

                @pl.when((i >= low) & (i < low + CHUNKS))
                def _(stage=stage, low=low):
                    stage(t, i - low)

        if t.g == 1:
            for lag, stage in zip(t.lags[:2], (after_a1, after_a2)):
                low = CHUNKS + lag

                @pl.when((i >= low) & y_first(i - low))
                def _(stage=stage, low=low):
                    stage(t, i - low)

    def first_step(i, carry):
        multiply(groups[0], i)
        later(groups[0], i, 0, CHUNKS)
        return carry

    def second_step(i, carry):
        multiply(groups[1], i)
        later(groups[0], i, CHUNKS, STEPS)
        later(groups[1], i, CHUNKS, STEPS)
        return carry

    def last_step(i, carry):
        later(groups[1], i, STEPS, STEPS + LAGS[1][2])
        return carry

    deliver_all(0)
    spread_second(1)
    arrived(0)
    lax.fori_loop(0, DELIVER_AT, first_step, 0)
    spread_done(1)
    deliver_all(1)
    lax.fori_loop(DELIVER_AT, CHUNKS, first_step, 0)
    arrived(1)
    lax.fori_loop(CHUNKS, STEPS, second_step, 0)
    lax.fori_loop(STEPS, STEPS + LAGS[1][2], last_step, 0)

    for copy in gathers:
        copy.wait_send()
    for way in others:
        spread(0, *way).wait_send()
        spread(1, *way).wait_send()
        deliver(0, *way).wait_send()
        deliver(1, *way).wait_send()

    def drain(c, carry):
        for t in groups:
            for copy in y1_copies(t, c) + y2_copies(t, c):
                copy.wait_send()
            for copy in out_copies(t, c):
                copy.wait()
        for copy in x_copies(groups[0], c):
            copy.wait_send()
        for a, copy in enumerate(x_copies(groups[1], c)):
            pl.when(goes_over_x(groups[1], c, flip(hi, a)))(copy.wait_send)

        @pl.when(y_first(c))
        def _():
            for copy in a1_copies(c) + a2_copies(c) + [x2_copy(c)]:
                copy.wait_send()

        return carry

    lax.fori_loop(0, CHUNKS, drain, 0)


def sum_scratch(g):
    rows = GROUPS[g] * UNIT
    return [
        pltpu.VMEM((LAGS[g][2] + 1, 4 * GROUPS[g], UNIT, CHUNK), BF16),
        pltpu.VMEM((CHUNKS, 2, 2 * GROUPS[g], UNIT, CHUNK), BF16),
        pltpu.VMEM((CHUNKS, 2, 2 * GROUPS[g], UNIT, CHUNK), BF16),
        pltpu.VMEM((CHUNKS, 2, rows, HALF), BF16),
        pltpu.VMEM((CHUNKS, 2, rows, HALF), BF16),
        pltpu.VMEM((CHUNKS, 2, rows, CHUNK), BF16),
        pltpu.VMEM((CHUNKS, 2, rows, CHUNK), BF16),
    ]


def on_device(queries, latent, segments, offsets, w_uk, w_uv, w_out):
    any_spec = pl.BlockSpec(memory_space=pl.ANY)
    smem_spec = pl.BlockSpec(memory_space=pltpu.SMEM)
    dma = pltpu.SemaphoreType.DMA
    out = pl.pallas_call(
        whole_kernel,
        out_shape=jax.ShapeDtypeStruct((3, UNIT, D), BF16),
        in_specs=[smem_spec] * 2 + [any_spec] * 5,
        out_specs=any_spec,
        scratch_shapes=[
            pltpu.VMEM((TP, OWN, KV), BF16),
            pltpu.VMEM((ROWS, HEADS * (NOPE + ROPE)), BF16),
            pltpu.VMEM((HEADS, NOPE, LAT), BF16),
            pltpu.VMEM((HEADS, LAT, VH), BF16),
            pltpu.VMEM((ROWS, 2 * ROPE), BF16),
            pltpu.VMEM((ROWS, 2 * ROPE), BF16),
            pltpu.VMEM((NB, BLK, WINDOW * BLK), F32),
            pltpu.VMEM((2, ROWS, 2 * NOPE), BF16),
            pltpu.VMEM((2, ROWS, 2 * VH), BF16),
            pltpu.VMEM((PAIRS, PARTS, 2, 1, UNIT, PART), BF16),
            pltpu.VMEM((PAIRS, PARTS, 2, 2, UNIT, PART), BF16),
            pltpu.VMEM((DP, 2, 1, UNIT, PART), BF16),
            pltpu.VMEM((DP, 2, 2, UNIT, PART), BF16),
            pltpu.VMEM((8, 3, UNIT, PART), BF16),
            pltpu.VMEM((8, 6, UNIT, PART), BF16),
            pltpu.VMEM((8, 1, UNIT, PART), BF16),
            pltpu.VMEM((8, 2, UNIT, PART), BF16),
            pltpu.VMEM((8, 3, UNIT, PART), BF16),
            pltpu.VMEM((8, 6, UNIT, PART), BF16),
            pltpu.VMEM((8, 1, UNIT, PART), BF16),
            pltpu.VMEM((8, 2, UNIT, PART), BF16),
            pltpu.VMEM((8, UNIT, TP * VH), BF16),
            pltpu.VMEM((8, UNIT, TP * VH), BF16),
            pltpu.VMEM((2, 4, UNIT, TP * VH), BF16),
            pltpu.VMEM((W_SLOTS, TP * VH, CHUNK), BF16),
        ]
        + sum_scratch(0)
        + sum_scratch(1)
        + [
            pltpu.VMEM((Y_FIRST, 2, UNIT, HALF), BF16),
            pltpu.VMEM((Y_FIRST, 2, UNIT, HALF), BF16),
            pltpu.VMEM((Y_FIRST, 2, UNIT, CHUNK), BF16),
            pltpu.VMEM((Y_FIRST, 2, UNIT, CHUNK), BF16),
            pltpu.VMEM((Y_FIRST, UNIT, CHUNK), BF16),
            pltpu.VMEM((Y_FIRST, 2, UNIT, CHUNK), BF16),
            pltpu.VMEM((3, UNIT, D), BF16),
            dma((4,)),
            dma((TP - 1,)),
            dma((TP - 1,)),
            dma((2 * DP,)),
            dma((2 * DP,)),
            dma((2 * DP,)),
            dma((2 * DP,)),
            dma((W_SLOTS,)),
        ]
        + [dma((STEPS, 2))] * 6
        + [dma((Y_FIRST, 2))] * 4
        + [dma((Y_FIRST,)), dma((Y_FIRST, 2)), dma((CHUNKS, 3))],
        compiler_params=pltpu.CompilerParams(
            collective_id=0, has_side_effects=True, vmem_limit_bytes=58 * 2**20
        ),
        name="whole",
    )(segments.T, offsets, latent, queries, w_uk, w_uv, w_out)
    return out.reshape(OWN, D)


def solution(mesh):
    return jax.shard_map(
        on_device,
        mesh=mesh,
        in_specs=(
            P("dp", "tp"),
            P(("dp", "tp"), None),
            P(),
            P(),
            P("tp", None, None),
            P("tp", None, None),
            P("tp", None),
        ),
        out_specs=P(("dp", "tp"), None),
        check_vma=False,
    )
```

```python
import functools

import jax
import jax.numpy as jnp
from jax import lax
from jax.experimental import pallas as pl
from jax.experimental.pallas import tpu as pltpu
from jax.sharding import PartitionSpec as P

NOPE = 128
ROPE = 64
LAT = 512
VH = 128
BLK = 128
NB = 6
DP = 16
TP = 8
HEADS = 8
ROWS = NB * BLK
KV = LAT + ROPE
D = 7168
OWN = ROWS // TP
PARTS = 4
PAIRS = HEADS // 2
WINDOW = 4
UNIT = 32
PART = 256
SCALE = (NOPE + ROPE) ** (-0.5)
LOG2E = 1.4426950408889634

CHUNK = 512
CHUNKS = D // CHUNK
HALF = CHUNK // 2
STEPS = 2 * CHUNKS
W_SLOTS = 3
GROUPS = (1, 2)
LAGS = ((4, 7, 10), (3, 5, 8))
Y_FIRST = 5
AHEAD = 5
DELIVER_AT = 5

MESH = pl.DeviceIdType.MESH
BF16 = jnp.bfloat16
F32 = jnp.float32


def ranks():
    return lax.axis_index("dp"), lax.axis_index("tp")


def remote(src, dst, send, recv, dp, tp):
    return pltpu.make_async_remote_copy(
        src_ref=src,
        dst_ref=dst,
        send_sem=send,
        recv_sem=recv,
        device_id={"dp": dp, "tp": tp},
        device_id_type=MESH,
    )


def greet(peers):
    barrier = pltpu.get_barrier_semaphore()
    for dp, tp in peers:
        pl.semaphore_signal(
            barrier, inc=1, device_id={"dp": dp, "tp": tp}, device_id_type=MESH
        )
    pl.semaphore_wait(barrier, len(peers))


def nt_dot(a, b):
    return lax.dot_general(a, b, (((1,), (1,)), ((), ())), preferred_element_type=F32)


HOME = ((11, 3, 6), (4, 0, 5), (7, 1, 9), (2, 10, 8))
FIRST = (3, 1, 2, 0)
SECOND = ((2, 4), (0, 3), (1, 6), (7, 5))
AWAY = ((2, 0, 1, 3), (0, 1, 3, 2))


def unit_of(p, e, u):
    y, third = divmod(HOME[p][u], 3)
    unit = 6 * y + third
    return 23 - unit if e else unit


PLACE = {
    unit_of(p, e, u): (p, e, u) for p in range(PARTS) for e in range(2) for u in range(3)
}


HOLDS = (
    tuple(((FIRST.index(y) % 2, FIRST.index(y) // 2),) for y in range(4)),
    tuple(
        tuple(
            (p % 2, 2 * (p // 2) + n)
            for home in (2 * y, 2 * y + 1)
            for p in range(PARTS)
            for n in range(2)
            if SECOND[p][n] == home
        )
        for y in range(4)
    ),
)


def choose(p, options):
    value = options[0]
    for i in range(1, PARTS):
        value = jnp.where(p == i, options[i], value)
    return value


def block_of(p, e, u):
    first = choose(p, [unit_of(i, 0, u) // 4 for i in range(PARTS)])
    return jnp.where(e == 1, NB - 1 - first, first)


def write_bias(seg_ref, bias, dp):
    row = lax.broadcasted_iota(jnp.int32, (BLK, BLK), 0)
    col = lax.broadcasted_iota(jnp.int32, (BLK, BLK), 1)
    for qb in range(NB):
        first = max(0, qb - WINDOW + 1)
        for kb in range(first, qb + 1):
            if kb == qb:
                block = jnp.where(col <= row, 0.0, -jnp.inf).astype(F32)
            else:
                same = seg_ref[kb, dp] == seg_ref[qb, dp]
                block = jnp.full((BLK, BLK), jnp.where(same, 0.0, -jnp.inf), F32)
            bias[qb, :, (kb - first) * BLK : (kb - first + 1) * BLK] = block


def attend_pair(pair, slab, rope_even, rope_odd, bias, q_ref, wuk_ref, wuv_ref, keys, values, parts1, parts2):
    content = slab[:, :, :LAT].reshape(ROWS, LAT)
    up = wuk_ref[pl.ds(2 * pair, 2)].reshape(2 * NOPE, LAT)
    both = nt_dot(content, up)
    lane = lax.broadcasted_iota(jnp.int32, (ROWS, NOPE), 1)
    keys[0, :, :NOPE] = both[:, :NOPE].astype(BF16)
    keys[0, :, NOPE:] = rope_even[...]
    turned = pltpu.roll(both[:, NOPE:], 64, 1)
    keys[1, :, :NOPE] = jnp.where(lane < 64, 0.0, turned).astype(BF16)
    keys[1, :, NOPE:] = jnp.where(lane < 64, turned, rope_odd[...].astype(F32)).astype(BF16)
    for e in range(2):
        values[e, :, :VH] = jnp.dot(
            content, wuv_ref[2 * pair + e], preferred_element_type=F32
        ).astype(BF16)

    def window(qb):
        first = max(0, qb - WINDOW + 1)
        return pl.ds(first * BLK, (qb - first + 1) * BLK), (qb - first + 1) * BLK

    def score(qb, e):
        keep, width = window(qb)
        start = pl.multiple_of(pair * 384 + 128 * e, 128)
        q = q_ref[pl.ds(qb * BLK, BLK), pl.ds(start, 256)]
        return nt_dot(q, keys[e, keep, :]) + bias[qb, :, :width]

    def finish(qb, e, s):
        keep, _ = window(qb)
        top = jnp.max(s, axis=1, keepdims=True)
        p = jnp.exp2((s - top) * (SCALE * LOG2E)).astype(BF16)
        o = jnp.dot(p, values[e, keep, :], preferred_element_type=F32)
        o = (o[:, :VH] / o[:, VH:]).astype(BF16)
        for quarter in range(4):
            part, side, u = PLACE[4 * qb + quarter]
            target, n = (parts2, u - 1) if u else (parts1, 0)
            target[pair, part, side, n, :, e * VH : (e + 1) * VH] = o[
                quarter * UNIT : (quarter + 1) * UNIT
            ]

    units = [(qb, e) for qb in range(NB) for e in range(2)]
    waiting = []
    for unit in units:
        waiting.append((*unit, score(*unit)))
        if len(waiting) > AHEAD:
            finish(*waiting.pop(0))
    for held in waiting:
        finish(*held)


def whole_kernel(
    seg_ref, off_ref, lat_hbm, q_hbm, wuk_hbm, wuv_hbm, w_hbm, out_hbm,
    slab, q_ref, wuk_ref, wuv_ref, rope_even, rope_odd, bias, keys, values,
    parts1, parts2, gathered1, gathered2, staged_near1, staged_near2, staged_far1, staged_far2, near1, near2, far1, far2,
    rows1, keep2, away2, w_buf,
    acc1, x_out1, x_in1, y1_out1, y1_in1, y2_out1, y2_in1,
    acc2, x_out2, x_in2, y1_out2, y1_in2, y2_out2, y2_in2,
    a1_out, a1_in, a2_out, a2_in, x2_out, x2_in, out_ref,
    own_sem, ag_s, ag_r, p1_s, p1_r, p2_s, p2_r,
    w_sem, xs_sem, xr_sem, y1s_sem, y1r_sem, y2s_sem, y2r_sem,
    a1s_sem, a1r_sem, a2s_sem, a2r_sem, x2s_sem, x2r_sem, out_sem,
):
    dp, tp = ranks()
    y, lo = tp // 2, lax.rem(tp, 2)
    hi, z, core = dp // 8, lax.rem(dp // 2, 4), lax.rem(dp, 2)
    across = 2 * y + 1 - lo
    own_y = jnp.where(lo == 1, 3 - y, y)
    step_y = jnp.where(lo == 1, 3, 1)
    up = 2 * lax.rem(y + step_y, 4) + lo
    down = 2 * lax.rem(y + 4 - step_y, 4) + lo
    up_y, down_y, far_y = lax.rem(own_y + 1, 4), lax.rem(own_y + 3, 4), lax.rem(own_y + 2, 4)

    def flip(bit, by):
        return bit + by - 2 * bit * by

    def rank_at(o, a, b):
        return flip(hi, a) * 8 + lax.rem(z + o, 4) * 2 + flip(core, b)

    def load(c):
        start = pl.multiple_of(lax.rem(c, CHUNKS) * CHUNK, CHUNK)
        slot = lax.rem(c, W_SLOTS)
        return pltpu.make_async_copy(
            w_hbm.at[:, pl.ds(start, CHUNK)], w_buf.at[slot], w_sem.at[slot]
        )

    loads = [
        pltpu.make_async_copy(lat_hbm, slab.at[tp], own_sem.at[0]),
        pltpu.make_async_copy(wuk_hbm, wuk_ref, own_sem.at[1]),
        pltpu.make_async_copy(wuv_hbm, wuv_ref, own_sem.at[2]),
        pltpu.make_async_copy(q_hbm, q_ref, own_sem.at[3]),
    ]
    for copy in loads:
        copy.start()
    for c in range(W_SLOTS - 1):
        load(c).start()

    greet(
        [(lax.rem(dp + DP // 2, DP), across)]
        + [(lax.rem(dp + o, DP), tp) for o in range(DP - 1, 0, -1)]
        + [(dp, lax.rem(tp + o, TP)) for o in (4, 5, 3, 6, 2, 7, 1)]
    )

    opposite = 2 * lax.rem(y + 2, 4) + lo
    after, before = 2 * lax.rem(y + 1, 4) + lo, 2 * lax.rem(y + 3, 4) + lo

    def hand(index, src, at, to):
        return remote(src, slab.at[at], ag_s.at[index], ag_r.at[index], dp, to)

    gathers = [
        hand(0, lat_hbm, tp, opposite),
        hand(1, lat_hbm, tp, across),
        hand(2, lat_hbm, tp, after),
        hand(3, lat_hbm, tp, before),
        hand(4, slab.at[across], across, after),
        hand(5, slab.at[across], across, before),
        hand(6, slab.at[opposite], opposite, across),
    ]
    for copy in gathers[:4]:
        copy.start()
    gathers[1].wait_recv()
    gathers[4].start()
    gathers[5].start()
    gathers[0].wait_recv()
    gathers[6].start()
    write_bias(seg_ref, bias, dp)
    for copy in loads:
        copy.wait()
    for copy in gathers[2:]:
        copy.wait_recv()
    rope = slab[:, :, LAT:].reshape(ROWS, ROPE)
    blank = jnp.zeros((ROWS, ROPE), BF16)
    rope_even[...] = jnp.concatenate([rope, blank], axis=1)
    rope_odd[...] = jnp.concatenate([blank, rope], axis=1)
    values[:, :, VH:] = jnp.ones((2, ROWS, VH), BF16)

    parts, gathered = (parts1, parts2), (gathered1, gathered2)

    def spread(g, o, a, b):
        pair = lax.rem(z + o, 4)
        part = 2 * flip(core, b) + flip(hi, a)
        at = g * DP + o * 4 + a * 2 + b
        return remote(
            parts[g].at[pair, part], gathered[g].at[dp], p1_s.at[at], p1_r.at[at],
            rank_at(o, a, b), tp,
        )

    def own_part(g):
        return pltpu.make_async_copy(
            parts[g].at[z, 2 * core + hi], gathered[g].at[dp], p1_s.at[g * DP]
        )

    def attend_step(i, carry):
        o = jnp.where(i == 0, 2, jnp.where(i == 1, 1, jnp.where(i == 2, 3, 0)))
        attend_pair(
            lax.rem(z + o, 4), slab, rope_even, rope_odd, bias, q_ref, wuk_ref, wuv_ref,
            keys, values, parts1, parts2,
        )
        for a, b in ((1, 0), (1, 1), (0, 1)):
            spread(0, o, a, b).start()

        @pl.when(o != 0)
        def _():
            spread(0, o, 0, 0).start()

        return carry

    ways = [(o, a, b) for o in (2, 1, 3, 0) for a in (1, 0) for b in (1, 0)]
    others = [way for way in ways if way != (0, 0, 0)]

    def spread_second(a):
        for way in others:
            if way[1] == a:
                spread(1, *way).start()

    def spread_done(g):
        for way in others:
            spread(g, *way).wait_recv()
        own_part(g).wait()

    lax.fori_loop(0, PAIRS, attend_step, 0)
    own_part(0).start()
    own_part(1).start()
    spread_done(0)

    part = 2 * core + hi
    staged_near, staged_far = (staged_near1, staged_near2), (staged_far1, staged_far2)
    near, far = (near1, near2), (far1, far2)

    def taken(rank, e, u):
        source = lax.rem(rank + DP - off_ref[block_of(part, e, u)], DP)
        return gathered2[source, e, u - 1] if u else gathered1[source, e, 0]

    def deliver(g, o, a, b):
        at = g * DP + o * 4 + a * 2 + b
        src = (staged_far if a else staged_near)[g].at[2 * o + b]
        dst = (far if a else near)[g].at[2 * z + core]
        return remote(src, dst, p2_s.at[at], p2_r.at[at], rank_at(o, a, b), tp)

    def deliver_all(g):
        units = ((0,), (1, 2))[g]
        count = len(units)
        for o, a, b in ways:
            rank = rank_at(o, a, b)
            own = (o, a, b) == (0, 0, 0)
            if a:
                target, index = staged_far[g], 2 * o + b
            elif own:
                target, index = near[g], 2 * z + core
            else:
                target, index = staged_near[g], 2 * o + b
            for n, u in enumerate(units):
                target[index, n] = taken(rank, lo, u)
            if not a:
                for side in range(2):
                    for n, u in enumerate(units):
                        target[index, count * (1 + side) + n] = taken(
                            rank + (side - hi) * 8, 1 - lo, u
                        )
            if not own:
                deliver(g, o, a, b).start()

    def arrived(g):
        for way in others:
            deliver(g, *way).wait_recv()
        if g == 0:
            spread_second(0)
        count = g + 1
        for pair in range(PAIRS):
            columns = pl.ds(pair * PART, PART)
            for c in range(2):
                for n in range(count):
                    for a in range(2):
                        mine, yours = 2 * c + a, 2 * c + 1 - a
                        unit = (far if a else near)[g][2 * pair + c, n]
                        if g == 0:
                            home = jnp.where(hi == 0, FIRST[mine], FIRST[yours])
                            rows1[4 + home, :, columns] = unit
                        else:
                            home = jnp.where(hi == 0, SECOND[mine][n], SECOND[yours][n])
                            keep2[home, :, columns] = unit
                    for side in range(2):
                        unit = near[g][2 * pair + c, count * (1 + side) + n]
                        if g == 0:
                            rows1[2 * side + c, :, columns] = unit
                        else:
                            away2[side, 2 * c + n, :, columns] = unit

    class Group:
        pass

    groups = []
    for g, (acc, x_out, x_in, y1_out, y1_in, y2_out, y2_in) in enumerate(
        (
            (acc1, x_out1, x_in1, y1_out1, y1_in1, y2_out1, y2_in1),
            (acc2, x_out2, x_in2, y1_out2, y1_in2, y2_out2, y2_in2),
        )
    ):
        t = Group()
        t.acc, t.x_out, t.x_in, t.y1_out, t.y1_in, t.y2_out, t.y2_in = (
            acc, x_out, x_in, y1_out, y1_in, y2_out, y2_in,
        )
        t.g, t.count, t.rows, t.lags = g, GROUPS[g], GROUPS[g] * UNIT, LAGS[g]
        groups.append(t)

    def x_copies(t, c):
        sems = t.g * CHUNKS + c
        return [
            remote(
                t.x_out.at[c, flip(hi, a)], t.x_in.at[c, hi], xs_sem.at[sems, a],
                xr_sem.at[sems, a], rank_at(0, a, 0), across,
            )
            for a in range(2)
        ]

    def y_copies(t, c, out, into, send, recv):
        sems = t.g * CHUNKS + c
        return [
            remote(out.at[c, a], into.at[c, a], send.at[sems, a], recv.at[sems, a], dp, to)
            for a, to in enumerate((up, down))
        ]

    def y1_copies(t, c):
        return y_copies(t, c, t.y1_out, t.y1_in, y1s_sem, y1r_sem)

    def y2_copies(t, c):
        return y_copies(t, c, t.y2_out, t.y2_in, y2s_sem, y2r_sem)

    def sums(t, c, at, over_x):
        own = t.acc[lax.rem(c, t.lags[2] + 1), pl.ds(t.count * at, t.count)].astype(F32)
        if over_x:
            units = []
            for n in range(t.count):
                places = HOLDS[t.g]
                side = choose(at, [places[i][n][0] for i in range(4)])
                place = choose(at, [places[i][n][1] for i in range(4)])
                units.append(t.x_in[c, side, place].astype(F32))
            own = own + jnp.stack(units)
        return own.reshape(t.rows, CHUNK)

    def either_way(t, c, body):
        if t.g == 0:
            body(True)
        else:
            over_x = goes_over_x(t, c, hi)
            pl.when(over_x)(lambda: body(True))
            pl.when(jnp.logical_not(over_x))(lambda: body(False))

    def multiply(t, i):
        c = i - t.g * CHUNKS
        slot = lax.rem(i, W_SLOTS)
        load(i).wait()

        @pl.when(i + W_SLOTS - 1 < STEPS)
        def _():
            load(i + W_SLOTS - 1).start()

        w = w_buf[slot]
        at = lax.rem(c, t.lags[2] + 1)
        if t.g == 0:
            both = jnp.dot(
                rows1[...].reshape(8 * UNIT, TP * VH), w, preferred_element_type=F32
            )
            t.x_out[c] = both[: 4 * UNIT].astype(BF16).reshape(2, 2, UNIT, CHUNK)
            for copy in x_copies(t, c):
                copy.start()
            t.acc[at] = both[4 * UNIT :].astype(BF16).reshape(4, UNIT, CHUNK)
        else:
            t.x_out[c] = (
                jnp.dot(away2[...].reshape(8 * UNIT, TP * VH), w, preferred_element_type=F32)
                .astype(BF16)
                .reshape(2, 4, UNIT, CHUNK)
            )
            start_x(t, c)
            start_y_first(t, c)
            t.acc[at] = (
                jnp.dot(keep2[...].reshape(8 * UNIT, TP * VH), w, preferred_element_type=F32)
                .astype(BF16)
                .reshape(8, UNIT, CHUNK)
            )

    def y_first(c):
        return (lax.rem(c, 2) == 0) & (c < 2 * Y_FIRST)

    def y_side(c):
        return lax.rem(c // 2, 2)

    def goes_over_x(t, c, to):
        return jnp.logical_not(y_first(c)) | (y_side(c) != to)

    def start_x(t, c):
        for a, copy in enumerate(x_copies(t, c)):
            pl.when(goes_over_x(t, c, flip(hi, a)))(copy.start)

    def away_unit(c, to):
        at = choose(3 - to, [jnp.where(hi == 0, AWAY[0][i], AWAY[1][i]) for i in range(4)])
        return x_out2[c, y_side(c), at]

    def a1_copies(c):
        c = c // 2
        return [
            remote(a1_out.at[c, a], a1_in.at[c, a], a1s_sem.at[c, a], a1r_sem.at[c, a], dp, to)
            for a, to in enumerate((up, down))
        ]

    def a2_copies(c):
        c = c // 2
        return [
            remote(a2_out.at[c, a], a2_in.at[c, a], a2s_sem.at[c, a], a2r_sem.at[c, a], dp, to)
            for a, to in enumerate((up, down))
        ]

    def x2_copy(c):
        rank = y_side(c) * 8 + 2 * z + core
        c = c // 2
        return remote(x2_out.at[c], x2_in.at[c, hi], x2s_sem.at[c], x2r_sem.at[c, hi], rank, across)

    def start_y_first(t, c):
        @pl.when(y_first(c))
        def _():
            other = away_unit(c, far_y)
            a1_out[c // 2, 0] = other[:, :HALF]
            a1_out[c // 2, 1] = other[:, HALF:]
            for copy in a1_copies(c):
                copy.start()

    def after_a1(t, c):
        for copy in a1_copies(c):
            copy.wait_recv()
        to_up = away_unit(c, up_y)
        a2_out[c // 2, 0, :, :HALF] = (
            to_up[:, :HALF].astype(F32) + a1_in[c // 2, 0].astype(F32)
        ).astype(BF16)
        a2_out[c // 2, 0, :, HALF:] = to_up[:, HALF:]
        to_down = away_unit(c, down_y)
        a2_out[c // 2, 1, :, :HALF] = to_down[:, :HALF]
        a2_out[c // 2, 1, :, HALF:] = (
            to_down[:, HALF:].astype(F32) + a1_in[c // 2, 1].astype(F32)
        ).astype(BF16)
        for copy in a2_copies(c):
            copy.start()

    def after_a2(t, c):
        for copy in a2_copies(c):
            copy.wait_recv()
        x2_out[c // 2] = (
            away_unit(c, own_y).astype(F32) + a2_in[c // 2, 0].astype(F32) + a2_in[c // 2, 1].astype(F32)
        ).astype(BF16)
        x2_copy(c).start()

    def after_x(t, c):
        def body(over_x):
            if over_x:
                for copy in x_copies(t, c):
                    copy.wait_recv()
            other = sums(t, c, far_y, over_x).astype(BF16)
            t.y1_out[c, 0] = other[:, :HALF]
            t.y1_out[c, 1] = other[:, HALF:]

        either_way(t, c, body)
        for copy in y1_copies(t, c):
            copy.start()

    def after_y1(t, c):
        for copy in y1_copies(t, c):
            copy.wait_recv()

        def body(over_x):
            to_up = sums(t, c, up_y, over_x)
            t.y2_out[c, 0, :, :HALF] = (to_up[:, :HALF] + t.y1_in[c, 0].astype(F32)).astype(BF16)
            t.y2_out[c, 0, :, HALF:] = to_up[:, HALF:].astype(BF16)
            to_down = sums(t, c, down_y, over_x)
            t.y2_out[c, 1, :, :HALF] = to_down[:, :HALF].astype(BF16)
            t.y2_out[c, 1, :, HALF:] = (
                to_down[:, HALF:] + t.y1_in[c, 1].astype(F32)
            ).astype(BF16)

        either_way(t, c, body)
        for copy in y2_copies(t, c):
            copy.start()

    edge = (own_y == 0) | (own_y == 3)

    def thirds_of(t):
        thirds = [0, jnp.where(edge, 1, 2)] if t.g else [jnp.where(edge, 2, 1)]
        return [jnp.where(lo == 1, 2 - third, third) for third in thirds]

    def out_copies(t, c):
        columns = pl.ds(pl.multiple_of(c * CHUNK, CHUNK), CHUNK)
        return [
            pltpu.make_async_copy(
                out_ref.at[third, :, columns], out_hbm.at[third, :, columns],
                out_sem.at[c, t.g + n],
            )
            for n, third in enumerate(thirds_of(t))
        ]

    def after_y2(t, c):
        for copy in y2_copies(t, c):
            copy.wait_recv()
        start = pl.multiple_of(c * CHUNK, CHUNK)
        thirds = thirds_of(t)

        def body(over_x):
            if not over_x:
                for side in range(2):
                    remote(
                        x2_out.at[c // 2], x2_in.at[c // 2, side], x2s_sem.at[c // 2],
                        x2r_sem.at[c // 2, side], dp, across,
                    ).wait_recv()
            total = sums(t, c, own_y, over_x)
            total = total + t.y2_in[c, 0].astype(F32) + t.y2_in[c, 1].astype(F32)
            for n, third in enumerate(thirds):
                unit = total[n * UNIT : (n + 1) * UNIT]
                if not over_x:
                    side = jnp.where(own_y == 0, 1 - n, n)
                    unit = unit + x2_in[c // 2, side].astype(F32)
                out_ref[third, :, pl.ds(start, CHUNK)] = (
                    unit.astype(BF16)
                )

        either_way(t, c, body)
        for copy in out_copies(t, c):
            copy.start()

    def later(t, i, least, most):
        for lag, stage in zip(t.lags, (after_x, after_y1, after_y2)):
            low = t.g * CHUNKS + lag
            if most > low and least < low + CHUNKS:

                @pl.when((i >= low) & (i < low + CHUNKS))
                def _(stage=stage, low=low):
                    stage(t, i - low)

        if t.g == 1:
            for lag, stage in zip(t.lags[:2], (after_a1, after_a2)):
                low = CHUNKS + lag

                @pl.when((i >= low) & y_first(i - low))
                def _(stage=stage, low=low):
                    stage(t, i - low)

    def first_step(i, carry):
        multiply(groups[0], i)
        later(groups[0], i, 0, CHUNKS)
        return carry

    def second_step(i, carry):
        later(groups[0], i, CHUNKS, STEPS)
        multiply(groups[1], i)
        later(groups[1], i, CHUNKS, STEPS)
        return carry

    def last_step(i, carry):
        later(groups[1], i, STEPS, STEPS + LAGS[1][2])
        return carry

    deliver_all(0)
    spread_second(1)
    arrived(0)
    lax.fori_loop(0, DELIVER_AT, first_step, 0)
    spread_done(1)
    deliver_all(1)
    lax.fori_loop(DELIVER_AT, CHUNKS, first_step, 0)
    arrived(1)
    lax.fori_loop(CHUNKS, STEPS, second_step, 0)
    lax.fori_loop(STEPS, STEPS + LAGS[1][2], last_step, 0)

    for copy in gathers:
        copy.wait_send()
    for way in others:
        spread(0, *way).wait_send()
        spread(1, *way).wait_send()
        deliver(0, *way).wait_send()
        deliver(1, *way).wait_send()

    def drain(c, carry):
        for t in groups:
            for copy in y1_copies(t, c) + y2_copies(t, c):
                copy.wait_send()
            for copy in out_copies(t, c):
                copy.wait()
        for copy in x_copies(groups[0], c):
            copy.wait_send()
        for a, copy in enumerate(x_copies(groups[1], c)):
            pl.when(goes_over_x(groups[1], c, flip(hi, a)))(copy.wait_send)

        @pl.when(y_first(c))
        def _():
            for copy in a1_copies(c) + a2_copies(c) + [x2_copy(c)]:
                copy.wait_send()

        return carry

    lax.fori_loop(0, CHUNKS, drain, 0)


def sum_scratch(g):
    rows = GROUPS[g] * UNIT
    return [
        pltpu.VMEM((LAGS[g][2] + 1, 4 * GROUPS[g], UNIT, CHUNK), BF16),
        pltpu.VMEM((CHUNKS, 2, 2 * GROUPS[g], UNIT, CHUNK), BF16),
        pltpu.VMEM((CHUNKS, 2, 2 * GROUPS[g], UNIT, CHUNK), BF16),
        pltpu.VMEM((CHUNKS, 2, rows, HALF), BF16),
        pltpu.VMEM((CHUNKS, 2, rows, HALF), BF16),
        pltpu.VMEM((CHUNKS, 2, rows, CHUNK), BF16),
        pltpu.VMEM((CHUNKS, 2, rows, CHUNK), BF16),
    ]


def on_device(queries, latent, segments, offsets, w_uk, w_uv, w_out):
    any_spec = pl.BlockSpec(memory_space=pl.ANY)
    smem_spec = pl.BlockSpec(memory_space=pltpu.SMEM)
    dma = pltpu.SemaphoreType.DMA
    out = pl.pallas_call(
        whole_kernel,
        out_shape=jax.ShapeDtypeStruct((3, UNIT, D), BF16),
        in_specs=[smem_spec] * 2 + [any_spec] * 5,
        out_specs=any_spec,
        scratch_shapes=[
            pltpu.VMEM((TP, OWN, KV), BF16),
            pltpu.VMEM((ROWS, HEADS * (NOPE + ROPE)), BF16),
            pltpu.VMEM((HEADS, NOPE, LAT), BF16),
            pltpu.VMEM((HEADS, LAT, VH), BF16),
            pltpu.VMEM((ROWS, 2 * ROPE), BF16),
            pltpu.VMEM((ROWS, 2 * ROPE), BF16),
            pltpu.VMEM((NB, BLK, WINDOW * BLK), F32),
            pltpu.VMEM((2, ROWS, 2 * NOPE), BF16),
            pltpu.VMEM((2, ROWS, 2 * VH), BF16),
            pltpu.VMEM((PAIRS, PARTS, 2, 1, UNIT, PART), BF16),
            pltpu.VMEM((PAIRS, PARTS, 2, 2, UNIT, PART), BF16),
            pltpu.VMEM((DP, 2, 1, UNIT, PART), BF16),
            pltpu.VMEM((DP, 2, 2, UNIT, PART), BF16),
            pltpu.VMEM((8, 3, UNIT, PART), BF16),
            pltpu.VMEM((8, 6, UNIT, PART), BF16),
            pltpu.VMEM((8, 1, UNIT, PART), BF16),
            pltpu.VMEM((8, 2, UNIT, PART), BF16),
            pltpu.VMEM((8, 3, UNIT, PART), BF16),
            pltpu.VMEM((8, 6, UNIT, PART), BF16),
            pltpu.VMEM((8, 1, UNIT, PART), BF16),
            pltpu.VMEM((8, 2, UNIT, PART), BF16),
            pltpu.VMEM((8, UNIT, TP * VH), BF16),
            pltpu.VMEM((8, UNIT, TP * VH), BF16),
            pltpu.VMEM((2, 4, UNIT, TP * VH), BF16),
            pltpu.VMEM((W_SLOTS, TP * VH, CHUNK), BF16),
        ]
        + sum_scratch(0)
        + sum_scratch(1)
        + [
            pltpu.VMEM((Y_FIRST, 2, UNIT, HALF), BF16),
            pltpu.VMEM((Y_FIRST, 2, UNIT, HALF), BF16),
            pltpu.VMEM((Y_FIRST, 2, UNIT, CHUNK), BF16),
            pltpu.VMEM((Y_FIRST, 2, UNIT, CHUNK), BF16),
            pltpu.VMEM((Y_FIRST, UNIT, CHUNK), BF16),
            pltpu.VMEM((Y_FIRST, 2, UNIT, CHUNK), BF16),
            pltpu.VMEM((3, UNIT, D), BF16),
            dma((4,)),
            dma((TP - 1,)),
            dma((TP - 1,)),
            dma((2 * DP,)),
            dma((2 * DP,)),
            dma((2 * DP,)),
            dma((2 * DP,)),
            dma((W_SLOTS,)),
        ]
        + [dma((STEPS, 2))] * 6
        + [dma((Y_FIRST, 2))] * 4
        + [dma((Y_FIRST,)), dma((Y_FIRST, 2)), dma((CHUNKS, 3))],
        compiler_params=pltpu.CompilerParams(
            collective_id=0, has_side_effects=True, vmem_limit_bytes=58 * 2**20
        ),
        name="whole",
    )(segments.T, offsets, latent, queries, w_uk, w_uv, w_out)
    return out.reshape(OWN, D)


def solution(mesh):
    return jax.shard_map(
        on_device,
        mesh=mesh,
        in_specs=(
            P("dp", "tp"),
            P(("dp", "tp"), None),
            P(),
            P(),
            P("tp", None, None),
            P("tp", None, None),
            P("tp", None),
        ),
        out_specs=P(("dp", "tp"), None),
        check_vma=False,
    )
```
